32 devices in a mesh: seq: 4 (over z), exp: 8 (over y, x, core).
Axes of the slice: x: 2, y: 2, z: 4, core: 2. Of those that a mesh axis runs over, the one named last changes fastest.
Arguments:
- layer_input: bfloat16 [8, 2048, 768], P('exp', 'seq'), may hold values from -9 to 9
- lengths: int32 [8, 3], P('exp'), may hold values from 64 to 1792, as said below
- routes: int32 [8, 2048, 2], P('exp', 'seq'), may hold values from 0 to 31, all different within a row
- norm1_gain: float32 [768], replicated, may hold values from 0.5 to 1.5
- qkv_weight: bfloat16 [768, 2304], replicated, may hold values from -0.21875 to 0.21875
- out_weight: bfloat16 [768, 768], replicated, may hold values from -1.25 to 1.25
- norm2_gain: float32 [768], replicated, may hold values from 0.5 to 1.5
- router_weight: bfloat16 [768, 32], replicated, may hold values from -0.15625 to 0.15625
- frozen_up: bfloat16 [16, 768, 3072], P('exp'), may hold values from -0.21875 to 0.21875
- frozen_down: bfloat16 [16, 3072, 768], P('exp'), may hold values from -0.109375 to 0.109375
- train_up: bfloat16 [16, 768, 3072], P('exp'), may hold values from -0.21875 to 0.21875
- train_down: bfloat16 [16, 3072, 768], P('exp'), may hold values from -0.109375 to 0.109375
- cotangent: bfloat16 [8, 2048, 768], P('exp', 'seq'), may hold values from -6 to 6
Outputs:
- output: bfloat16 [8, 2048, 768], P('exp', 'seq')
- input_grad: bfloat16 [8, 2048, 768], P('exp', 'seq')
- norm1_gain_grad: float32 [768], replicated
- qkv_grad: float32 [768, 2304], replicated
- out_grad: float32 [768, 768], replicated
- norm2_gain_grad: float32 [768], replicated
- router_grad: float32 [768, 32], replicated
- train_up_grad: float32 [16, 768, 3072], P('exp')
- train_down_grad: float32 [16, 3072, 768], P('exp')
- stat_roots: float32 [3], replicated
The draws below stay inside these ranges and needn't reach their ends.
Inputs may be any that keep to these rules, and one draw needn't show every extreme that they name: `lengths`: the 3 documents of a group lie end to end from its first slot, the rest of the group is padding; one document of each group has 1792 tokens, the others at most a quarter of 512.
All inputs are finite; a program needn't handle non-finite values.
Results may differ from the reference program's by a relative error of at most 0.019.
Values may be sent and summed in bfloat16 or wider, within the bound.
No kernel may reach another device: no remote copies, remote signals or barrier semaphores. Data moves between devices by JAX's collectives and lax.ppermute only.
A program may use at most 256 MiB of HBM per device.

```python
import math
from functools import partial
import jax
import jax.numpy as jnp
from jax import lax

D = 768
HEADS = 12
HEAD_DIM = 64
FF = 3072
EXPERTS = 32
FROZEN = 16
TOK_DEV = 512
NDOC = 3
MINLEN = 64
GROUP_TOK = 2048
LONGLEN = 1792
GROUPS = 8
FDEV = 2
CAP = 48
N_SEQ = 4
N_EXP = 8


def draw_layer_input(key, part):
    key = jax.random.fold_in(key, 11)
    position_share = jnp.arange(GROUP_TOK, dtype=jnp.float32)[None, :, None] / GROUP_TOK
    base_values = jnp.clip(jax.random.normal(key, (GROUPS, GROUP_TOK, D), jnp.float32), -6.0, 6.0)
    row_scale = 0.5 + position_share
    return (base_values * row_scale).astype(jnp.bfloat16)


def draw_lengths(key, part):
    key = jax.random.fold_in(key, 23)
    long_key, short_key = jax.random.split(key)
    long_index = jax.random.randint(long_key, (GROUPS, 1), 0, NDOC)
    short_len = jax.random.randint(short_key, (GROUPS, NDOC), MINLEN, TOK_DEV // (2 * (NDOC - 1)) + 1)
    return jnp.where(jnp.arange(NDOC)[None, :] == long_index, LONGLEN, short_len).astype(jnp.int32)


def shard_levels(key, extent, shards, least, largest):
    gain = 1.0
    for dim, blocks in shards:
        draws = jax.random.uniform(jax.random.fold_in(jax.random.fold_in(key, 6), dim), (blocks,), jnp.float32, least / len(shards), largest / len(shards))
        gain = gain * jnp.repeat(jnp.exp(draws), extent[dim] // blocks).reshape((-1,) + (1,) * (len(extent) - 1 - dim))
    return gain


def picks_of(rng, rows, count, top, lift):
    order = jax.random.permutation(jax.random.fold_in(rng, 1), count)
    pull = order
    for power in range(3):
        pull = pull * pull // count
    pull = pull * lift // count
    tickets = jax.random.randint(jax.random.fold_in(rng, 2), (rows, count), 0, 4096) + pull
    sure = jax.random.permutation(jax.random.fold_in(rng, 3), rows)[jnp.arange(count) % rows]
    tickets = jnp.where(jnp.arange(rows)[:, None] == sure[None, :], 1 << 14, tickets)
    score = tickets * count + jnp.arange(count)
    return lax.top_k(score.astype(jnp.int32), top)[1].astype(jnp.int32)


def normal_values(stream_key, shape, spread, most, shards=(), kind=jnp.bfloat16):
    entries = jax.random.normal(stream_key, shape, jnp.float32) * spread
    if len(shards) > 0:
        entries = shard_levels(stream_key, shape, shards, -0.22, 0.18) * entries
    return jnp.clip(entries, min=-most, max=most).astype(kind)


def setup_inputs(seed: int = 0) -> dict:
    key_list = jax.random.split(jax.random.key(seed), 14)
    layer_input = draw_layer_input(jax.random.fold_in(key_list[13], 71), 0)
    lengths = draw_lengths(jax.random.fold_in(key_list[13], 71), 0)
    routes = picks_of(key_list[2], GROUPS * GROUP_TOK, EXPERTS, 2, 512).reshape((GROUPS, GROUP_TOK, 2))
    norm1_gain = jnp.clip(1.0 + 0.1 * jax.random.normal(key_list[3], (D,), jnp.float32), 0.5, 1.5)
    qkv_weight = normal_values(key_list[4], (D, 3 * D), D ** -0.5, 0.21875)
    out_weight = normal_values(key_list[5], (D, D), (D // 32) ** -0.5, 1.25)
    norm2_gain = jnp.clip(1.0 + 0.1 * jax.random.normal(key_list[6], (D,), jnp.float32), 0.5, 1.5)
    router_weight = normal_values(key_list[7], (D, EXPERTS), (2 * D) ** -0.5, 0.15625)
    frozen_up = normal_values(key_list[8], (FROZEN, D, FF), D ** -0.5, 0.21875, ((0, 8),))
    frozen_down = normal_values(key_list[9], (FROZEN, FF, D), FF ** -0.5, 0.109375, ((0, 8),))
    train_up = normal_values(key_list[10], (EXPERTS - FROZEN, D, FF), D ** -0.5, 0.21875, ((0, 8),))
    train_down = normal_values(key_list[11], (EXPERTS - FROZEN, FF, D), FF ** -0.5, 0.109375, ((0, 8),))
    cotangent = normal_values(key_list[12], (GROUPS, GROUP_TOK, D), 1.0, 6.0, ((0, 8), (1, 4)))
    return {"layer_input": layer_input, "lengths": lengths, "routes": routes, "norm1_gain": norm1_gain, "qkv_weight": qkv_weight, "out_weight": out_weight, "norm2_gain": norm2_gain, "router_weight": router_weight, "frozen_up": frozen_up, "frozen_down": frozen_down, "train_up": train_up, "train_down": train_down, "cotangent": cotangent}


epsilon = 1e-06
masked_score = -1e+30
highest = lax.Precision.HIGHEST

@jax.custom_vjp
def low(v):
    return lax.optimization_barrier(v.astype(jnp.bfloat16)).astype(jnp.float32)

@jax.custom_vjp
def low_back(v):
    return v

def low_keep(v):
    return (low(v), None)

def low_pass(kept, grad):
    return (grad,)

def back_keep(v):
    return (v, None)

def back_low(kept, grad):
    return (low(grad),)
low.defvjp(low_keep, low_pass)
low_back.defvjp(back_keep, back_low)

def product(form, left_side, right_side):
    return jnp.einsum(form, left_side, right_side, precision=highest)

def norm_scaled(values, gain_vector):
    return values * lax.rsqrt(lax.optimization_barrier(jnp.mean(values * values, axis=-1, keepdims=True)) + epsilon) * gain_vector

def segment_index(positions, doc_bounds):
    return lax.optimization_barrier(jnp.sum((positions[:, None] >= doc_bounds[None, :]).astype(jnp.int32), axis=1))

def pair_slots(route_rows, valid_rows, expert_count, frozen_count, frozen_dev, capacity):
    flat_routes = route_rows.reshape(-1).astype(jnp.int32)
    live_pair = jnp.repeat(valid_rows, 2)
    route_onehot = (flat_routes[:, None] == jnp.arange(expert_count, dtype=jnp.int32)[None, :]) & live_pair[:, None]
    running_count = jnp.cumsum(route_onehot.astype(jnp.int32), axis=0)
    place_index = lax.optimization_barrier(jnp.sum(jnp.where(route_onehot, running_count - 1, 0), axis=1)).astype(jnp.int32)
    is_frozen = flat_routes < frozen_count
    own_index = jnp.where(is_frozen, flat_routes, flat_routes - frozen_count)
    local_slot = jnp.where(is_frozen, own_index % frozen_dev, frozen_dev + own_index % frozen_dev)
    row_index = own_index // frozen_dev * (2 * frozen_dev) + local_slot
    kept_pair = live_pair & (place_index < capacity)
    slot_index = jnp.where(kept_pair, row_index * capacity + place_index, expert_count * capacity).astype(jnp.int32)
    pair_count = flat_routes.shape[0]
    source_pair = jnp.full((expert_count * capacity,), pair_count, jnp.int32).at[slot_index].set(jnp.arange(pair_count, dtype=jnp.int32), mode='drop')
    return (slot_index, source_pair)

@jax.checkpoint
def query_block(key_heads, value_heads, key_segment, doc_bounds, query_rows, query_pos):
    positions = jnp.arange(GROUP_TOK, dtype=jnp.int32)
    query_segment = segment_index(query_pos, doc_bounds)
    allowed = (query_segment[:, None] == key_segment[None, :]) & (positions[None, :] <= query_pos[:, None])
    scores = low_back(product('qhd,khd->hqk', query_rows, key_heads) * HEAD_DIM ** (-0.5))
    scores = jnp.where(allowed[None], scores, masked_score)
    probs = low(jax.nn.softmax(scores, axis=2))
    return product('hqk,khd->qhd', probs, value_heads)

def attend_group(qkv_group, doc_bounds):
    positions = jnp.arange(GROUP_TOK, dtype=jnp.int32)
    queries = qkv_group[:, :D].reshape(GROUP_TOK, HEADS, HEAD_DIM)
    key_heads = qkv_group[:, D:2 * D].reshape(GROUP_TOK, HEADS, HEAD_DIM)
    value_heads = qkv_group[:, 2 * D:].reshape(GROUP_TOK, HEADS, HEAD_DIM)
    block_width = math.gcd(GROUP_TOK, 512)
    block_count = GROUP_TOK // block_width
    key_segment = segment_index(positions, doc_bounds)
    attended = lax.map(lambda item_pair: query_block(key_heads, value_heads, key_segment, doc_bounds, item_pair[0], item_pair[1]), (queries.reshape(block_count, block_width, HEADS, HEAD_DIM), positions.reshape(block_count, block_width)))
    return attended.reshape(GROUP_TOK, D)

@jax.checkpoint
def expert_rows(item_group):
    rows_in, up_mat, down_mat = item_group
    hidden_pre = low_back(product('rd,df->rf', rows_in, up_mat))
    activated = low(jax.nn.gelu(hidden_pre, approximate=True))
    return product('rf,fd->rd', activated, down_mat)

def layer_forward(tokens_in, gain_one, qkv_mat, out_mat, gain_two, router_mat, train_up_mat, train_down_mat, frozen_up_mat, frozen_down_mat, doc_bounds, route_rows, slot_index, source_pair):
    normed_one = low(norm_scaled(tokens_in, gain_one))
    qkv_rows = low(low_back(product('gtd,de->gte', normed_one, qkv_mat)))
    attended = lax.map(lambda item_pair: attend_group(item_pair[0], item_pair[1]), (qkv_rows, doc_bounds))
    attended = low(low_back(attended))
    branch = low_back(product('gtd,de->gte', attended, out_mat))
    mid_stream = tokens_in + branch
    normed_two = low(norm_scaled(mid_stream, gain_two))
    logits = low_back(product('gtd,de->gte', normed_two, router_mat))
    picked = jnp.take_along_axis(logits, route_rows, axis=2)
    gate_weights = jax.nn.softmax(picked, axis=2)
    block_total = GROUPS * N_SEQ
    normed_blocks = normed_two.reshape(block_total, TOK_DEV, D)
    outgoing = jax.vmap(lambda block_rows, block_source: jnp.take(block_rows, block_source // 2, axis=0, mode='fill', fill_value=0.0))(normed_blocks, source_pair)
    outgoing = low_back(outgoing)
    up_all = jnp.concatenate([frozen_up_mat.reshape(N_EXP, FDEV, D, FF), train_up_mat.reshape(N_EXP, FDEV, D, FF)], axis=1).reshape(EXPERTS, D, FF)
    down_all = jnp.concatenate([frozen_down_mat.reshape(N_EXP, FDEV, FF, D), train_down_mat.reshape(N_EXP, FDEV, FF, D)], axis=1).reshape(EXPERTS, FF, D)
    by_expert = outgoing.reshape(block_total, EXPERTS, CAP, D).transpose(1, 0, 2, 3).reshape(EXPERTS, block_total * CAP, D)
    returned = lax.map(expert_rows, (by_expert, up_all, down_all))
    returned = low(low_back(returned))
    returned = returned.reshape(EXPERTS, block_total, CAP, D).transpose(1, 0, 2, 3).reshape(block_total, EXPERTS * CAP, D)
    pair_out = jax.vmap(lambda block_rows, block_slots: jnp.take(block_rows, block_slots, axis=0, mode='fill', fill_value=0.0))(returned, slot_index)
    pair_out = pair_out.reshape(GROUPS, GROUP_TOK, 2, D)
    expert_mix = lax.optimization_barrier(jnp.sum(gate_weights[..., None] * pair_out, axis=2))
    return (mid_stream + expert_mix, (branch, expert_mix))

def reference(layer_input, lengths, routes, norm1_gain, qkv_weight, out_weight, norm2_gain, router_weight, frozen_up, frozen_down, train_up, train_down, cotangent):
    doc_bounds = jnp.cumsum(lengths, axis=1).astype(jnp.int32)
    positions = jnp.arange(GROUP_TOK, dtype=jnp.int32)
    valid_rows = positions[None, :] < doc_bounds[:, -1:]
    block_total = GROUPS * N_SEQ
    slot_index, source_pair = jax.vmap(lambda route_block, valid_block: pair_slots(route_block, valid_block, EXPERTS, FROZEN, FDEV, CAP))(routes.reshape(block_total, TOK_DEV, 2), valid_rows.reshape(block_total, TOK_DEV))
    forward_fn = partial(layer_forward, frozen_up_mat=frozen_up.astype(jnp.float32), frozen_down_mat=frozen_down.astype(jnp.float32), doc_bounds=doc_bounds, route_rows=routes.astype(jnp.int32), slot_index=slot_index, source_pair=source_pair)
    tokens_in = layer_input.astype(jnp.float32)
    primals = (tokens_in, norm1_gain.astype(jnp.float32), qkv_weight.astype(jnp.float32), out_weight.astype(jnp.float32), norm2_gain.astype(jnp.float32), router_weight.astype(jnp.float32), train_up.astype(jnp.float32), train_down.astype(jnp.float32))
    result, pull_back, aux_pair = jax.vjp(forward_fn, *primals, has_aux=True)
    grads = pull_back(cotangent.astype(jnp.float32))
    branch, expert_mix = aux_pair
    valid_mask = valid_rows.astype(jnp.float32)[:, :, None]
    valid_count = jnp.sum(valid_rows.astype(jnp.float32)) * D
    stat_roots = jnp.sqrt(jnp.stack([jnp.sum(valid_mask * tokens_in * tokens_in), jnp.sum(valid_mask * branch * branch), jnp.sum(valid_mask * expert_mix * expert_mix)]) / valid_count)
    return (result.astype(jnp.bfloat16), grads[0].astype(jnp.bfloat16), grads[1], grads[2], grads[3], grads[4], grads[5], grads[6], grads[7], stat_roots)
```

```python
import jax
import jax.numpy as jnp
from jax import lax
from jax.experimental import pallas as pl
from jax.experimental.pallas import tpu as pltpu
from jax.sharding import PartitionSpec as P

D = 768
HEADS = 12
HEAD = 64
EXPERTS = 32
FROZEN = 16
CAP = 48

EPS = 1e-06
MASKED = -1e30
BF = jnp.bfloat16
F32 = jnp.float32
TANH_A = 0.7978845608028654
TANH_B = 0.044715
GRAD_ROWS = 1536
VMEM_BYTES = 56 * 1024 * 1024


def mm(a, b):
    return jnp.dot(a, b, preferred_element_type=F32)


def mm_nt(a, b):
    return lax.dot_general(a, b, (((1,), (1,)), ((), ())), preferred_element_type=F32)


def ein(form, a, b):
    return jnp.einsum(form, a, b, preferred_element_type=F32)


def params():
    return pltpu.CompilerParams(vmem_limit_bytes=VMEM_BYTES)


def gelu_parts(h):
    h2 = h * h
    t = jnp.tanh(h * (TANH_A + (TANH_A * TANH_B) * h2))
    half = 0.5 * t + 0.5
    act = h * half
    slope = half + act * (1.0 - half) * (2.0 * TANH_A + (6.0 * TANH_A * TANH_B) * h2)
    return act, slope


def attend_kernel(
    first, last, where_ref, start_ref, q_ref, k_ref, v_ref, m_in, l_in, acc_in, *rest
):
    if last:
        m_ref, l_ref, acc_ref, out_ref = rest
    else:
        m_ref, l_ref, acc_ref = rest
    block = where_ref[0]
    rows = k_ref.shape[0]
    cols = q_ref.shape[0]

    def work():
        q = q_ref[...]
        k = k_ref[...]
        lane = lax.broadcasted_iota(jnp.int32, q.shape, 1)
        key_pos = block * rows + lax.broadcasted_iota(jnp.int32, (rows, cols), 0)
        allowed = key_pos >= start_ref[...]
        if first:
            query_pos = block * rows + lax.broadcasted_iota(jnp.int32, (rows, cols), 1)
            allowed = allowed & (key_pos <= query_pos)
        for half in range(2):
            mine = (lane < HEAD) if half == 0 else (lane >= HEAD)
            scores = mm_nt(k, jnp.where(mine, q, jnp.zeros_like(q)))
            scores = jnp.where(allowed, scores, MASKED)
            top = jnp.max(scores, axis=0, keepdims=True)
            if not first:
                old = m_in[0, half : half + 1, :]
                top = jnp.maximum(top, old)
            probs = jnp.exp(scores - top)
            total = jnp.sum(probs, axis=0, keepdims=True)
            part = slice(half * HEAD, (half + 1) * HEAD)
            value = mm(v_ref[part, :], probs.astype(BF))
            if not first:
                decay = jnp.exp(old - top)
                total = total + l_in[0, half : half + 1, :] * decay
                value = value + acc_in[part, :] * decay
            m_ref[0, half : half + 1, :] = top
            l_ref[0, half : half + 1, :] = total
            acc_ref[part, :] = value

    if first:
        work()
    else:

        @pl.when(block >= 0)
        def _():
            work()

        @pl.when(block < 0)
        def _():
            m_ref[...] = m_in[...]
            l_ref[...] = l_in[...]
            acc_ref[...] = acc_in[...]

    if last:
        for half in range(2):
            part = slice(half * HEAD, (half + 1) * HEAD)
            total = l_ref[0, half : half + 1, :]
            acc_ref[part, :] = acc_ref[part, :] / total
            l_ref[0, half : half + 1, :] = m_ref[0, half : half + 1, :] + jnp.log(total)
        out_ref[...] = acc_ref[...].T.astype(BF)


def attend_step(step, last, block, start, q, k, v_t, state):
    tok = q.shape[0]
    pairs = HEADS // 2
    first = step == 0
    stat = jax.ShapeDtypeStruct((pairs, 2, tok), F32)
    acc = jax.ShapeDtypeStruct((D, tok), F32)
    if first:
        state = (jnp.zeros(stat.shape, F32), jnp.zeros(stat.shape, F32), jnp.zeros(acc.shape, F32))
    outs = [stat, stat, acc] + ([jax.ShapeDtypeStruct((tok, D), BF)] if last else [])
    stat_spec = pl.BlockSpec((1, 2, tok), lambda p, w: (p, 0, 0))
    acc_spec = pl.BlockSpec((2 * HEAD, tok), lambda p, w: (p, 0))
    row_spec = pl.BlockSpec((tok, 2 * HEAD), lambda p, w: (0, p))
    out_specs = [stat_spec, stat_spec, acc_spec] + ([row_spec] if last else [])

    def kernel(*refs):
        attend_kernel(first, last, *refs)

    return pl.pallas_call(
        kernel,
        out_shape=outs,
        grid_spec=pltpu.PrefetchScalarGridSpec(
            num_scalar_prefetch=1,
            grid=(pairs,),
            in_specs=[
                pl.BlockSpec((1, tok), lambda p, w: (0, 0)),
                row_spec,
                row_spec,
                acc_spec,
                stat_spec,
                stat_spec,
                acc_spec,
            ],
            out_specs=out_specs,
        ),
        compiler_params=params(),
        cost_estimate=pl.CostEstimate(
            flops=4 * tok * tok * D, bytes_accessed=8 * tok * D, transcendentals=tok * tok * HEADS
        ),
        name="attend_step",
    )(block, start, q, k, v_t, *state)


def attend_back_kernel(
    blocks, start_ref, q_ref, k_ref, v_ref, do_ref, lse_ref, delta_ref, out_ref, dq_ref, k_t_ref
):
    head = pl.program_id(0)
    rows = q_ref.shape[0] // blocks
    lane = lax.broadcasted_iota(jnp.int32, (rows, 2 * HEAD), 1)
    mine = (lane // HEAD) == lax.rem(head, 2)
    low = lax.rem(head, 2) == 0
    dq_ref[...] = jnp.zeros_like(dq_ref)

    def pick(x):
        return jnp.where(low, x[:HEAD, :], x[HEAD:, :])

    def key_step(kb, carry):
        key_rows = pl.ds(pl.multiple_of(kb * rows, rows), rows)
        k = k_ref[key_rows, :]
        zero = jnp.zeros_like(k)
        k_mine = jnp.where(mine, k, zero)
        v_mine = jnp.where(mine, v_ref[key_rows, :], zero)
        k_t_ref[...] = pick(k.T)

        def pair(qb, diagonal, dk, dv):
            query_rows = pl.ds(pl.multiple_of(qb * rows, rows), rows)
            q = q_ref[query_rows, :]
            do = do_ref[query_rows, :]
            key_pos = kb * rows + lax.broadcasted_iota(jnp.int32, (rows, rows), 0)
            allowed = key_pos >= start_ref[qb]
            if diagonal:
                query_pos = kb * rows + lax.broadcasted_iota(jnp.int32, (rows, rows), 1)
                allowed = allowed & (key_pos <= query_pos)
            scores = mm_nt(k_mine, q)
            probs = jnp.where(allowed, jnp.exp(scores - lse_ref[qb, 0]), 0.0)
            dprobs = mm_nt(v_mine, do)
            dscores = (probs * (dprobs - delta_ref[qb, 0])).astype(BF)
            dv = dv + mm(probs.astype(BF), do)
            dk = dk + mm(dscores, q)
            dq_ref[qb] = dq_ref[qb] + mm(k_t_ref[...], dscores)
            return dk, dv

        empty = jnp.zeros((rows, 2 * HEAD), F32)
        dk, dv = pair(kb, True, empty, empty)
        dk, dv = lax.fori_loop(kb + 1, blocks, lambda qb, c: pair(qb, False, *c), (dk, dv))
        out_ref[kb, 1] = pick(dk.T).astype(BF)
        out_ref[kb, 2] = pick(dv.T).astype(BF)
        return carry

    lax.fori_loop(0, blocks, key_step, 0)
    for b in range(blocks):
        out_ref[b, 0] = (dq_ref[b] * HEAD**-0.5).astype(BF)


def attend_back(blocks, heads, start, qkv, do, lse, delta):
    rows = qkv.shape[0]
    tok = rows // blocks
    slabs = qkv.shape[1] // (3 * 2 * HEAD)

    def part(i):
        return pl.BlockSpec((rows, 2 * HEAD), lambda h: (0, i * slabs + h // 2))

    stat_spec = pl.BlockSpec((blocks, 1, 1, tok), lambda h: (0, h, 0, 0))

    def kernel(*refs):
        attend_back_kernel(blocks, *refs)

    return pl.pallas_call(
        kernel,
        out_shape=jax.ShapeDtypeStruct((blocks, 3, heads * HEAD, tok), BF),
        grid=(heads,),
        in_specs=[
            pl.BlockSpec((blocks, 1, tok), lambda h: (0, 0, 0)),
            part(0),
            part(1),
            part(2),
            part(0),
            stat_spec,
            stat_spec,
        ],
        out_specs=pl.BlockSpec((blocks, 3, HEAD, tok), lambda h: (0, 0, h, 0)),
        scratch_shapes=[pltpu.VMEM((blocks, HEAD, tok), F32), pltpu.VMEM((HEAD, tok), BF)],
        compiler_params=params(),
        cost_estimate=pl.CostEstimate(
            flops=5 * rows * rows * heads * HEAD,
            bytes_accessed=16 * rows * heads * HEAD,
            transcendentals=rows * rows * heads // 2,
        ),
        name="attend_back",
    )(start, qkv, qkv, qkv, do, lse, delta)


def expert_kernel(
    x_ref, g_ref, gate_ref, up_ref, down_ref, mix_ref, dx_ref, dgate_ref, xs, dos, eacc, dacc
):
    step = pl.program_id(1)
    rows = xs.shape[0]
    block = x_ref.shape

    @pl.when(step == 0)
    def _():
        xs[...] = x_ref[...].reshape(rows, D)
        dos[...] = (gate_ref[0] * g_ref[...].reshape(rows, D).astype(F32)).astype(BF)
        eacc[...] = jnp.zeros_like(eacc)
        dacc[...] = jnp.zeros_like(dacc)

    act, slope = gelu_parts(mm(xs[...], up_ref[0]))
    dhid = (mm_nt(dos[...], down_ref[0]) * slope).astype(BF)
    eacc[...] += mm(act.astype(BF), down_ref[0])
    dacc[...] += mm_nt(dhid, up_ref[0])

    @pl.when(step == pl.num_programs(1) - 1)
    def _():
        out = eacc[...]
        g = g_ref[...].reshape(rows, D).astype(F32)
        mix_ref[...] = (gate_ref[0] * out).astype(BF).reshape(block)
        dx_ref[...] = dacc[...].astype(BF).reshape(block)
        dgate_ref[0] = jnp.sum(g * out, axis=1, keepdims=True)


def expert_rows(x, g, gate, up, down):
    sources, experts = x.shape[:2]
    rows = sources * CAP
    hidden = up.shape[2]
    tile = 768
    row_spec = pl.BlockSpec((sources, 1, CAP, D), lambda e, f: (0, e, 0, 0))
    gate_spec = pl.BlockSpec((1, rows, 1), lambda e, f: (e, 0, 0))
    return pl.pallas_call(
        expert_kernel,
        out_shape=[
            jax.ShapeDtypeStruct(x.shape, BF),
            jax.ShapeDtypeStruct(x.shape, BF),
            jax.ShapeDtypeStruct((experts, rows, 1), F32),
        ],
        grid=(experts, hidden // tile),
        in_specs=[
            row_spec,
            row_spec,
            gate_spec,
            pl.BlockSpec((1, D, tile), lambda e, f: (e, 0, f)),
            pl.BlockSpec((1, tile, D), lambda e, f: (e, f, 0)),
        ],
        out_specs=[row_spec, row_spec, gate_spec],
        scratch_shapes=[
            pltpu.VMEM((rows, D), BF),
            pltpu.VMEM((rows, D), BF),
            pltpu.VMEM((rows, D), F32),
            pltpu.VMEM((rows, D), F32),
        ],
        compiler_params=params(),
        cost_estimate=pl.CostEstimate(
            flops=8 * experts * rows * D * hidden,
            bytes_accessed=4 * experts * D * hidden,
            transcendentals=experts * rows * hidden,
        ),
        name="expert_rows",
    )(x, g, gate, up, down)


def expert_grad_kernel(blocks, gate_ref, up_ref, down_ref, *refs):
    x_refs, g_refs = refs[:blocks], refs[blocks : 2 * blocks]
    dup_ref, ddown_ref, xs, dos, xs_t = refs[2 * blocks :]
    rows = xs.shape[0] // blocks

    @pl.when(pl.program_id(1) == 0)
    def _():
        for b in range(blocks):
            part = slice(b * rows, (b + 1) * rows)
            x = x_refs[b][...].reshape(rows, D)
            xs[part, :] = x
            xs_t[:, part] = x.T
            g = g_refs[b][...].reshape(rows, D).astype(F32)
            dos[part, :] = (gate_ref[0, part, :] * g).astype(BF)

    hid = mm_nt(up_ref[0].T, xs[...])
    act, slope = gelu_parts(hid)
    dhid = (mm_nt(down_ref[0], dos[...]) * slope).astype(BF)
    ddown_ref[0] = mm(act.astype(BF), dos[...])
    dup_ref[0] = mm_nt(xs_t[...], dhid)


def expert_grads(xs, gs, gate, up, down):
    blocks = len(xs)
    sources, experts = xs[0].shape[:2]
    rows = blocks * sources * CAP
    hidden = up.shape[2]
    tile = 512
    row_spec = pl.BlockSpec((sources, 1, CAP, D), lambda e, f: (0, e, 0, 0))
    up_spec = pl.BlockSpec((1, D, tile), lambda e, f: (e, 0, f))
    down_spec = pl.BlockSpec((1, tile, D), lambda e, f: (e, f, 0))

    def kernel(*refs):
        expert_grad_kernel(blocks, *refs)

    return pl.pallas_call(
        kernel,
        out_shape=[
            jax.ShapeDtypeStruct(up.shape, F32),
            jax.ShapeDtypeStruct(down.shape, F32),
        ],
        grid=(experts, hidden // tile),
        in_specs=[pl.BlockSpec((1, rows, 1), lambda e, f: (e, 0, 0)), up_spec, down_spec]
        + [row_spec] * (2 * blocks),
        out_specs=[up_spec, down_spec],
        scratch_shapes=[
            pltpu.VMEM((rows, D), BF),
            pltpu.VMEM((rows, D), BF),
            pltpu.VMEM((D, rows), BF),
        ],
        compiler_params=params(),
        cost_estimate=pl.CostEstimate(
            flops=8 * experts * rows * D * hidden,
            bytes_accessed=12 * experts * D * hidden,
            transcendentals=experts * rows * hidden,
        ),
        name="expert_grads",
    )(gate, up, down, *xs, *gs)


def expert_grads_all(xs, gs, gates, up, down):
    group = max(1, GRAD_ROWS // gates[0].shape[1])
    totals = None
    for first in range(0, len(xs), group):
        part = slice(first, first + group)
        gate = jnp.concatenate(gates[part], axis=1)
        grads = expert_grads(xs[part], gs[part], gate, up, down)
        totals = grads if totals is None else [t + g for t, g in zip(totals, grads)]
    return totals


def unit_rows(values):
    return values * lax.rsqrt(jnp.mean(values * values, axis=-1, keepdims=True) + EPS)


def unit_back(values, gain, grad):
    r = lax.rsqrt(jnp.mean(values * values, axis=-1, keepdims=True) + EPS)
    u = values * r
    scaled = grad * gain
    return r * (scaled - u * jnp.mean(scaled * u, axis=-1, keepdims=True)), u


def ring_next(x, count):
    return lax.ppermute(x, "seq", [(i, (i + 1) % count) for i in range(count)])


def ring_all(x, count):
    found = [x]
    for _ in range(count - 1):
        found.append(ring_next(found[-1], count))
    return found


def swap(x, axis):
    return lax.all_to_all(x, axis, split_axis=0, concat_axis=0, tiled=True)


def after(x, *others):
    return lax.optimization_barrier((x,) + others)[0]


def body(
    layer_input,
    lengths,
    routes,
    norm1_gain,
    qkv_weight,
    out_weight,
    norm2_gain,
    router_weight,
    frozen_up,
    frozen_down,
    train_up,
    train_down,
    cotangent,
):
    tok = layer_input.shape[1]
    n_seq = lax.axis_size("seq")
    n_exp = lax.axis_size("exp")
    rank = lax.axis_index("seq")
    heads = -(-HEADS // n_seq)
    slots = heads + heads % 2
    x_own = layer_input[0]
    g_own = cotangent[0]
    bounds = jnp.cumsum(lengths[0])

    scale = HEAD**-0.5
    w_q = qkv_weight[:, :D] * jnp.asarray(scale, BF)
    w_k = qkv_weight[:, D : 2 * D]
    w_v = qkv_weight[:, 2 * D :]
    w_parts = jnp.pad(
        qkv_weight.reshape(D, 3, HEADS, HEAD), ((0, 0), (0, 0), (0, heads * n_seq - HEADS), (0, 0))
    )
    w_groups = w_parts.reshape(D, 3, n_seq, heads * HEAD)
    w_by_group = w_groups.transpose(0, 2, 1, 3).reshape(D, n_seq * 3 * heads * HEAD)
    w_mine = lax.dynamic_index_in_dim(w_groups, rank, axis=2, keepdims=False)
    w_mine = w_mine * jnp.asarray([scale, 1.0, 1.0], BF)[None, :, None]
    w_mine = jnp.pad(w_mine, ((0, 0), (0, 0), (0, (slots - heads) * HEAD)))
    w_mine = w_mine.reshape(D, 3 * slots * HEAD)

    pos_all = jnp.arange(n_seq * tok, dtype=jnp.int32)
    start_all = jnp.max(jnp.where(pos_all[None, :] >= bounds[:, None], bounds[:, None], 0), axis=0)
    pos_own = rank * tok + jnp.arange(tok, dtype=jnp.int32)
    start_own = jnp.max(jnp.where(pos_own[None, :] >= bounds[:, None], bounds[:, None], 0), axis=0)
    valid = pos_own < bounds[-1]
    expert_ids = jnp.arange(EXPERTS, dtype=jnp.int32)[:, None]
    route_rows = routes[0]
    routed = (expert_ids == route_rows[:, 0][None, :]) | (expert_ids == route_rows[:, 1][None, :])
    live = routed & valid[None, :]
    order = jnp.arange(tok, dtype=jnp.int32)
    earlier = (order[:, None] < order[None, :]).astype(BF)
    place = mm(live.astype(BF), earlier).astype(jnp.int32)
    taken = (
        live[:, None, :]
        & (place[:, None, :] == jnp.arange(CAP, dtype=jnp.int32)[None, :, None])
    )
    pick = taken.astype(BF)

    def halves(rows):
        return [
            rows[i * FROZEN : (i + 1) * FROZEN].reshape((n_exp, FROZEN // n_exp) + rows.shape[1:])
            for i in range(2)
        ]

    def project(x):
        n1 = (unit_rows(x.astype(F32)) * norm1_gain).astype(BF)
        return n1, mm(n1, w_k).astype(BF), ein("de,td->et", w_v, n1).astype(BF)

    n1_own, k_own, v_own = project(x_own)
    q_own = mm(n1_own, w_q).astype(BF)
    n1_all = jnp.zeros((n_seq * tok, D), BF)
    x_now = x_own
    state = None
    for step in range(n_seq):
        if step == 0:
            n1, k, v_t = n1_own, k_own, v_own
        else:
            x_now = ring_next(x_now, n_seq)
            n1, k, v_t = project(x_now)
        n1_all = lax.dynamic_update_slice(n1_all, n1, (lax.rem(rank - step + n_seq, n_seq) * tok, 0))
        block = jnp.reshape(rank - step, (1,)).astype(jnp.int32)
        state = attend_step(
            step, step == n_seq - 1, block, start_own[None, :], q_own, k, v_t, state
        )
    unused, lse, attn_t, attn = state

    g_frozen, g_train = [swap(h, "exp") for h in halves(ein("ect,td->ecd", pick, g_own).astype(BF))]

    tokens_in = x_own.astype(F32)
    branch = mm(attn, out_weight)
    mid = tokens_in + branch
    n2 = (unit_rows(mid) * norm2_gain).astype(BF)
    logits = ein("de,td->et", router_weight, n2)
    gates = jax.nn.softmax(jnp.where(routed, logits, -jnp.inf), axis=0)
    slot_gate = jnp.sum(jnp.where(taken, gates[:, None, :], 0.0), axis=2)
    sent = ein("ect,td->ecd", pick, n2).astype(BF)
    x_frozen, x_train = [swap(h, "exp") for h in halves(sent)]
    gate_frozen, gate_train = [swap(h, "exp") for h in halves(slot_gate)]

    def by_expert(gate):
        return gate.transpose(1, 0, 2).reshape(gate.shape[1], -1, 1)

    mix_t, dx_t, dgate_t = expert_rows(x_train, g_train, by_expert(gate_train), train_up, train_down)
    mix_f, dx_f, dgate_f = expert_rows(
        x_frozen, g_frozen, by_expert(gate_frozen), frozen_up, frozen_down
    )

    def from_expert(dgate):
        return dgate.reshape(-1, n_exp, CAP).transpose(1, 0, 2)

    def joined(frozen_part, train_part):
        parts = [swap(frozen_part, "exp"), swap(train_part, "exp")]
        return jnp.concatenate([p.reshape((FROZEN,) + p.shape[2:]) for p in parts], axis=0)

    dx_rows = joined(dx_f, dx_t)
    dgate_slots = joined(from_expert(dgate_f), from_expert(dgate_t))
    mix_rows = joined(mix_f, mix_t)

    xs = ring_all(x_train, n_seq)
    gs = ring_all(g_train, n_seq)
    gate_blocks = [by_expert(p) for p in ring_all(gate_train, n_seq)]

    expert_mix = ein("ect,ecd->td", pick, mix_rows)
    output = (mid + expert_mix).astype(BF)
    dgates = jnp.sum(jnp.where(taken, dgate_slots[:, :, None], 0.0), axis=1)
    dlogits = (gates * (dgates - jnp.sum(gates * dgates, axis=0, keepdims=True))).astype(BF)
    router_part = ein("td,et->de", n2, dlogits)
    dn2 = ein("et,de->td", dlogits, router_weight) + ein("ect,ecd->td", pick, dx_rows)
    dx_mid, u2 = unit_back(mid, norm2_gain, dn2)
    gain2_part = jnp.sum(dn2 * u2, axis=0)
    dmid = g_own.astype(F32) + dx_mid
    dbranch = dmid.astype(BF)
    out_part = ein("td,te->de", attn, dbranch)

    out_groups = jnp.pad(out_weight, ((0, heads * n_seq * HEAD - D), (0, 0)))
    dattn = ein("te,gde->gtd", dbranch, out_groups.reshape(n_seq, heads * HEAD, D)).astype(BF)
    dattn_t = ein("de,te->dt", out_weight, dbranch)
    delta = jnp.sum((dattn_t.astype(BF).astype(F32) * attn_t).reshape(HEADS, HEAD, tok), axis=1)

    def stat_groups(stat):
        stat = jnp.pad(stat.reshape(HEADS, tok), ((0, heads * n_seq - HEADS), (0, 0)))
        return stat.reshape(n_seq, heads, 1, tok)

    do = swap(dattn, "seq").reshape(n_seq * tok, heads * HEAD)
    do = jnp.pad(do, ((0, 0), (0, (slots - heads) * HEAD)))
    stats = swap(jnp.stack([stat_groups(lse), stat_groups(delta)], axis=1), "seq")
    qkv_mine = mm(n1_all, w_mine).astype(BF)
    dqkv_t = attend_back(
        n_seq, heads, start_all.reshape(n_seq, 1, tok), qkv_mine, do, stats[:, 0], stats[:, 1]
    )
    dqkv_t = dqkv_t.reshape(n_seq, 3 * heads * HEAD, tok)
    qkv_part = ein("ntd,nct->dc", n1_all.reshape(n_seq, tok, D), dqkv_t)
    dqkv_own = swap(dqkv_t, "seq").reshape(n_seq * 3 * heads * HEAD, tok)

    pieces = swap(qkv_part.astype(BF).reshape(n_exp, D // n_exp, 3 * heads * HEAD), "exp")
    piece = jnp.sum(pieces.astype(F32), axis=0).astype(BF)
    whole = lax.all_gather(piece, ("seq", "exp"), axis=0, tiled=False)
    whole = whole.reshape(n_seq, D, 3, heads * HEAD).transpose(1, 2, 0, 3)
    qkv_total = whole.reshape(D, 3, n_seq * heads * HEAD)[:, :, :D].reshape(D, 3 * D).astype(F32)
    gain1_total = jnp.sum(qkv_total * qkv_weight.astype(F32), axis=1) / norm1_gain

    up_total, down_total = expert_grads_all(xs, gs, gate_blocks, train_up, train_down)

    dn1 = ein("dc,ct->td", w_by_group, dqkv_own)
    dx_in, unused_u = unit_back(tokens_in, norm1_gain, dn1)
    input_grad = (dmid + dx_in).astype(BF)

    mask = valid.astype(F32)[:, None]
    stat_part = jnp.stack(
        [
            jnp.sum(mask * tokens_in * tokens_in),
            jnp.sum(mask * branch * branch),
            jnp.sum(mask * expert_mix * expert_mix),
            jnp.sum(mask),
        ]
    )
    out_total, router_total = lax.psum(
        (out_part.astype(BF), router_part.astype(BF)), ("seq", "exp")
    )
    gain2_total, stat_sums = lax.psum((gain2_part, stat_part), ("seq", "exp"))
    stat_roots = jnp.sqrt(stat_sums[:3] / (stat_sums[3] * D))
    return (
        output[None],
        input_grad[None],
        gain1_total,
        qkv_total,
        out_total.astype(F32),
        gain2_total,
        router_total.astype(F32),
        up_total,
        down_total,
        stat_roots,
    )


def solution(mesh):
    return jax.shard_map(
        body,
        mesh=mesh,
        in_specs=(
            P("exp", "seq", None),
            P("exp", None),
            P("exp", "seq", None),
            P(),
            P(),
            P(),
            P(),
            P(),
            P("exp", None, None),
            P("exp", None, None),
            P("exp", None, None),
            P("exp", None, None),
            P("exp", "seq", None),
        ),
        out_specs=(
            P("exp", "seq", None),
            P("exp", "seq", None),
            P(),
            P(),
            P(),
            P(),
            P(),
            P("exp", None, None),
            P("exp", None, None),
            P(),
        ),
        check_vma=False,
    )
```

```python
import jax
import jax.numpy as jnp
from jax import lax
from jax.experimental import pallas as pl
from jax.experimental.pallas import tpu as pltpu
from jax.sharding import PartitionSpec as P

D = 768
HEADS = 12
HEAD = 64
EXPERTS = 32
FROZEN = 16
CAP = 48

EPS = 1e-06
MASKED = -1e30
BF = jnp.bfloat16
F32 = jnp.float32
TANH_A = 0.7978845608028654
TANH_B = 0.044715
GRAD_ROWS = 1536
GRAD_TILE = 768
MISC = 896
VMEM_BYTES = 56 * 1024 * 1024


def mm(a, b):
    return jnp.dot(a, b, preferred_element_type=F32)


def mm_nt(a, b):
    return lax.dot_general(a, b, (((1,), (1,)), ((), ())), preferred_element_type=F32)


def ein(form, a, b):
    return jnp.einsum(form, a, b, preferred_element_type=F32)


def mm_tn(a, b):
    return lax.dot_general(a, b, (((0,), (0,)), ((), ())), preferred_element_type=F32)


def params():
    return pltpu.CompilerParams(vmem_limit_bytes=VMEM_BYTES)


def cost(micros):
    return pl.CostEstimate(flops=int(micros * 1.1e9), bytes_accessed=0, transcendentals=0)


def whole(shape):
    return pl.BlockSpec(shape, lambda *unused: (0,) * len(shape))


def called(
    kernel,
    name,
    outs,
    info,
    operands,
    in_specs=None,
    scratch=(),
    micros=5,
    grid=(1,),
    out_specs=None,
    aliases=None,
    deps=(),
    through=(),
):
    specs = [None] * len(operands) if in_specs is None else in_specs
    specs = [whole(a.shape) if b is None else b for a, b in zip(operands, specs)]
    results = [whole(shape) for shape, unused in outs] if out_specs is None else list(out_specs)
    shapes = [jax.ShapeDtypeStruct(shape, kind) for shape, kind in outs]
    shapes += [jax.ShapeDtypeStruct(a.shape, a.dtype) for a in through]
    held = pl.BlockSpec(memory_space=pl.ANY)
    aliases = dict(aliases or {})
    for i in range(len(through)):
        aliases[1 + len(operands) + i] = len(outs) + i
    extra = len(through) + len(deps)

    def inner(info_ref, *refs):
        ins, rest = refs[: len(operands)], refs[len(operands) + extra :]
        kernel(info_ref, *ins, *rest[: len(outs)], *rest[len(outs) + len(through) :])

    call = pl.pallas_call(
        inner,
        out_shape=shapes,
        grid_spec=pltpu.PrefetchScalarGridSpec(
            num_scalar_prefetch=1,
            grid=grid,
            in_specs=specs + [held] * extra,
            out_specs=results + [held] * len(through),
            scratch_shapes=list(scratch),
        ),
        input_output_aliases=aliases,
        compiler_params=params(),
        cost_estimate=cost(micros),
        name=name,
    )
    return list(call(info, *operands, *through, *deps))


INFO = 2


def doc_start(info_ref, position):
    bound = 0
    start = jnp.zeros_like(position)
    for i in range(INFO, info_ref.shape[0]):
        bound = bound + info_ref[i]
        start = jnp.where(position >= bound, bound, start)
    return start


def doc_end(info_ref):
    bound = 0
    for i in range(INFO, info_ref.shape[0]):
        bound = bound + info_ref[i]
    return bound


def need_mask(info_ref, key_start, last_query):
    return doc_start(info_ref, jnp.full((1, 128), last_query, jnp.int32))[0, 0] > key_start


def route_kernel(local, info_ref, routes_ref, g_ref, pick_ref, train_ref, frozen_ref):
    tok = g_ref.shape[0]
    half = pick_ref.shape[0] // 2
    first, second = routes_ref[0:1, :], routes_ref[1:2, :]
    row = lax.broadcasted_iota(jnp.int32, (EXPERTS, tok), 0)
    expert = jnp.where(row < FROZEN, row + FROZEN, row - FROZEN)
    position = info_ref[0] * tok + lax.broadcasted_iota(jnp.int32, (EXPERTS, tok), 1)
    live = ((expert == first) | (expert == second)) & (position < doc_end(info_ref))
    earlier = lax.broadcasted_iota(jnp.int32, (tok, tok), 0) < lax.broadcasted_iota(
        jnp.int32, (tok, tok), 1
    )
    place = mm(jnp.where(live, 1.0, 0.0).astype(BF), jnp.where(earlier, 1.0, 0.0).astype(BF))
    place = jnp.where(live, place, -1.0)
    slot = lax.broadcasted_iota(jnp.int32, (CAP, tok), 0).astype(F32)
    sums = jnp.broadcast_to((first + second).astype(F32), (16, tok)).astype(BF)
    sum_row = lax.broadcasted_iota(jnp.int32, (16, CAP), 0)
    for part, out_ref in ((0, train_ref), (1, frozen_ref)):
        for d in range(FROZEN // local):
            found = jnp.zeros((16, CAP), F32)
            for i in range(local):
                e = part * FROZEN + d * local + i
                taken = jnp.where(place[e : e + 1, :] == slot, 1.0, 0.0).astype(BF)
                pick_ref[e * CAP : (e + 1) * CAP, :] = taken
                found = jnp.where(sum_row == i, mm_nt(sums, taken), found)
            out_ref[d, local * CAP :, :] = jnp.zeros((16, D), BF)
            out_ref[d, local * CAP :, 0:CAP] = found.astype(BF)
        rows = mm(pick_ref[part * half : (part + 1) * half, :], g_ref[...]).astype(BF)
        for d in range(FROZEN // local):
            out_ref[d, : local * CAP, :] = rows[d * local * CAP : (d + 1) * local * CAP, :]


def route(info, local, routes, g):
    tok = g.shape[0]
    sent = (FROZEN // local, local * CAP + 16, D)

    def kernel(*refs):
        route_kernel(local, *refs)

    return called(
        kernel,
        "route",
        [((EXPERTS * CAP, tok), BF), (sent, BF), (sent, BF)],
        info,
        [routes, g],
        [None, None],
        micros=6,
    )


def slot_sums(tile, local_id):
    parts = []
    for i in range(tile.shape[0]):
        turned = tile[i].astype(F32).T
        lane = lax.broadcasted_iota(jnp.int32, turned.shape, 1)
        column = jnp.sum(jnp.where(lane == local_id, turned, 0.0), axis=1, keepdims=True)
        parts.append(column[:CAP, :])
    return jnp.concatenate(parts, axis=0)


def gelu_parts(h):
    h2 = h * h
    t = jnp.tanh(h * (TANH_A + (TANH_A * TANH_B) * h2))
    half = 0.5 * t + 0.5
    act = h * half
    slope = half + act * (1.0 - half) * (2.0 * TANH_A + (6.0 * TANH_A * TANH_B) * h2)
    return act, slope


def attend_kernel(step, last, info_ref, x_ref, gain_ref, w_q_ref, w_k_ref, w_v_ref, *refs):
    first = step == 0
    refs = list(refs)
    if first:
        n1_ref, q_ref = refs[:2]
        refs = refs[2:]
    else:
        q_ref, m_in, l_in, acc_in, n1_ref = refs[:5]
        refs = refs[5:]
    if last:
        attn_ref = refs.pop(0)
        l_ref = refs.pop(0)
        m_ref, acc_ref, k_all, v_all = refs
    else:
        m_ref, l_ref, acc_ref, k_all, v_all = refs
    block = info_ref[0] - step
    rows = x_ref.shape[0]
    pairs = k_all.shape[0]

    x = x_ref[...].astype(F32)
    n1 = x * lax.rsqrt(jnp.mean(x * x, axis=1, keepdims=True) + EPS) * gain_ref[...]
    n1_ref[...] = n1.astype(BF)

    def project():
        n1 = n1_ref[...]
        for i in range(pairs // 2):
            cols = slice(i * 4 * HEAD, (i + 1) * 4 * HEAD)
            k = mm(n1, w_k_ref[:, cols]).astype(BF)
            v = mm(n1, w_v_ref[:, cols]).T.astype(BF)
            for j in range(2):
                k_all[2 * i + j] = k[:, j * 2 * HEAD : (j + 1) * 2 * HEAD]
                v_all[2 * i + j] = v[j * 2 * HEAD : (j + 1) * 2 * HEAD, :]
            if first:
                q = mm(n1, w_q_ref[:, cols]).astype(BF) * jnp.asarray(HEAD**-0.5, BF)
                for j in range(2):
                    q_ref[2 * i + j] = q[:, j * 2 * HEAD : (j + 1) * 2 * HEAD]

    def attend(masked):
        key_pos = block * rows + lax.broadcasted_iota(jnp.int32, (rows, rows), 0)
        query_pos = info_ref[0] * rows + lax.broadcasted_iota(jnp.int32, (1, rows), 1)
        start = doc_start(info_ref, query_pos)

        def pair(p, carry):
            q = q_ref[p]
            k = k_all[p]
            lane = lax.broadcasted_iota(jnp.int32, q.shape, 1)
            zero = jnp.zeros_like(q)
            found = [
                mm_nt(k, jnp.where(lane < HEAD, q, zero)),
                mm_nt(k, jnp.where(lane < HEAD, zero, q)),
            ]
            for half in range(2):
                scores = found[half]
                if masked:
                    allowed = key_pos >= start
                    if first:
                        allowed = allowed & (key_pos <= query_pos)
                    scores = jnp.where(allowed, scores, MASKED)
                top = jnp.max(scores, axis=0, keepdims=True)
                if not first:
                    old = m_in[p, half : half + 1, :]
                    top = jnp.maximum(top, old)
                probs = jnp.exp(scores - top)
                total = jnp.sum(probs, axis=0, keepdims=True)
                value = mm(v_all[p, half * HEAD : (half + 1) * HEAD, :], probs.astype(BF))
                part = pl.ds(pl.multiple_of(p * 2 * HEAD + half * HEAD, HEAD), HEAD)
                if not first:
                    decay = jnp.exp(old - top)
                    total = total + l_in[p, half : half + 1, :] * decay
                    value = value + acc_in[part, :] * decay
                m_ref[p, half : half + 1, :] = top
                l_ref[p, half : half + 1, :] = total
                acc_ref[part, :] = value
            return carry

        lax.fori_loop(0, pairs, pair, 0)

    if first:
        project()
        attend(True)
    else:
        masked = need_mask(info_ref, block * rows, info_ref[0] * rows + rows - 1)

        @pl.when(block >= 0)
        def _():
            project()

        @pl.when((block >= 0) & masked)
        def _():
            attend(True)

        @pl.when((block >= 0) & jnp.logical_not(masked))
        def _():
            attend(False)

        @pl.when(block < 0)
        def _():
            m_ref[...] = m_in[...]
            l_ref[...] = l_in[...]
            acc_ref[...] = acc_in[...]

    if last:
        for p in range(pairs):
            for half in range(2):
                part = slice((2 * p + half) * HEAD, (2 * p + half + 1) * HEAD)
                total = l_ref[p, half : half + 1, :]
                acc_ref[part, :] = acc_ref[part, :] / total
                l_ref[p, half : half + 1, :] = m_ref[p, half : half + 1, :] + jnp.log(total)
            part = slice(p * 2 * HEAD, (p + 1) * 2 * HEAD)
            attn_ref[:, part] = acc_ref[part, :].T.astype(BF)


def attend_step(step, last, info, x, gain, w, state, deps=(), through=()):
    tok = x.shape[0]
    pairs = HEADS // 2
    stat, acc = ((pairs, 2, tok), F32), ((D, tok), F32)
    row, by_pair = ((tok, D), BF), ((pairs, tok, 2 * HEAD), BF)
    outs = [row] + ([by_pair] if step == 0 else []) + ([row, stat] if last else [stat, stat, acc])
    scratch = [pltpu.VMEM(*by_pair), pltpu.VMEM((pairs, 2 * HEAD, tok), BF)]
    if last:
        scratch = [pltpu.VMEM(*stat), pltpu.VMEM(*acc)] + scratch

    def kernel(*refs):
        attend_kernel(step, last, *refs)

    square = (D, D)
    return called(
        kernel,
        "attend_step",
        outs,
        info,
        [x, gain, w, w, w, *state],
        [
            None,
            None,
            pl.BlockSpec(square, lambda i, r: (0, 0)),
            pl.BlockSpec(square, lambda i, r: (0, 1)),
            pl.BlockSpec(square, lambda i, r: (0, 2)),
        ]
        + [None] * len(state),
        scratch,
        micros=13,
        deps=deps,
        through=through,
    )


def attend_back_kernel(blocks, heads, info_ref, qkv_ref, misc_ref, *refs):
    n1_refs, do_refs, out_refs = [refs[i * blocks : (i + 1) * blocks] for i in range(3)]
    part_ref, dq_ref, dk_ref, dv_ref, k_mine, v_mine, k_t, do_all, lse_all, delta_all, out_all = refs[
        3 * blocks :
    ]
    rows = qkv_ref.shape[0] // blocks
    tiles, deep, width = do_refs[0].shape
    lane = lax.broadcasted_iota(jnp.int32, (rows, 2 * HEAD), 1)
    dq_ref[...] = jnp.zeros_like(dq_ref)

    def turn(b):
        return lax.rem(info_ref[0] - b + blocks, blocks)

    for b in range(blocks):
        do_all[b] = do_refs[b][:, :width, :].reshape(rows, width)
        stats = [do_refs[b][t, width:, :].astype(F32) for t in range(tiles)]
        stats = jnp.concatenate(stats, axis=1)
        delta_all[b] = stats[:heads] + stats[heads : 2 * heads]
        lse_all[b] = stats[2 * heads : 3 * heads] + stats[3 * heads : 4 * heads]

    def key_step(kb, carry):
        kt = turn(kb)
        key_rows = pl.ds(pl.multiple_of(kt * rows, rows), rows)
        for h in range(heads):
            first = (h // 2) * 2 * HEAD
            k = qkv_ref[key_rows, width + first : width + first + 2 * HEAD]
            v = qkv_ref[key_rows, 2 * width + first : 2 * width + first + 2 * HEAD]
            mine = (lane < HEAD) if h % 2 == 0 else (lane >= HEAD)
            zero = jnp.zeros_like(k)
            k_mine[h] = jnp.where(mine, k, zero)
            v_mine[h] = jnp.where(mine, v, zero)
            k_t[h] = k.T[(h % 2) * HEAD : (h % 2 + 1) * HEAD, :]
        dk_ref[...] = jnp.zeros_like(dk_ref)
        dv_ref[...] = jnp.zeros_like(dv_ref)

        def pair(qb, diagonal, masked):
            qt = turn(qb)
            query_rows = pl.ds(pl.multiple_of(qt * rows, rows), rows)
            if masked:
                key_pos = kb * rows + lax.broadcasted_iota(jnp.int32, (rows, rows), 0)
                query_pos = qb * rows + lax.broadcasted_iota(jnp.int32, (1, rows), 1)
                allowed = key_pos >= doc_start(info_ref, query_pos)
                if diagonal:
                    allowed = allowed & (key_pos <= query_pos)

            def of_head(h):
                cols = slice((h // 2) * 2 * HEAD, (h // 2 + 1) * 2 * HEAD)
                return qkv_ref[query_rows, cols], do_all[qt, :, cols]

            def products(h):
                q, do = of_head(h)
                return mm_nt(k_mine[h], q), mm_nt(v_mine[h], do)

            later = products(0)
            for h in range(heads):
                scores, dprobs = later
                if h + 1 < heads:
                    later = products(h + 1)
                q, do = of_head(h)
                probs = jnp.exp(scores - lse_all[qt, h : h + 1, :])
                if masked:
                    probs = jnp.where(allowed, probs, 0.0)
                dscores = (probs * (dprobs - delta_all[qt, h : h + 1, :])).astype(BF)
                dv_ref[h] += mm(probs.astype(BF), do)
                dk_ref[h] += mm(dscores, q)
                dq_ref[qt, h] += mm(k_t[h], dscores)

        pair(kb, True, True)

        def query_step(qb, carry):
            masked = need_mask(info_ref, kb * rows, qb * rows + rows - 1)

            @pl.when(masked)
            def _():
                pair(qb, False, True)

            @pl.when(jnp.logical_not(masked))
            def _():
                pair(qb, False, False)

            return carry

        lax.fori_loop(kb + 1, blocks, query_step, 0)
        for h in range(heads):
            part = slice((h % 2) * HEAD, (h % 2 + 1) * HEAD)
            for i, grad_ref in ((1, dk_ref), (2, dv_ref)):
                at = (i * heads + h) * HEAD
                out_all[kt, at : at + HEAD, :] = grad_ref[h].T[part, :].astype(BF)
        return carry

    lax.fori_loop(0, blocks, key_step, 0)
    total = 0.0
    for b in range(blocks):
        for h in range(heads):
            out_all[b, h * HEAD : (h + 1) * HEAD, :] = (dq_ref[b, h] * HEAD**-0.5).astype(BF)
        grads = out_all[b]
        out_refs[b][...] = grads
        total = total + mm(grads, n1_refs[b][...])
    part_ref[:, :MISC] = misc_ref[...]
    part_ref[:, MISC:] = total.T.astype(BF)


def attend_back(heads, info, qkv, misc, n1, dos, deps):
    rows = qkv.shape[0]
    blocks = len(dos)
    tiles, deep, width = dos[0].shape
    tok = rows // blocks
    cols = 3 * heads * HEAD

    def kernel(*refs):
        attend_back_kernel(blocks, heads, *refs)

    *grads, part = called(
        kernel,
        "attend_back",
        [((cols, tok), BF)] * blocks + [((D, MISC + cols), BF)],
        info,
        [qkv, misc, *n1, *dos],
        scratch=[
            pltpu.VMEM((blocks, heads, HEAD, tok), F32),
            pltpu.VMEM((heads, tok, 2 * HEAD), F32),
            pltpu.VMEM((heads, tok, 2 * HEAD), F32),
            pltpu.VMEM((heads, tok, 2 * HEAD), BF),
            pltpu.VMEM((heads, tok, 2 * HEAD), BF),
            pltpu.VMEM((heads, HEAD, tok), BF),
            pltpu.VMEM((blocks, tok, width), BF),
            pltpu.VMEM((blocks, heads, tok), F32),
            pltpu.VMEM((blocks, heads, tok), F32),
            pltpu.VMEM((blocks, cols, tok), BF),
        ],
        micros=32,
        deps=deps,
    )
    return grads, part


def project_back_kernel(blocks, info_ref, w_ref, *refs):
    out_ref = refs[blocks]
    rows = refs[0].shape[0]
    for b in range(blocks):
        out_ref[b * rows : (b + 1) * rows, :] = mm_nt(refs[b][...], w_ref[...]).astype(BF)


def project_back(info, w, n1, deps, through):
    blocks = len(n1)

    def kernel(*refs):
        project_back_kernel(blocks, *refs)

    shape = (blocks * n1[0].shape[0], w.shape[0])
    return called(
        kernel, "project_back", [(shape, BF)], info, [w, *n1], micros=1, deps=deps, through=through
    )


def slot_gate(own, sums, x, router):
    lane = lax.broadcasted_iota(jnp.int32, (x.shape[0], router.shape[1]), 1)
    other = sums.astype(jnp.int32) - own
    signs = jnp.where(lane == own, 1.0, 0.0) - jnp.where(lane == other, 1.0, 0.0)
    margin = jnp.sum(mm(x, router) * signs, axis=1, keepdims=True)
    return 1.0 / (1.0 + jnp.exp(-margin)), signs


def expert_kernel(
    first_id,
    info_ref,
    x_ref,
    g_ref,
    sums_ref,
    router_ref,
    up_ref,
    down_ref,
    mix_ref,
    dx_ref,
    do_ref,
    drouter_ref,
    xs,
    dos,
    gate_ref,
    signs_ref,
    eacc,
    dacc,
):
    expert = pl.program_id(0)
    step = pl.program_id(1)
    rows = xs.shape[0]
    block = x_ref.shape

    @pl.when(step == 0)
    def _():
        x = x_ref[...].reshape(rows, D)
        xs[...] = x
        own = first_id + info_ref[1] * pl.num_programs(0) + expert
        gate, signs = slot_gate(own, slot_sums(sums_ref, expert), x, router_ref[...])
        gate_ref[...] = gate
        signs_ref[...] = signs
        do = (gate * g_ref[...].reshape(rows, D).astype(F32)).astype(BF)
        dos[...] = do
        do_ref[...] = do.reshape(block)

    act, slope = gelu_parts(mm(xs[...], up_ref[0]))
    dhid = (mm_nt(dos[...], down_ref[0]) * slope).astype(BF)
    out = mm(act.astype(BF), down_ref[0])
    dx = mm_nt(dhid, up_ref[0])

    @pl.when(step == 0)
    def _():
        eacc[...] = out
        dacc[...] = dx

    @pl.when(step > 0)
    def _():
        eacc[...] += out
        dacc[...] += dx

    @pl.when(step == pl.num_programs(1) - 1)
    def _():
        out = eacc[...]
        gate = gate_ref[...]
        g = g_ref[...].reshape(rows, D).astype(F32)
        mix_ref[...] = (gate * out).astype(BF).reshape(block)
        dgate = jnp.sum(g * out, axis=1, keepdims=True)
        dlogits = (gate * (1.0 - gate) * dgate * signs_ref[...]).astype(BF)
        dx_ref[...] = (dacc[...] + mm_nt(dlogits, router_ref[...])).astype(BF).reshape(block)
        drouter = mm_tn(dlogits, xs[...])

        @pl.when(expert == 0)
        def _():
            drouter_ref[...] = drouter

        @pl.when(expert > 0)
        def _():
            drouter_ref[...] += drouter


def expert_rows(first_id, info, x, g, router, up, down, deps, through=()):
    sources, experts = x.shape[:2]
    rows = sources * CAP
    hidden = up.shape[2]
    tile = 1536
    row_spec = pl.BlockSpec((sources, 1, CAP, D), lambda e, f, r: (0, e, 0, 0))

    def kernel(*refs):
        expert_kernel(first_id, *refs)

    return called(
        kernel,
        "expert_rows",
        [(x.shape, BF), (x.shape, BF), (x.shape, BF), ((router.shape[1], D), F32)],
        info,
        [x, g, g, router, up, down],
        [
            row_spec,
            pl.BlockSpec((sources, CAP, D), lambda e, f, r: (0, e, 0)),
            pl.BlockSpec((sources, 16, 128), lambda e, f, r: (0, experts * CAP // 16, 0)),
            None,
            pl.BlockSpec((1, D, tile), lambda e, f, r: (e, 0, f)),
            pl.BlockSpec((1, tile, D), lambda e, f, r: (e, f, 0)),
        ],
        [
            pltpu.VMEM((rows, D), BF),
            pltpu.VMEM((rows, D), BF),
            pltpu.VMEM((rows, 1), F32),
            pltpu.VMEM((rows, 128), F32),
            pltpu.VMEM((rows, D), F32),
            pltpu.VMEM((rows, D), F32),
        ],
        micros=23,
        grid=(experts, hidden // tile),
        out_specs=[row_spec, row_spec, row_spec, whole((router.shape[1], D))],
        deps=deps,
        through=through,
    )


def gated_kernel(count, info_ref, router_ref, *refs):
    x_refs, g_refs, sum_refs, out_refs = [refs[i * count : (i + 1) * count] for i in range(4)]
    sources, experts = x_refs[0].shape[:2]
    for b in range(count):
        for e in range(experts):
            own = FROZEN + info_ref[1] * experts + e
            x = x_refs[b][:, e].reshape(sources * CAP, D)
            gate, unused = slot_gate(own, slot_sums(sum_refs[b], e), x, router_ref[...])
            g = g_refs[b][:, e * CAP : (e + 1) * CAP, :].reshape(sources * CAP, D).astype(F32)
            out_refs[b][:, e] = (gate * g).astype(BF).reshape(sources, CAP, D)


def gated(info, router, xs, gs, sums, deps=()):
    count = len(xs)

    def kernel(*refs):
        gated_kernel(count, *refs)

    return called(
        kernel,
        "gated",
        [(x.shape, BF) for x in xs],
        info,
        [router, *xs, *gs, *sums],
        micros=1,
        deps=deps,
    )


def expert_grad_kernel(group, add, info_ref, ins, dup_ref, ddown_ref, done_ref, xs, dos):
    up_ref, down_ref = ins[:2]
    x_refs, do_refs = ins[2 : 2 + group], ins[2 + group : 2 + 2 * group]
    rows = xs.shape[0] // group

    @pl.when(pl.program_id(0) == 0)
    def _():
        done_ref[...] = jnp.zeros_like(done_ref)
        for b in range(group):
            part = slice(b * rows, (b + 1) * rows)
            xs[part, :] = x_refs[b][...].reshape(rows, D)
            dos[part, :] = do_refs[b][...].reshape(rows, D)

    act, slope = gelu_parts(mm(xs[...], up_ref[0]))
    dhid = (mm_nt(dos[...], down_ref[0]) * slope).astype(BF)
    ddown = mm_tn(act.astype(BF), dos[...])
    dup = mm_tn(xs[...], dhid)
    if add:
        ddown = ddown + ins[-1][0]
        dup = dup + ins[-2][0]
    ddown_ref[0] = ddown
    dup_ref[0] = dup


def expert_grads(expert, span, first, group, info, xs, dos, up, down, totals, deps, through):
    sources, experts = xs[0].shape[:2]
    rows = group * sources * CAP
    tile = GRAD_TILE
    start, count = span
    add = first > 0
    up_spec = pl.BlockSpec((1, D, tile), lambda f, r: (expert, 0, start + f))
    down_spec = pl.BlockSpec((1, tile, D), lambda f, r: (expert, start + f, 0))
    in_specs = [up_spec, down_spec]
    in_specs += [pl.BlockSpec((sources, 1, CAP, D), lambda f, r: (0, expert, 0, 0))] * (2 * group)
    part = slice(first, first + group)
    operands = [up, down, *xs[part], *dos[part]]
    aliases = {}
    if totals is not None:
        aliases = {1 + len(operands): 0, 2 + len(operands): 1}
        in_specs += [up_spec, down_spec] if add else [pl.BlockSpec(memory_space=pl.ANY)] * 2
        operands += list(totals)

    def kernel(info_ref, *refs):
        ins, rest = refs[: len(operands)], refs[len(operands) :]
        expert_grad_kernel(group, add, info_ref, ins, *rest)

    return called(
        kernel,
        "expert_grads",
        [(up.shape, F32), (down.shape, F32), ((8, 128), F32)],
        info,
        operands,
        in_specs,
        [pltpu.VMEM((rows, D), BF), pltpu.VMEM((rows, D), BF)],
        micros=9 * count,
        grid=(count,),
        out_specs=[up_spec, down_spec, whole((8, 128))],
        aliases=aliases,
        deps=deps,
        through=through,
    )


def expert_grads_part(expert, span, info, xs, dos, up, down, totals, deps, through):
    blocks = len(xs)
    sources, experts = xs[0].shape[:2]
    group = max(1, min(blocks, GRAD_ROWS // (sources * CAP)))
    for first in range(0, blocks, group):
        dup, ddown, done, *through = expert_grads(
            expert, span, first, group, info, xs, dos, up, down, totals, deps, through
        )
        totals = [dup, ddown]
    return totals, [done, *through]


def token_forward_kernel(
    info_ref, attn_ref, x_ref, gain_ref, w_ref, pick_ref, mid_ref, square_ref, train_ref, frozen_ref
):
    tok = x_ref.shape[0]
    half = pick_ref.shape[0] // 2
    branch = mm(attn_ref[...], w_ref[...])
    mid = x_ref[...].astype(F32) + branch
    mid_ref[...] = mid
    r = lax.rsqrt(jnp.mean(mid * mid, axis=1, keepdims=True) + EPS)
    n2 = (mid * r * gain_ref[...]).astype(BF)
    train_ref[...] = mm(pick_ref[:half, :], n2).astype(BF)
    frozen_ref[...] = mm(pick_ref[half:, :], n2).astype(BF)
    position = info_ref[0] * tok + lax.broadcasted_iota(jnp.int32, (tok, D), 0)
    square = jnp.where(position < doc_end(info_ref), branch * branch, 0.0)
    square_ref[...] = jnp.sum(square, axis=0, keepdims=True)


def token_forward(info, attn, x, gain, w, pick):
    tok = x.shape[0]
    half = ((pick.shape[0] // 2, D), BF)
    return called(
        token_forward_kernel,
        "token_forward",
        [((tok, D), F32), ((1, D), F32), half, half],
        info,
        [attn, x, gain, w, pick],
        [None] * 5,
        micros=6,
    )


def token_back_kernel(
    heads,
    groups,
    info_ref,
    pick_ref,
    dx_t_ref,
    dx_f_ref,
    mid_ref,
    g_ref,
    gain_ref,
    w_ref,
    wg_ref,
    attn_ref,
    lse_ref,
    head_ref,
    *refs,
):
    send_refs = refs[:groups]
    dmid_ref, dbranch_ref, dgain_ref = refs[groups:]
    tiles, deep, width = send_refs[0].shape
    tok = mid_ref.shape[0]
    half = pick_ref.shape[0] // 2

    dn2 = mm_tn(pick_ref[:half, :], dx_t_ref[...].reshape(half, D))
    dn2 = dn2 + mm_tn(pick_ref[half:, :], dx_f_ref[...].reshape(half, D))
    mid = mid_ref[...]
    r = lax.rsqrt(jnp.mean(mid * mid, axis=1, keepdims=True) + EPS)
    u = mid * r
    dgain_ref[...] = jnp.sum(dn2 * u, axis=0, keepdims=True)
    scaled = dn2 * gain_ref[...]
    dmid = g_ref[...].astype(F32) + r * (scaled - u * jnp.mean(scaled * u, axis=1, keepdims=True))
    dmid_ref[...] = dmid
    dbranch = dmid.astype(BF)
    dbranch_ref[...] = dbranch

    dattn = mm_nt(dbranch, w_ref[...]).astype(BF).astype(F32)
    prod = dattn * attn_ref[...].astype(F32)
    high = prod.astype(BF)
    low = (prod - high.astype(F32)).astype(BF)
    for turn in range(groups):
        g = lax.rem(info_ref[0] + turn, groups)
        sent = mm_nt(dbranch, wg_ref[g]).astype(BF)
        delta = mm_nt(head_ref[g], high) + mm_nt(head_ref[g], low)
        parts = []
        for stat in (delta[:heads], lse_ref[g][:heads]):
            high_part = stat.astype(BF).astype(F32)
            parts += [high_part, stat - high_part]
        blank = jnp.zeros((16 - 4 * heads, tok), F32)
        stats = jnp.concatenate(parts + [blank], axis=0).astype(BF)
        for t in range(tiles):
            part = slice(t * width, (t + 1) * width)
            send_refs[turn][t, :width, :] = sent[part, :]
            send_refs[turn][t, width:, :] = stats[:, part]


def token_back(
    heads, groups, width, info, pick, dx_t, dx_f, mid, g, gain, w, w_groups, attn, lse, head_rows, deps
):
    tok = mid.shape[0]
    tiles = tok // width

    def kernel(*refs):
        token_back_kernel(heads, groups, *refs)

    outs = [((tiles, width + 16, width), BF)] * groups
    operands = [pick, dx_t, dx_f, mid, g, gain, w, w_groups, attn, lse, head_rows]
    found = called(
        kernel,
        "token_back",
        outs + [((tok, D), F32), ((tok, D), BF), ((1, D), F32)],
        info,
        operands,
        micros=10,
        deps=deps,
    )
    return [found[:groups]] + found[groups:]


def token_mix_kernel(
    info_ref, pick_ref, mix_ref, mid_ref, x_ref, attn_ref, dbranch_ref, rt_ref, rf_ref, dgain_ref, square_ref, out_ref, misc_ref
):
    tok = mid_ref.shape[0]
    half = pick_ref.shape[0] // 2
    mix = 0.0
    for i in range(2):
        rows = mix_ref[:, i].reshape(half, D)
        mix = mix + mm_tn(pick_ref[i * half : (i + 1) * half, :], rows)
    out_ref[...] = (mid_ref[...] + mix).astype(BF)
    valid = info_ref[0] * tok + lax.broadcasted_iota(jnp.int32, (tok, D), 0) < doc_end(info_ref)
    x = x_ref[...].astype(F32)
    stats = [
        jnp.sum(jnp.where(valid, x * x, 0.0)),
        jnp.sum(square_ref[...]),
        jnp.sum(jnp.where(valid, mix * mix, 0.0)),
        jnp.clip(doc_end(info_ref) - info_ref[0] * tok, 0, tok).astype(F32),
    ]
    misc_ref[:, :D] = mm_tn(attn_ref[...], dbranch_ref[...]).astype(BF)
    tail = (rt_ref[...] + rf_ref[...]).T
    gains = jnp.broadcast_to(dgain_ref[...], (8, D)).T[:, 0:1]
    row = lax.broadcasted_iota(jnp.int32, tail.shape, 0)
    lane = lax.broadcasted_iota(jnp.int32, tail.shape, 1)
    tail = jnp.where(lane < EXPERTS, tail, 0.0) + jnp.where(lane == EXPERTS, gains, 0.0)
    for i, stat in enumerate(stats):
        tail = tail + jnp.where((lane == EXPERTS + 1 + i) & (row == 0), stat, 0.0)
    misc_ref[:, D : D + 128] = tail.astype(BF)


def token_mix(info, pick, mix, mid, x, attn, dbranch, router_t, router_f, dgain, square):
    tok = mid.shape[0]
    operands = [pick, mix, mid, x, attn, dbranch, router_t, router_f, dgain, square]
    return called(
        token_mix_kernel,
        "token_mix",
        [((tok, D), BF), ((D, MISC), BF)],
        info,
        operands,
        micros=1,
    )


def input_grad_kernel(heads, blocks, info_ref, x_ref, gain_ref, dmid_ref, w_ref, *refs):
    grad_refs, out_ref = refs[:blocks], refs[blocks]
    wide = heads * HEAD
    dn1 = 0.0
    for turn in range(blocks):
        g = lax.rem(info_ref[0] + turn, blocks)
        for c in range(3):
            rows = pl.ds(pl.multiple_of(c * blocks * wide + g * wide, HEAD), wide)
            part = grad_refs[turn][c * wide : (c + 1) * wide, :]
            dn1 = dn1 + mm_tn(part, w_ref[rows, :])
    x = x_ref[...].astype(F32)
    r = lax.rsqrt(jnp.mean(x * x, axis=1, keepdims=True) + EPS)
    u = x * r
    scaled = dn1 * gain_ref[...]
    dx = r * (scaled - u * jnp.mean(scaled * u, axis=1, keepdims=True))
    out_ref[...] = (dmid_ref[...] + dx).astype(BF)


def input_grad_rows(heads, info, x, gain, dmid, w_t, grads, deps):
    blocks = len(grads)

    def kernel(*refs):
        input_grad_kernel(heads, blocks, *refs)

    operands = [x, gain, dmid, w_t, *grads]
    return called(
        kernel, "input_grad", [(x.shape, BF)], info, operands, micros=8, deps=deps
    )[0]


def sum_kernel(info_ref, a_ref, out_ref):
    total = a_ref[0].astype(F32)
    for i in range(1, a_ref.shape[0]):
        total = total + a_ref[i].astype(F32)
    out_ref[...] = total.astype(BF)


def sum_parts(info, a, deps):
    return called(sum_kernel, "sum_parts", [(a.shape[1:], BF)], info, [a], micros=3, deps=deps)[0]


def join_kernel(info_ref, *refs):
    found, out_ref, again_ref = refs[:-2], refs[-2], refs[-1]
    total = found[0][:, :MISC].astype(F32)
    for ref in found[1:]:
        total = total + ref[:, :MISC].astype(F32)
    out_ref[:, :MISC] = total.astype(BF)
    cols = found[0].shape[1] - MISC
    for i, ref in enumerate(found):
        out_ref[:, MISC + i * cols : MISC + (i + 1) * cols] = ref[:, MISC:]
    again_ref[...] = out_ref[...]


def join_blocks(info, found, deps):
    rows, cols = found[0].shape
    shape = (rows, MISC + len(found) * (cols - MISC))
    return called(
        join_kernel, "join_blocks", [(shape, BF)] * 2, info, list(found), micros=3, deps=deps
    )


def layout_kernel(heads, groups, info_ref, here_ref, there_ref, w_ref, gain_ref, qkv_ref, out_ref, tail_ref, dgain_ref):
    same = lax.rem(pl.program_id(0), 2) == lax.rem(info_ref[1], 2)
    wide = heads * HEAD
    pieces = jnp.where(same, here_ref[0], there_ref[0])
    out_ref[...] = pieces[:, :D].astype(F32)
    tail_ref[...] = pieces[:, D : D + 128].astype(F32)
    for turn in range(groups):
        g = lax.rem(info_ref[0] - turn + groups, groups)
        for c in range(3):
            at = MISC + (3 * turn + c) * wide
            grad = pieces[:, at : at + wide].astype(F32)
            for g_now in range(groups):
                first = g_now * wide
                cols = min(wide, D - first)
                if cols <= 0:
                    continue
                to = c * D + first

                @pl.when(g == g_now)
                def _():
                    qkv_ref[:, to : to + cols] = grad[:, :cols]

    total = jnp.sum(qkv_ref[...] * w_ref[...].astype(F32), axis=1, keepdims=True)
    dgain_ref[...] = total


def layout(heads, groups, info, here, there, w, gain, deps):
    chips, rows, width = here.shape

    def kernel(*refs):
        layout_kernel(heads, groups, *refs)

    piece_spec = pl.BlockSpec((1, rows, width), lambda e, r: ((e // 2) ^ (r[1] // 2), 0, 0))

    def row_spec(cols):
        return pl.BlockSpec((rows, cols), lambda e, r: (e, 0))

    return called(
        kernel,
        "layout",
        [((D, 3 * D), F32), ((D, D), F32), ((D, 128), F32), ((D, 1), F32)],
        info,
        [here, there, w, gain],
        [piece_spec, piece_spec, row_spec(3 * D), None],
        micros=13,
        grid=(2 * chips,),
        out_specs=[row_spec(3 * D), row_spec(D), row_spec(128), row_spec(1)],
        deps=deps,
    )


def shifted(x, by, count):
    return lax.ppermute(x, "seq", [(i, (i + by) % count) for i in range(count)])


def swap(x, axis):
    return lax.all_to_all(x, axis, split_axis=0, concat_axis=0, tiled=True)


def both_ways(found, step, count):
    up = shifted(found[0], 1, count)
    if 2 * step < count:
        return [up, shifted(found[1], -1, count)]
    return [up]


def body(
    layer_input,
    lengths,
    routes,
    norm1_gain,
    qkv_weight,
    out_weight,
    norm2_gain,
    router_weight,
    frozen_up,
    frozen_down,
    train_up,
    train_down,
    cotangent,
):
    tok = layer_input.shape[1]
    n_seq = lax.axis_size("seq")
    n_exp = lax.axis_size("exp")
    rank = lax.axis_index("seq")
    column = lax.axis_index("exp")
    heads = -(-HEADS // n_seq)
    wide = heads * HEAD
    width = (heads + heads % 2) * HEAD
    local = FROZEN // n_exp
    x_own = layer_input[0]
    g_own = cotangent[0]
    gain1 = norm1_gain[None, :]
    gain2 = norm2_gain[None, :]
    info = jnp.concatenate([jnp.stack([rank, column]).astype(jnp.int32), lengths[0]])

    w_t = qkv_weight.T
    w_parts = jnp.pad(w_t.reshape(3, D, D), ((0, 0), (0, n_seq * wide - D), (0, 0)))
    w_mine = lax.dynamic_slice_in_dim(w_parts, rank * wide, wide, axis=1)
    w_mine = w_mine * jnp.asarray([HEAD**-0.5, 1.0, 1.0], BF)[:, None, None]
    w_mine = jnp.pad(w_mine, ((0, 0), (0, width - wide), (0, 0))).reshape(3 * width, D)
    w_parts = w_parts.reshape(3 * n_seq * wide, D)
    out_groups = jnp.pad(out_weight, ((0, n_seq * wide - D), (0, 0)))
    out_groups = jnp.pad(out_groups.reshape(n_seq, wide, D), ((0, 0), (0, width - wide), (0, 0)))
    feature_head = jnp.arange(D, dtype=jnp.int32) // HEAD
    row_id = jnp.arange(8, dtype=jnp.int32)[None, :] + heads * jnp.arange(n_seq, dtype=jnp.int32)[:, None]
    row_id = jnp.where(jnp.arange(8)[None, :] < heads, row_id, -1)
    head_rows = (row_id[:, :, None] == feature_head[None, None, :]).astype(BF)
    router = jnp.pad(router_weight, ((0, 0), (0, 128 - EXPERTS)))

    pick, g_train, g_frozen = route(info, local, routes[0].T, g_own)
    g_train = swap(g_train, "exp")
    g_frozen = swap(g_frozen, "exp")

    x_now = x_own
    n1_list = []
    state = ()
    sums_own = g_train[:, local * CAP :, :128]
    g_rows = g_train[:, : local * CAP]
    for step in range(n_seq):
        last = step == n_seq - 1
        x_next = None if last else shifted(x_now, 1, n_seq)
        found = attend_step(
            step,
            last,
            info,
            x_now,
            gain1,
            qkv_weight,
            state,
            deps=[g_frozen] if last else [],
            through=[g_rows] if step == n_seq - 2 else [],
        )
        if step == n_seq - 2:
            g_rows = found.pop()
        n1_list.append(found[0])
        state = tuple(found[1:]) if step == 0 else (state[0],) + tuple(found[1:])
        x_now = x_next
    unused_q, attn, lse = state

    mid, branch_squares, rows_train, rows_frozen = token_forward(
        info, attn, x_own, gain2, out_weight, pick
    )
    x_train = swap(rows_train.reshape(n_exp, local, CAP, D), "exp")
    x_frozen = swap(rows_frozen.reshape(n_exp, local, CAP, D), "exp")

    steps = range(1, n_seq // 2 + 1)
    g_steps, x_steps = [[g_rows, g_rows]], []
    for step in steps:
        g_steps.append(both_ways(g_steps[-1], step, n_seq))
    g_steps = g_steps[1:]
    sums = {by: shifted(sums_own, by, n_seq) for by in range(1, n_seq)}
    sum_steps = [
        [sums[step]] + ([sums[n_seq - step]] if 2 * step < n_seq else [])
        for step in steps
    ]

    mix_t, dx_t, do_own, router_t = expert_rows(
        FROZEN, info, x_train, g_train, router, train_up, train_down, []
    )
    dx_t = swap(dx_t, "exp")
    mix_f, dx_f, unused_do, router_f = expert_rows(
        0, info, x_frozen, g_frozen, router, frozen_up, frozen_down, g_steps[0] + [w_mine]
    )
    dx_f = swap(dx_f, "exp")
    x_steps = [both_ways([x_train, x_train], 1, n_seq)]
    for step in steps[1:]:
        x_steps.append(both_ways(x_steps[-1], step, n_seq))

    lse_rows = jnp.pad(lse.reshape(HEADS, tok), ((0, heads * n_seq - HEADS), (0, 0)))
    lse_rows = jnp.pad(lse_rows.reshape(n_seq, heads, tok), ((0, 0), (0, 8 - heads), (0, 0)))
    send, dmid, dbranch, dgain2 = token_back(
        heads,
        n_seq,
        width,
        info,
        pick,
        dx_t,
        dx_f,
        mid,
        g_own,
        gain2,
        out_weight,
        out_groups,
        attn,
        lse_rows,
        head_rows,
        [g for step in g_steps for g in step] + x_steps[0],
    )
    dos = [send[0]] + [shifted(send[step], step, n_seq) for step in range(1, n_seq)]
    qkv_mine, *mix = project_back(info, w_mine, n1_list, [dmid], [mix_t, mix_f])
    mix = swap(jnp.stack(mix, axis=1), "exp")
    gated_steps = [gated(info, router, x_steps[0], g_steps[0], sum_steps[0], [qkv_mine])]
    output, misc = token_mix(
        info, pick, mix, mid, x_own, attn, dbranch, router_t, router_f, dgain2, branch_squares
    )

    dqkv, part = attend_back(heads, info, qkv_mine, misc, n1_list, dos, gated_steps[0])

    parts = swap(part.reshape(n_exp, D // n_exp, part.shape[1]), "exp")
    dqkv_own = [dqkv[0]] + [shifted(dqkv[step], -step, n_seq) for step in range(1, n_seq)]

    for i in range(1, len(x_steps)):
        gated_steps.append(gated(info, router, x_steps[i], g_steps[i], sum_steps[i], [dqkv[0]]))
    xs = [x_train] + [x for step in x_steps for x in step]
    gs = [do_own] + [g for step in gated_steps for g in step]
    tiles = train_up.shape[2] // GRAD_TILE
    grad_parts = [(expert, (0, tiles)) for expert in range(local - 1)]
    grad_parts += [(local - 1, (first, tiles // 2)) for first in (0, tiles // 2)]
    totals = None

    def more_grads(wait, totals, through=()):
        expert, span = grad_parts.pop(0)
        return expert_grads_part(
            expert, span, info, xs, gs, train_up, train_down, totals, wait, through
        )

    totals, done = more_grads([dqkv[0]], totals)
    piece = sum_parts(info, parts, done)

    found = [shifted(piece, step, n_seq) for step in range(1, n_seq)]
    if len(grad_parts) > 1:
        totals, done = more_grads(done, totals)
    found, again = join_blocks(info, [piece] + found, done)
    here = [lax.ppermute(found, "exp", [(i, i ^ m) for i in range(n_exp)]) for m in range(2, n_exp, 2)]
    input_grad = input_grad_rows(heads, info, x_own, gain1, dmid, w_parts, dqkv_own, done)
    while grad_parts:
        totals, (done, again) = more_grads([input_grad], totals, [again])
    here = jnp.stack([again] + here)
    there = lax.ppermute(here, "exp", [(i, i ^ 1) for i in range(n_exp)])
    up_total, down_total = totals
    qkv_total, out_total, tail, dgain1 = layout(
        heads, n_seq, info, here, there, qkv_weight, gain1, [input_grad]
    )
    stat_sums = tail[0, EXPERTS + 1 : EXPERTS + 5]
    stat_roots = jnp.sqrt(stat_sums[:3] / (stat_sums[3] * D))
    return (
        output[None],
        input_grad[None],
        dgain1[:, 0] / norm1_gain,
        qkv_total,
        out_total,
        tail[:, EXPERTS],
        tail[:, :EXPERTS],
        up_total,
        down_total,
        stat_roots,
    )


def solution(mesh):
    return jax.shard_map(
        body,
        mesh=mesh,
        in_specs=(
            P("exp", "seq", None),
            P("exp", None),
            P("exp", "seq", None),
            P(),
            P(),
            P(),
            P(),
            P(),
            P("exp", None, None),
            P("exp", None, None),
            P("exp", None, None),
            P("exp", None, None),
            P("exp", "seq", None),
        ),
        out_specs=(
            P("exp", "seq", None),
            P("exp", "seq", None),
            P(),
            P(),
            P(),
            P(),
            P(),
            P("exp", None, None),
            P("exp", None, None),
            P(),
        ),
        check_vma=False,
    )
```

```python
import jax
import jax.numpy as jnp
from jax import lax
from jax.experimental import pallas as pl
from jax.experimental.pallas import tpu as pltpu
from jax.sharding import PartitionSpec as P

D = 768
HEADS = 12
HEAD = 64
EXPERTS = 32
FROZEN = 16
CAP = 48

EPS = 1e-06
MASKED = -1e30
BF = jnp.bfloat16
F32 = jnp.float32
TANH_A = 0.7978845608028654
TANH_B = 0.044715
GRAD_ROWS = 1536
GRAD_TILE = 768
MISC = 896
GAIN1_AT = 64
VMEM_BYTES = 56 * 1024 * 1024


def mm(a, b):
    return jnp.dot(a, b, preferred_element_type=F32)


def mm_nt(a, b):
    return lax.dot_general(a, b, (((1,), (1,)), ((), ())), preferred_element_type=F32)


def ein(form, a, b):
    return jnp.einsum(form, a, b, preferred_element_type=F32)


def mm_tn(a, b):
    return lax.dot_general(a, b, (((0,), (0,)), ((), ())), preferred_element_type=F32)


def params():
    return pltpu.CompilerParams(vmem_limit_bytes=VMEM_BYTES)


def cost(micros):
    return pl.CostEstimate(flops=int(micros * 1.1e9), bytes_accessed=0, transcendentals=0)


def whole(shape):
    return pl.BlockSpec(shape, lambda *unused: (0,) * len(shape))


def called(
    kernel,
    name,
    outs,
    info,
    operands,
    in_specs=None,
    scratch=(),
    micros=5,
    grid=(1,),
    out_specs=None,
    aliases=None,
    deps=(),
    through=(),
):
    specs = [None] * len(operands) if in_specs is None else in_specs
    specs = [whole(a.shape) if b is None else b for a, b in zip(operands, specs)]
    results = [whole(shape) for shape, unused in outs] if out_specs is None else list(out_specs)
    shapes = [jax.ShapeDtypeStruct(shape, kind) for shape, kind in outs]
    shapes += [jax.ShapeDtypeStruct(a.shape, a.dtype) for a in through]
    held = pl.BlockSpec(memory_space=pl.ANY)
    aliases = dict(aliases or {})
    for i in range(len(through)):
        aliases[1 + len(operands) + i] = len(outs) + i
    extra = len(through) + len(deps)

    def inner(info_ref, *refs):
        ins, rest = refs[: len(operands)], refs[len(operands) + extra :]
        kernel(info_ref, *ins, *rest[: len(outs)], *rest[len(outs) + len(through) :])

    call = pl.pallas_call(
        inner,
        out_shape=shapes,
        grid_spec=pltpu.PrefetchScalarGridSpec(
            num_scalar_prefetch=1,
            grid=grid,
            in_specs=specs + [held] * extra,
            out_specs=results + [held] * len(through),
            scratch_shapes=list(scratch),
        ),
        input_output_aliases=aliases,
        compiler_params=params(),
        cost_estimate=cost(micros),
        name=name,
    )
    return list(call(info, *operands, *through, *deps))


def released(info, arrays, deps):
    def kernel(info_ref, out_ref):
        out_ref[...] = jnp.zeros_like(out_ref)

    return called(kernel, "released", [((8, 128), F32)], info, [], micros=1, deps=deps, through=arrays)[1:]


INFO = 2


def doc_start(info_ref, position):
    bound = 0
    start = jnp.zeros_like(position)
    for i in range(INFO, info_ref.shape[0]):
        bound = bound + info_ref[i]
        start = jnp.where(position >= bound, bound, start)
    return start


def doc_end(info_ref):
    bound = 0
    for i in range(INFO, info_ref.shape[0]):
        bound = bound + info_ref[i]
    return bound


def need_mask(info_ref, key_start, last_query):
    return doc_start(info_ref, jnp.full((1, 128), last_query, jnp.int32))[0, 0] > key_start


def route_kernel(local, info_ref, routes_ref, g_ref, pick_ref, train_ref, frozen_ref):
    tok = g_ref.shape[0]
    half = pick_ref.shape[0] // 2
    first, second = routes_ref[0:1, :], routes_ref[1:2, :]
    row = lax.broadcasted_iota(jnp.int32, (EXPERTS, tok), 0)
    expert = jnp.where(row < FROZEN, row + FROZEN, row - FROZEN)
    position = info_ref[0] * tok + lax.broadcasted_iota(jnp.int32, (EXPERTS, tok), 1)
    live = ((expert == first) | (expert == second)) & (position < doc_end(info_ref))
    earlier = lax.broadcasted_iota(jnp.int32, (tok, tok), 0) < lax.broadcasted_iota(
        jnp.int32, (tok, tok), 1
    )
    place = mm(jnp.where(live, 1.0, 0.0).astype(BF), jnp.where(earlier, 1.0, 0.0).astype(BF))
    place = jnp.where(live, place, -1.0)
    slot = lax.broadcasted_iota(jnp.int32, (CAP, tok), 0).astype(F32)
    sums = jnp.broadcast_to((first + second).astype(F32), (16, tok)).astype(BF)
    sum_row = lax.broadcasted_iota(jnp.int32, (16, CAP), 0)
    for part, out_ref in ((0, train_ref), (1, frozen_ref)):
        for d in range(FROZEN // local):
            found = jnp.zeros((16, CAP), F32)
            for i in range(local):
                e = part * FROZEN + d * local + i
                taken = jnp.where(place[e : e + 1, :] == slot, 1.0, 0.0).astype(BF)
                pick_ref[e * CAP : (e + 1) * CAP, :] = taken
                found = jnp.where(sum_row == i, mm_nt(sums, taken), found)
            out_ref[d, local * CAP :, :] = jnp.zeros((16, D), BF)
            out_ref[d, local * CAP :, 0:CAP] = found.astype(BF)
        rows = mm(pick_ref[part * half : (part + 1) * half, :], g_ref[...]).astype(BF)
        for d in range(FROZEN // local):
            out_ref[d, : local * CAP, :] = rows[d * local * CAP : (d + 1) * local * CAP, :]


def route(info, local, routes, g):
    tok = g.shape[0]
    sent = (FROZEN // local, local * CAP + 16, D)

    def kernel(*refs):
        route_kernel(local, *refs)

    return called(
        kernel,
        "route",
        [((EXPERTS * CAP, tok), BF), (sent, BF), (sent, BF)],
        info,
        [routes, g],
        [None, None],
        micros=6,
    )


def slot_sums(tile, local_id):
    parts = []
    for i in range(tile.shape[0]):
        turned = tile[i].astype(F32).T
        lane = lax.broadcasted_iota(jnp.int32, turned.shape, 1)
        column = jnp.sum(jnp.where(lane == local_id, turned, 0.0), axis=1, keepdims=True)
        parts.append(column[:CAP, :])
    return jnp.concatenate(parts, axis=0)


def gelu_parts(h):
    h2 = h * h
    t = jnp.tanh(h * (TANH_A + (TANH_A * TANH_B) * h2))
    half = 0.5 * t + 0.5
    act = h * half
    slope = half + act * (1.0 - half) * (2.0 * TANH_A + (6.0 * TANH_A * TANH_B) * h2)
    return act, slope


def attend_kernel(step, last, info_ref, x_ref, gain_ref, w_q_ref, w_k_ref, w_v_ref, *refs):
    first = step == 0
    refs = list(refs)
    if first:
        n1_ref, q_ref = refs[:2]
        refs = refs[2:]
    else:
        q_ref, m_in, l_in, acc_in, n1_ref = refs[:5]
        refs = refs[5:]
    if last:
        attn_ref = refs.pop(0)
        l_ref = refs.pop(0)
        m_ref, acc_ref, k_all, v_all = refs
    else:
        m_ref, l_ref, acc_ref, k_all, v_all = refs
    block = info_ref[0] - step
    rows = x_ref.shape[0]
    pairs = k_all.shape[0]

    x = x_ref[...].astype(F32)
    n1 = x * lax.rsqrt(jnp.mean(x * x, axis=1, keepdims=True) + EPS) * gain_ref[...]
    n1_ref[...] = n1.astype(BF)

    def project():
        n1 = n1_ref[...]
        for i in range(pairs // 2):
            cols = slice(i * 4 * HEAD, (i + 1) * 4 * HEAD)
            k = mm(n1, w_k_ref[:, cols]).astype(BF)
            v = mm(n1, w_v_ref[:, cols]).T.astype(BF)
            for j in range(2):
                k_all[2 * i + j] = k[:, j * 2 * HEAD : (j + 1) * 2 * HEAD]
                v_all[2 * i + j] = v[j * 2 * HEAD : (j + 1) * 2 * HEAD, :]
            if first:
                q = mm(n1, w_q_ref[:, cols]).astype(BF) * jnp.asarray(HEAD**-0.5, BF)
                for j in range(2):
                    q_ref[2 * i + j] = q[:, j * 2 * HEAD : (j + 1) * 2 * HEAD]

    def attend(masked):
        key_pos = block * rows + lax.broadcasted_iota(jnp.int32, (rows, rows), 0)
        query_pos = info_ref[0] * rows + lax.broadcasted_iota(jnp.int32, (1, rows), 1)
        start = doc_start(info_ref, query_pos)

        def pair(p, carry):
            q = q_ref[p]
            k = k_all[p]
            lane = lax.broadcasted_iota(jnp.int32, q.shape, 1)
            zero = jnp.zeros_like(q)
            found = [
                mm_nt(k, jnp.where(lane < HEAD, q, zero)),
                mm_nt(k, jnp.where(lane < HEAD, zero, q)),
            ]
            for half in range(2):
                scores = found[half]
                if masked:
                    allowed = key_pos >= start
                    if first:
                        allowed = allowed & (key_pos <= query_pos)
                    scores = jnp.where(allowed, scores, MASKED)
                top = jnp.max(scores, axis=0, keepdims=True)
                if not first:
                    old = m_in[p, half : half + 1, :]
                    top = jnp.maximum(top, old)
                probs = jnp.exp(scores - top)
                total = jnp.sum(probs, axis=0, keepdims=True)
                value = mm(v_all[p, half * HEAD : (half + 1) * HEAD, :], probs.astype(BF))
                part = pl.ds(pl.multiple_of(p * 2 * HEAD + half * HEAD, HEAD), HEAD)
                if not first:
                    decay = jnp.exp(old - top)
                    total = total + l_in[p, half : half + 1, :] * decay
                    value = value + acc_in[part, :] * decay
                m_ref[p, half : half + 1, :] = top
                l_ref[p, half : half + 1, :] = total
                acc_ref[part, :] = value
            return carry

        lax.fori_loop(0, pairs, pair, 0)

    if first:
        project()
        attend(True)
    else:
        masked = need_mask(info_ref, block * rows, info_ref[0] * rows + rows - 1)

        @pl.when(block >= 0)
        def _():
            project()

        @pl.when((block >= 0) & masked)
        def _():
            attend(True)

        @pl.when((block >= 0) & jnp.logical_not(masked))
        def _():
            attend(False)

        @pl.when(block < 0)
        def _():
            m_ref[...] = m_in[...]
            l_ref[...] = l_in[...]
            acc_ref[...] = acc_in[...]

    if last:
        for p in range(pairs):
            for half in range(2):
                part = slice((2 * p + half) * HEAD, (2 * p + half + 1) * HEAD)
                total = l_ref[p, half : half + 1, :]
                acc_ref[part, :] = acc_ref[part, :] / total
                l_ref[p, half : half + 1, :] = m_ref[p, half : half + 1, :] + jnp.log(total)
            part = slice(p * 2 * HEAD, (p + 1) * 2 * HEAD)
            attn_ref[:, part] = acc_ref[part, :].T.astype(BF)


def attend_step(step, last, info, x, gain, w, state, deps=(), through=()):
    tok = x.shape[0]
    pairs = HEADS // 2
    stat, acc = ((pairs, 2, tok), F32), ((D, tok), F32)
    row, by_pair = ((tok, D), BF), ((pairs, tok, 2 * HEAD), BF)
    outs = [row] + ([by_pair] if step == 0 else []) + ([row, stat] if last else [stat, stat, acc])
    scratch = [pltpu.VMEM(*by_pair), pltpu.VMEM((pairs, 2 * HEAD, tok), BF)]
    if last:
        scratch = [pltpu.VMEM(*stat), pltpu.VMEM(*acc)] + scratch

    def kernel(*refs):
        attend_kernel(step, last, *refs)

    square = (D, D)
    return called(
        kernel,
        "attend_step",
        outs,
        info,
        [x, gain, w, w, w, *state],
        [
            None,
            None,
            pl.BlockSpec(square, lambda i, r: (0, 0)),
            pl.BlockSpec(square, lambda i, r: (0, 1)),
            pl.BlockSpec(square, lambda i, r: (0, 2)),
        ]
        + [None] * len(state),
        scratch,
        micros=13,
        deps=deps,
        through=through,
    )


def attend_back_kernel(blocks, heads, info_ref, qkv_ref, misc_ref, *refs):
    n1_refs, do_refs, out_refs = [refs[i * blocks : (i + 1) * blocks] for i in range(3)]
    part_ref, dq_ref, dk_ref, dv_ref, k_mine, v_mine, k_t, do_all, lse_all, delta_all, out_all = refs[
        3 * blocks :
    ]
    rows = qkv_ref.shape[0] // blocks
    tiles, deep, width = do_refs[0].shape
    lane = lax.broadcasted_iota(jnp.int32, (rows, 2 * HEAD), 1)
    dq_ref[...] = jnp.zeros_like(dq_ref)

    def turn(b):
        return lax.rem(info_ref[0] - b + blocks, blocks)

    for b in range(blocks):
        do_all[b] = do_refs[b][:, :width, :].reshape(rows, width)
        stats = [do_refs[b][t, width:, :].astype(F32) for t in range(tiles)]
        stats = jnp.concatenate(stats, axis=1)
        delta_all[b] = stats[:heads] + stats[heads : 2 * heads]
        lse_all[b] = stats[2 * heads : 3 * heads] + stats[3 * heads : 4 * heads]

    def key_step(kb, carry):
        kt = turn(kb)
        key_rows = pl.ds(pl.multiple_of(kt * rows, rows), rows)
        for h in range(heads):
            first = (h // 2) * 2 * HEAD
            k = qkv_ref[key_rows, width + first : width + first + 2 * HEAD]
            v = qkv_ref[key_rows, 2 * width + first : 2 * width + first + 2 * HEAD]
            mine = (lane < HEAD) if h % 2 == 0 else (lane >= HEAD)
            zero = jnp.zeros_like(k)
            k_mine[h] = jnp.where(mine, k, zero)
            v_mine[h] = jnp.where(mine, v, zero)
            k_t[h] = k.T[(h % 2) * HEAD : (h % 2 + 1) * HEAD, :]
        dk_ref[...] = jnp.zeros_like(dk_ref)
        dv_ref[...] = jnp.zeros_like(dv_ref)

        def pair(qb, diagonal, masked):
            qt = turn(qb)
            query_rows = pl.ds(pl.multiple_of(qt * rows, rows), rows)
            if masked:
                key_pos = kb * rows + lax.broadcasted_iota(jnp.int32, (rows, rows), 0)
                query_pos = qb * rows + lax.broadcasted_iota(jnp.int32, (1, rows), 1)
                allowed = key_pos >= doc_start(info_ref, query_pos)
                if diagonal:
                    allowed = allowed & (key_pos <= query_pos)

            def of_head(h):
                cols = slice((h // 2) * 2 * HEAD, (h // 2 + 1) * 2 * HEAD)
                return qkv_ref[query_rows, cols], do_all[qt, :, cols]

            def products(h):
                q, do = of_head(h)
                return mm_nt(k_mine[h], q), mm_nt(v_mine[h], do)

            later = products(0)
            for h in range(heads):
                scores, dprobs = later
                if h + 1 < heads:
                    later = products(h + 1)
                q, do = of_head(h)
                probs = jnp.exp(scores - lse_all[qt, h : h + 1, :])
                if masked:
                    probs = jnp.where(allowed, probs, 0.0)
                dscores = (probs * (dprobs - delta_all[qt, h : h + 1, :])).astype(BF)
                dv_ref[h] += mm(probs.astype(BF), do)
                dk_ref[h] += mm(dscores, q)
                dq_ref[qt, h] += mm(k_t[h], dscores)

        pair(kb, True, True)

        def query_step(qb, carry):
            masked = need_mask(info_ref, kb * rows, qb * rows + rows - 1)

            @pl.when(masked)
            def _():
                pair(qb, False, True)

            @pl.when(jnp.logical_not(masked))
            def _():
                pair(qb, False, False)

            return carry

        lax.fori_loop(kb + 1, blocks, query_step, 0)
        for h in range(heads):
            part = slice((h % 2) * HEAD, (h % 2 + 1) * HEAD)
            for i, grad_ref in ((1, dk_ref), (2, dv_ref)):
                at = (i * heads + h) * HEAD
                out_all[kt, at : at + HEAD, :] = grad_ref[h].T[part, :].astype(BF)
        return carry

    lax.fori_loop(0, blocks, key_step, 0)
    total = 0.0
    for b in range(blocks):
        for h in range(heads):
            out_all[b, h * HEAD : (h + 1) * HEAD, :] = (dq_ref[b, h] * HEAD**-0.5).astype(BF)
        grads = out_all[b]
        out_refs[b][...] = grads
        total = total + mm(grads, n1_refs[b][...])
    part_ref[:, :MISC] = misc_ref[...]
    part_ref[:, MISC:] = total.T.astype(BF)


def attend_back(heads, info, qkv, misc, n1, dos, deps):
    rows = qkv.shape[0]
    blocks = len(dos)
    tiles, deep, width = dos[0].shape
    tok = rows // blocks
    cols = 3 * heads * HEAD

    def kernel(*refs):
        attend_back_kernel(blocks, heads, *refs)

    *grads, part = called(
        kernel,
        "attend_back",
        [((cols, tok), BF)] * blocks + [((D, MISC + cols), BF)],
        info,
        [qkv, misc, *n1, *dos],
        scratch=[
            pltpu.VMEM((blocks, heads, HEAD, tok), F32),
            pltpu.VMEM((heads, tok, 2 * HEAD), F32),
            pltpu.VMEM((heads, tok, 2 * HEAD), F32),
            pltpu.VMEM((heads, tok, 2 * HEAD), BF),
            pltpu.VMEM((heads, tok, 2 * HEAD), BF),
            pltpu.VMEM((heads, HEAD, tok), BF),
            pltpu.VMEM((blocks, tok, width), BF),
            pltpu.VMEM((blocks, heads, tok), F32),
            pltpu.VMEM((blocks, heads, tok), F32),
            pltpu.VMEM((blocks, cols, tok), BF),
        ],
        micros=32,
        deps=deps,
    )
    return grads, part


def project_back_kernel(blocks, info_ref, w_ref, *refs):
    out_ref = refs[blocks]
    rows = refs[0].shape[0]
    for b in range(blocks):
        out_ref[b * rows : (b + 1) * rows, :] = mm_nt(refs[b][...], w_ref[...]).astype(BF)


def project_back(info, w, n1, deps):
    blocks = len(n1)

    def kernel(*refs):
        project_back_kernel(blocks, *refs)

    shape = (blocks * n1[0].shape[0], w.shape[0])
    return called(kernel, "project_back", [(shape, BF)], info, [w, *n1], micros=7, deps=deps)[0]


def slot_gate(own, sums, x, router):
    lane = lax.broadcasted_iota(jnp.int32, (x.shape[0], router.shape[1]), 1)
    other = sums.astype(jnp.int32) - own
    signs = jnp.where(lane == own, 1.0, 0.0) - jnp.where(lane == other, 1.0, 0.0)
    margin = jnp.sum(mm(x, router) * signs, axis=1, keepdims=True)
    return 1.0 / (1.0 + jnp.exp(-margin)), signs


def expert_kernel(
    first_id, info_ref, x_ref, g_ref, sums_ref, router_ref, up_ref, down_ref, back_ref, drouter_ref, *refs
):
    handed = refs[:-6]
    xs, dos, gate_ref, signs_ref, eacc, dacc = refs[-6:]
    expert = pl.program_id(0)
    step = pl.program_id(1)
    rows = xs.shape[0]
    block = x_ref.shape

    @pl.when(step == 0)
    def _():
        x = x_ref[...].reshape(rows, D)
        xs[...] = x
        own = first_id + info_ref[1] * pl.num_programs(0) + expert
        gate, signs = slot_gate(own, slot_sums(sums_ref, expert), x, router_ref[...])
        gate_ref[...] = gate
        signs_ref[...] = signs
        do = (gate * g_ref[...].reshape(rows, D).astype(F32)).astype(BF)
        dos[...] = do
        if handed:
            handed[0][...] = do.reshape(block)
            for x_out in handed[1:]:
                x_out[:, pl.ds(pl.multiple_of(expert * CAP, 16), CAP), :] = x.reshape(-1, CAP, D)

    if handed:

        @pl.when((step == 0) & (expert == 0))
        def _():
            for x_out in handed[1:]:
                last = x_out.shape[1] - 16
                x_out[:, last:, :] = jnp.zeros((block[0], 16, D), BF)
                x_out[:, last:, 0:128] = sums_ref[...]

    act, slope = gelu_parts(mm(xs[...], up_ref[0]))
    dhid = (mm_nt(dos[...], down_ref[0]) * slope).astype(BF)
    out = mm(act.astype(BF), down_ref[0])
    dx = mm_nt(dhid, up_ref[0])

    @pl.when(step == 0)
    def _():
        eacc[...] = out
        dacc[...] = dx

    @pl.when(step > 0)
    def _():
        eacc[...] += out
        dacc[...] += dx

    @pl.when(step == pl.num_programs(1) - 1)
    def _():
        out = eacc[...]
        gate = gate_ref[...]
        g = g_ref[...].reshape(rows, D).astype(F32)
        back_ref[:, 1] = (gate * out).astype(BF).reshape(block)
        dgate = jnp.sum(g * out, axis=1, keepdims=True)
        dlogits = (gate * (1.0 - gate) * dgate * signs_ref[...]).astype(BF)
        dx = dacc[...] + mm_nt(dlogits, router_ref[...])
        back_ref[:, 0] = dx.astype(BF).reshape(block)
        drouter = mm_tn(dlogits, xs[...])

        @pl.when(expert == 0)
        def _():
            drouter_ref[...] = drouter

        @pl.when(expert > 0)
        def _():
            drouter_ref[...] += drouter


def expert_rows(first_id, info, x, g, router, up, down, handing, deps, through=()):
    sources, experts = x.shape[:2]
    rows = sources * CAP
    hidden = up.shape[2]
    tile = 1536
    row_spec = pl.BlockSpec((sources, 1, CAP, D), lambda e, f, r: (0, e, 0, 0))


    def kernel(*refs):
        expert_kernel(first_id, *refs)

    outs = [((sources, 2) + x.shape[1:], BF), ((router.shape[1], D), F32)]
    out_specs = [
        pl.BlockSpec((sources, 2, 1, CAP, D), lambda e, f, r: (0, 0, e, 0, 0)),
        whole((router.shape[1], D)),
    ]
    if handing:
        outs += [(x.shape, BF), (g.shape, BF), (g.shape, BF)]
        out_specs += [row_spec, whole(g.shape), whole(g.shape)]

    return called(
        kernel,
        "expert_rows",
        outs,
        info,
        [x, g, g, router, up, down],
        [
            row_spec,
            pl.BlockSpec((sources, CAP, D), lambda e, f, r: (0, e, 0)),
            pl.BlockSpec((sources, 16, 128), lambda e, f, r: (0, experts * CAP // 16, 0)),
            None,
            pl.BlockSpec((1, D, tile), lambda e, f, r: (e, 0, f)),
            pl.BlockSpec((1, tile, D), lambda e, f, r: (e, f, 0)),
        ],
        [
            pltpu.VMEM((rows, D), BF),
            pltpu.VMEM((rows, D), BF),
            pltpu.VMEM((rows, 1), F32),
            pltpu.VMEM((rows, 128), F32),
            pltpu.VMEM((rows, D), F32),
            pltpu.VMEM((rows, D), F32),
        ],
        micros=23,
        grid=(experts, hidden // tile),
        out_specs=out_specs,
        deps=deps,
        through=through,
    )


def gated_kernel(count, experts, info_ref, router_ref, *refs):
    x_refs, g_refs, out_refs = [refs[i * count : (i + 1) * count] for i in range(3)]
    for i, again_ref in enumerate(refs[3 * count :]):
        again_ref[...] = x_refs[i][...]
    sources = x_refs[0].shape[0]
    for b in range(count):
        for e in range(experts):
            own = FROZEN + info_ref[1] * experts + e
            part = slice(e * CAP, (e + 1) * CAP)
            x = x_refs[b][:, part, :].reshape(sources * CAP, D)
            sums = slot_sums(x_refs[b][:, experts * CAP :, 0:128], e)
            gate, unused = slot_gate(own, sums, x, router_ref[...])
            g = g_refs[b][:, part, :].reshape(sources * CAP, D).astype(F32)
            out_refs[b][:, e] = (gate * g).astype(BF).reshape(sources, CAP, D)


def gated(info, router, xs, gs, deps=(), again=0):
    count = len(xs)
    sources, rows = xs[0].shape[:2]
    experts = (rows - 16) // CAP

    def kernel(*refs):
        gated_kernel(count, experts, *refs)

    return called(
        kernel,
        "gated",
        [((sources, experts, CAP, D), BF)] * count + [(x.shape, BF) for x in xs[:again]],
        info,
        [router, *xs, *gs],
        micros=1,
        deps=deps,
    )


def expert_grad_kernel(group, add, info_ref, ins, dup_ref, ddown_ref, done_ref, xs, dos):
    up_ref, down_ref = ins[:2]
    x_refs, do_refs = ins[2 : 2 + group], ins[2 + group : 2 + 2 * group]
    rows = xs.shape[0] // group

    @pl.when(pl.program_id(0) == 0)
    def _():
        done_ref[...] = jnp.zeros_like(done_ref)
        for b in range(group):
            part = slice(b * rows, (b + 1) * rows)
            xs[part, :] = x_refs[b][...].reshape(rows, D)
            dos[part, :] = do_refs[b][...].reshape(rows, D)

    act, slope = gelu_parts(mm(xs[...], up_ref[0]))
    dhid = (mm_nt(dos[...], down_ref[0]) * slope).astype(BF)
    ddown = mm_tn(act.astype(BF), dos[...])
    dup = mm_tn(xs[...], dhid)
    if add:
        ddown = ddown + ins[-1][0]
        dup = dup + ins[-2][0]
    ddown_ref[0] = ddown
    dup_ref[0] = dup


def expert_grads(expert, span, first, group, info, xs, dos, up, down, totals, deps, through):
    sources, experts = dos[0].shape[:2]
    rows = group * sources * CAP
    tile = GRAD_TILE
    start, count = span
    add = first > 0
    up_spec = pl.BlockSpec((1, D, tile), lambda f, r: (expert, 0, start + f))
    down_spec = pl.BlockSpec((1, tile, D), lambda f, r: (expert, start + f, 0))
    in_specs = [up_spec, down_spec]
    in_specs += [pl.BlockSpec((sources, CAP, D), lambda f, r: (0, expert, 0))] * group
    in_specs += [pl.BlockSpec((sources, 1, CAP, D), lambda f, r: (0, expert, 0, 0))] * group
    part = slice(first, first + group)
    operands = [up, down, *xs[part], *dos[part]]
    aliases = {}
    if totals is not None:
        aliases = {1 + len(operands): 0, 2 + len(operands): 1}
        in_specs += [up_spec, down_spec] if add else [pl.BlockSpec(memory_space=pl.ANY)] * 2
        operands += list(totals)

    def kernel(info_ref, *refs):
        ins, rest = refs[: len(operands)], refs[len(operands) :]
        expert_grad_kernel(group, add, info_ref, ins, *rest)

    return called(
        kernel,
        "expert_grads",
        [(up.shape, F32), (down.shape, F32), ((8, 128), F32)],
        info,
        operands,
        in_specs,
        [pltpu.VMEM((rows, D), BF), pltpu.VMEM((rows, D), BF)],
        micros=9 * count,
        grid=(count,),
        out_specs=[up_spec, down_spec, whole((8, 128))],
        aliases=aliases,
        deps=deps,
        through=through,
    )


def expert_grads_part(expert, span, info, xs, dos, up, down, totals, deps, through):
    blocks = len(xs)
    group = max(1, min(blocks, GRAD_ROWS // (dos[0].shape[0] * CAP)))
    for first in range(0, blocks, group):
        dup, ddown, done, *through = expert_grads(
            expert, span, first, group, info, xs, dos, up, down, totals, deps, through
        )
        totals = [dup, ddown]
    return totals, [done, *through]


def token_forward_kernel(
    info_ref, attn_ref, x_ref, gain_ref, w_ref, pick_ref, mid_ref, square_ref, train_ref, frozen_ref
):
    tok = x_ref.shape[0]
    half = pick_ref.shape[0] // 2
    branch = mm(attn_ref[...], w_ref[...])
    mid = x_ref[...].astype(F32) + branch
    mid_ref[...] = mid
    r = lax.rsqrt(jnp.mean(mid * mid, axis=1, keepdims=True) + EPS)
    n2 = (mid * r * gain_ref[...]).astype(BF)
    train_ref[...] = mm(pick_ref[:half, :], n2).astype(BF)
    frozen_ref[...] = mm(pick_ref[half:, :], n2).astype(BF)
    position = info_ref[0] * tok + lax.broadcasted_iota(jnp.int32, (tok, D), 0)
    square = jnp.where(position < doc_end(info_ref), branch * branch, 0.0)
    square_ref[...] = jnp.sum(square, axis=0, keepdims=True)


def token_forward(info, attn, x, gain, w, pick):
    tok = x.shape[0]
    half = ((pick.shape[0] // 2, D), BF)
    return called(
        token_forward_kernel,
        "token_forward",
        [((tok, D), F32), ((1, D), F32), half, half],
        info,
        [attn, x, gain, w, pick],
        [None] * 5,
        micros=6,
    )


def token_back_kernel(
    heads,
    groups,
    info_ref,
    pick_ref,
    dx_t_ref,
    dx_f_ref,
    mid_ref,
    g_ref,
    gain_ref,
    w_ref,
    wg_ref,
    attn_ref,
    lse_ref,
    head_ref,
    *refs,
):
    send_refs = refs[:groups]
    dmid_ref, dbranch_ref, dgain_ref = refs[groups:]
    tiles, deep, width = send_refs[0].shape
    tok = mid_ref.shape[0]
    half = pick_ref.shape[0] // 2

    dn2 = mm_tn(pick_ref[:half, :], dx_t_ref[...].reshape(half, D))
    dn2 = dn2 + mm_tn(pick_ref[half:, :], dx_f_ref[...].reshape(half, D))
    mid = mid_ref[...]
    r = lax.rsqrt(jnp.mean(mid * mid, axis=1, keepdims=True) + EPS)
    u = mid * r
    dgain_ref[...] = jnp.sum(dn2 * u, axis=0, keepdims=True)
    scaled = dn2 * gain_ref[...]
    dmid = g_ref[...].astype(F32) + r * (scaled - u * jnp.mean(scaled * u, axis=1, keepdims=True))
    dmid_ref[...] = dmid
    dbranch = dmid.astype(BF)
    dbranch_ref[...] = dbranch

    dattn = mm_nt(dbranch, w_ref[...]).astype(BF).astype(F32)
    prod = dattn * attn_ref[...].astype(F32)
    high = prod.astype(BF)
    low = (prod - high.astype(F32)).astype(BF)
    for turn in range(groups):
        g = lax.rem(info_ref[0] + turn, groups)
        sent = mm_nt(dbranch, wg_ref[g]).astype(BF)
        delta = mm_nt(head_ref[g], high) + mm_nt(head_ref[g], low)
        parts = []
        for stat in (delta[:heads], lse_ref[g][:heads]):
            high_part = stat.astype(BF).astype(F32)
            parts += [high_part, stat - high_part]
        blank = jnp.zeros((16 - 4 * heads, tok), F32)
        stats = jnp.concatenate(parts + [blank], axis=0).astype(BF)
        for t in range(tiles):
            part = slice(t * width, (t + 1) * width)
            send_refs[turn][t, :width, :] = sent[part, :]
            send_refs[turn][t, width:, :] = stats[:, part]


def token_back(
    heads, groups, width, info, pick, dx_t, dx_f, mid, g, gain, w, w_groups, attn, lse, head_rows, deps, through
):
    tok = mid.shape[0]
    tiles = tok // width

    def kernel(*refs):
        token_back_kernel(heads, groups, *refs)

    outs = [((tiles, width + 16, width), BF)] * groups
    operands = [pick, dx_t, dx_f, mid, g, gain, w, w_groups, attn, lse, head_rows]
    half = (dx_f.shape[0], 1) + dx_f.shape[1:]
    found = called(
        kernel,
        "token_back",
        outs + [((tok, D), F32), ((tok, D), BF), ((1, D), F32)],
        info,
        operands,
        [None, pl.BlockSpec(half, lambda i, r: (0, 0, 0, 0, 0))] + [None] * (len(operands) - 2),
        micros=10,
        deps=deps,
        through=through,
    )
    return [found[:groups]] + found[groups:]


def token_mix_kernel(
    info_ref, pick_ref, mix_t_ref, mix_f_ref, mid_ref, x_ref, attn_ref, dbranch_ref, rt_ref, rf_ref, dgain_ref, square_ref, out_ref, misc_ref
):
    tok = mid_ref.shape[0]
    half = pick_ref.shape[0] // 2
    mix = mm_tn(pick_ref[:half, :], mix_t_ref[...].reshape(half, D))
    mix = mix + mm_tn(pick_ref[half:, :], mix_f_ref[...].reshape(half, D))
    out_ref[...] = (mid_ref[...] + mix).astype(BF)
    valid = info_ref[0] * tok + lax.broadcasted_iota(jnp.int32, (tok, D), 0) < doc_end(info_ref)
    x = x_ref[...].astype(F32)
    stats = [
        jnp.sum(jnp.where(valid, x * x, 0.0)),
        jnp.sum(square_ref[...]),
        jnp.sum(jnp.where(valid, mix * mix, 0.0)),
        jnp.clip(doc_end(info_ref) - info_ref[0] * tok, 0, tok).astype(F32),
    ]
    misc_ref[:, :D] = mm_tn(attn_ref[...], dbranch_ref[...]).astype(BF)
    tail = (rt_ref[...] + rf_ref[...]).T
    gains = jnp.broadcast_to(dgain_ref[...], (8, D)).T[:, 0:1]
    row = lax.broadcasted_iota(jnp.int32, tail.shape, 0)
    lane = lax.broadcasted_iota(jnp.int32, tail.shape, 1)
    tail = jnp.where(lane < EXPERTS, tail, 0.0) + jnp.where(lane == EXPERTS, gains, 0.0)
    for i, stat in enumerate(stats):
        tail = tail + jnp.where((lane == EXPERTS + 1 + i) & (row == 0), stat, 0.0)
    misc_ref[:, D : D + 128] = tail.astype(BF)


def token_mix(info, pick, back_t, mix_f, mid, x, attn, dbranch, router_t, router_f, dgain, square):
    tok = mid.shape[0]
    operands = [pick, back_t, mix_f, mid, x, attn, dbranch, router_t, router_f, dgain, square]
    half = (mix_f.shape[0], 1) + mix_f.shape[1:]
    return called(
        token_mix_kernel,
        "token_mix",
        [((tok, D), BF), ((D, MISC), BF)],
        info,
        operands,
        [None, pl.BlockSpec(half, lambda i, r: (0, 1, 0, 0, 0))] + [None] * (len(operands) - 2),
        micros=1,
    )


def input_grad_kernel(heads, blocks, info_ref, x_ref, gain_ref, dmid_ref, w_ref, *refs):
    grad_refs, out_ref = refs[:blocks], refs[blocks]
    wide = heads * HEAD
    dn1 = 0.0
    for turn in range(blocks):
        g = lax.rem(info_ref[0] + turn, blocks)
        for c in range(3):
            rows = pl.ds(pl.multiple_of(c * blocks * wide + g * wide, HEAD), wide)
            part = grad_refs[turn][c * wide : (c + 1) * wide, :]
            dn1 = dn1 + mm_tn(part, w_ref[rows, :])
    x = x_ref[...].astype(F32)
    r = lax.rsqrt(jnp.mean(x * x, axis=1, keepdims=True) + EPS)
    u = x * r
    scaled = dn1 * gain_ref[...]
    dx = r * (scaled - u * jnp.mean(scaled * u, axis=1, keepdims=True))
    out_ref[...] = (dmid_ref[...] + dx).astype(BF)


def input_grad_rows(heads, info, x, gain, dmid, w_t, grads, deps):
    blocks = len(grads)

    def kernel(*refs):
        input_grad_kernel(heads, blocks, *refs)

    operands = [x, gain, dmid, w_t, *grads]
    return called(
        kernel, "input_grad", [(x.shape, BF)], info, operands, micros=8, deps=deps
    )[0]


def sum_kernel(info_ref, a_ref, w_ref, out_ref):
    total = a_ref[0].astype(F32)
    for i in range(1, a_ref.shape[0]):
        total = total + a_ref[i].astype(F32)
    out_ref[...] = total.astype(BF)
    gain = jnp.sum(total[:, MISC:] * w_ref[...].astype(F32), axis=1, keepdims=True)
    lane = lax.broadcasted_iota(jnp.int32, (total.shape[0], 128), 1)
    out_ref[:, D:MISC] = jnp.where(lane == GAIN1_AT, gain, total[:, D:MISC]).astype(BF)


def sum_parts(info, a, w, deps):
    return called(sum_kernel, "sum_parts", [(a.shape[1:], BF)], info, [a, w], micros=3, deps=deps)[0]


def join_kernel(info_ref, *refs):
    found, out_ref, again_ref = refs[:-2], refs[-2], refs[-1]
    total = found[0][:, :MISC].astype(F32)
    for ref in found[1:]:
        total = total + ref[:, :MISC].astype(F32)
    out_ref[:, :MISC] = total.astype(BF)
    cols = found[0].shape[1] - MISC
    for i, ref in enumerate(found):
        out_ref[:, MISC + i * cols : MISC + (i + 1) * cols] = ref[:, MISC:]
    again_ref[...] = out_ref[...]


def join_blocks(info, found, deps):
    rows, cols = found[0].shape
    shape = (rows, MISC + len(found) * (cols - MISC))
    return called(
        join_kernel, "join_blocks", [(shape, BF)] * 2, info, list(found), micros=3, deps=deps
    )


def layout_kernel(heads, info_ref, here_ref, there_ref, gain_ref, qkv_ref, out_ref, router_ref, gain1_ref, gain2_ref, stat_ref, tails):
    step = pl.program_id(0)
    rows = here_ref.shape[1]
    wide = heads * HEAD
    groups = (here_ref.shape[2] - MISC) // (3 * wide)

    def lay(part, piece):
        out_ref[part, :] = piece[:, :D].astype(F32)
        tail = piece[:, D:MISC].astype(F32)
        for turn in range(groups):
            g = lax.rem(info_ref[0] - turn + groups, groups)
            for c in range(3):
                at = MISC + (3 * turn + c) * wide
                grad = piece[:, at : at + wide].astype(F32)
                for g_now in range(groups):
                    cols = min(wide, D - g_now * wide)
                    to = c * D + g_now * wide
                    if cols > 0:

                        @pl.when(g == g_now)
                        def _():
                            qkv_ref[part, to : to + cols] = grad[:, :cols]

        return tail

    mine = lax.rem(info_ref[1], 2)
    for core in range(2):
        part = slice(core * rows, (core + 1) * rows)
        at = pl.ds(pl.multiple_of((2 * step + core) * rows, rows), rows)

        @pl.when(mine == core)
        def _():
            tails[at, :] = lay(part, here_ref[0])

        @pl.when(mine != core)
        def _():
            tails[at, :] = lay(part, there_ref[0])

    @pl.when(step == pl.num_programs(0) - 1)
    def _():
        turned = tails[...].T
        gain1_ref[...] = turned[GAIN1_AT] / gain_ref[0]
        gain2_ref[...] = turned[EXPERTS]
        router_ref[...] = turned[:EXPERTS]
        stats = tails[0:8, :]
        lane = lax.broadcasted_iota(jnp.int32, stats.shape, 1)
        count = jnp.sum(jnp.where(lane == EXPERTS + 4, stats, 0.0), axis=1, keepdims=True)
        used = (lane > EXPERTS) & (lane < EXPERTS + 4)
        stat_ref[...] = jnp.sqrt(jnp.where(used, stats, 0.0) / (jnp.maximum(count, 1.0) * D))


def layout(heads, info, here, there, gain):
    chips, rows, width = here.shape

    def kernel(*refs):
        layout_kernel(heads, *refs)

    piece_spec = pl.BlockSpec((1, rows, width), lambda e, r: (e ^ (r[1] // 2), 0, 0))

    def row_spec(cols):
        return pl.BlockSpec((2 * rows, cols), lambda e, r: (e, 0))

    return called(
        kernel,
        "layout",
        [((D, 3 * D), F32), ((D, D), F32), ((EXPERTS, D), F32), ((D,), F32), ((D,), F32), ((8, 128), F32)],
        info,
        [here, there, gain],
        [piece_spec, piece_spec, None],
        [pltpu.VMEM((D, 128), F32)],
        micros=12,
        grid=(chips,),
        out_specs=[row_spec(3 * D), row_spec(D), whole((EXPERTS, D)), whole((D,)), whole((D,)), whole((8, 128))],
    )


def shifted(x, by, count):
    return lax.ppermute(x, "seq", [(i, (i + by) % count) for i in range(count)])


def swap(x, axis):
    return lax.all_to_all(x, axis, split_axis=0, concat_axis=0, tiled=True)


def both_ways(found, step, count):
    found = [shifted(found[0], 1, count), shifted(found[1], -1, count)] if 2 * step < count else [
        shifted(found[0], 1, count)
    ]
    return found


def body(
    layer_input,
    lengths,
    routes,
    norm1_gain,
    qkv_weight,
    out_weight,
    norm2_gain,
    router_weight,
    frozen_up,
    frozen_down,
    train_up,
    train_down,
    cotangent,
):
    tok = layer_input.shape[1]
    n_seq = lax.axis_size("seq")
    n_exp = lax.axis_size("exp")
    rank = lax.axis_index("seq")
    column = lax.axis_index("exp")
    heads = -(-HEADS // n_seq)
    wide = heads * HEAD
    width = (heads + heads % 2) * HEAD
    local = FROZEN // n_exp
    x_own = layer_input[0]
    g_own = cotangent[0]
    gain1 = norm1_gain[None, :]
    gain2 = norm2_gain[None, :]
    info = jnp.concatenate([jnp.stack([rank, column]).astype(jnp.int32), lengths[0]])

    w_t = qkv_weight.T
    w_parts = jnp.pad(w_t.reshape(3, D, D), ((0, 0), (0, n_seq * wide - D), (0, 0)))
    w_mine = lax.dynamic_slice_in_dim(w_parts, rank * wide, wide, axis=1)
    w_chunk = lax.dynamic_slice_in_dim(w_mine, column * (D // n_exp), D // n_exp, axis=2)
    w_chunk = w_chunk.reshape(3 * wide, D // n_exp).T
    w_mine = w_mine * jnp.asarray([HEAD**-0.5, 1.0, 1.0], BF)[:, None, None]
    w_mine = jnp.pad(w_mine, ((0, 0), (0, width - wide), (0, 0))).reshape(3 * width, D)
    w_parts = w_parts.reshape(3 * n_seq * wide, D)
    out_groups = jnp.pad(out_weight, ((0, n_seq * wide - D), (0, 0)))
    out_groups = jnp.pad(out_groups.reshape(n_seq, wide, D), ((0, 0), (0, width - wide), (0, 0)))
    feature_head = jnp.arange(D, dtype=jnp.int32) // HEAD
    row_id = jnp.arange(8, dtype=jnp.int32)[None, :] + heads * jnp.arange(n_seq, dtype=jnp.int32)[:, None]
    row_id = jnp.where(jnp.arange(8)[None, :] < heads, row_id, -1)
    head_rows = (row_id[:, :, None] == feature_head[None, None, :]).astype(BF)
    router = jnp.pad(router_weight, ((0, 0), (0, 128 - EXPERTS)))

    pick, g_train, g_frozen = route(info, local, routes[0].T, g_own)
    g_train = swap(g_train, "exp")
    g_frozen = swap(g_frozen, "exp")

    x_now = x_own
    n1_list = []
    state = ()
    g_rows = g_train[:, : local * CAP]
    for step in range(n_seq):
        last = step == n_seq - 1
        if last:
            [g_rows] = released(info, [g_rows], [x_now])
        x_next = None if last else shifted(x_now, 1, n_seq)
        found = attend_step(
            step,
            last,
            info,
            x_now,
            gain1,
            qkv_weight,
            state,
            deps=[g_frozen] if last else [],
        )
        n1_list.append(found[0])
        state = tuple(found[1:]) if step == 0 else (state[0],) + tuple(found[1:])
        x_now = x_next
    unused_q, attn, lse = state

    mid, branch_squares, rows_train, rows_frozen = token_forward(
        info, attn, x_own, gain2, out_weight, pick
    )
    x_train = swap(rows_train.reshape(n_exp, local, CAP, D), "exp")
    x_frozen = swap(rows_frozen.reshape(n_exp, local, CAP, D), "exp")

    steps = range(1, n_seq // 2 + 1)
    g_steps = [both_ways([g_rows, g_rows], 1, n_seq)]
    for step in steps[1:]:
        g_steps.append(both_ways(g_steps[-1], step, n_seq))
    back_t, router_t, do_own, x_up, x_down = expert_rows(
        FROZEN, info, x_train, g_train, router, train_up, train_down, True, g_steps[0]
    )
    back_t = swap(back_t, "exp")
    x_own_rows = x_up
    back_f, router_f = expert_rows(
        0,
        info,
        x_frozen,
        g_frozen,
        router,
        frozen_up,
        frozen_down,
        False,
        [w_mine, w_chunk] + [g for step in g_steps for g in step],
    )
    dx_f = swap(back_f[:, 0], "exp")
    x_steps = [both_ways([x_up, x_down], 1, n_seq)]
    qkv_mine = project_back(info, w_mine, n1_list, [back_f])

    lse_rows = jnp.pad(lse.reshape(HEADS, tok), ((0, heads * n_seq - HEADS), (0, 0)))
    lse_rows = jnp.pad(lse_rows.reshape(n_seq, heads, tok), ((0, 0), (0, 8 - heads), (0, 0)))
    send, dmid, dbranch, dgain2, back_f = token_back(
        heads,
        n_seq,
        width,
        info,
        pick,
        back_t,
        dx_f,
        mid,
        g_own,
        gain2,
        out_weight,
        out_groups,
        attn,
        lse_rows,
        head_rows,
        [qkv_mine, *x_steps[0]],
        [back_f],
    )
    dos = [send[0]] + [shifted(send[step], step, n_seq) for step in range(1, n_seq)]
    mix_f = swap(back_f[:, 1], "exp")
    sends = 0 if n_seq < 4 else 1 if n_seq == 4 else 2
    found = gated(info, router, x_steps[0], g_steps[0], [send[0]], sends)
    gated_steps, x_go = [found[: len(x_steps[0])]], found[len(x_steps[0]) :]
    output, misc = token_mix(
        info, pick, back_t, mix_f, mid, x_own, attn, dbranch, router_t, router_f, dgain2, branch_squares
    )

    if len(steps) > 1:
        x_go = released(info, x_go, [misc, *dos])
    for step in steps[1:]:
        x_steps.append(both_ways(x_go if step == 2 else x_steps[-1], step, n_seq))
    dqkv, part = attend_back(heads, info, qkv_mine, misc, n1_list, dos, gated_steps[0])

    parts = swap(part.reshape(n_exp, D // n_exp, part.shape[1]), "exp")
    dqkv_own = [dqkv[0]] + [shifted(dqkv[step], -step, n_seq) for step in range(1, n_seq)]

    for i in range(1, len(x_steps)):
        gated_steps.append(gated(info, router, x_steps[i], g_steps[i], [dqkv[0]]))
    xs = [x_own_rows] + [x for step in x_steps for x in step]
    gs = [do_own] + [g for step in gated_steps for g in step]
    tiles = train_up.shape[2] // GRAD_TILE
    grad_parts = [(expert, (0, tiles)) for expert in range(local - 1)]
    grad_parts += [(local - 1, (first, tiles // 2)) for first in (0, tiles // 2)]
    totals = None

    def more_grads(wait, totals, through=()):
        expert, span = grad_parts.pop(0)
        return expert_grads_part(
            expert, span, info, xs, gs, train_up, train_down, totals, wait, through
        )

    totals, done = more_grads([dqkv[0]], totals)
    piece = sum_parts(info, parts, w_chunk, done)

    found = [shifted(piece, step, n_seq) for step in range(1, n_seq)]
    if len(grad_parts) > 1:
        totals, done = more_grads([piece], totals)
    found, again = join_blocks(info, [piece] + found, done)
    here = [lax.ppermute(found, "exp", [(i, i ^ m) for i in range(n_exp)]) for m in range(2, n_exp, 2)]
    input_grad = input_grad_rows(heads, info, x_own, gain1, dmid, w_parts, dqkv_own, done)
    while grad_parts:
        totals, (done, again) = more_grads([input_grad], totals, [again])
    here = jnp.stack([again] + here)
    there = lax.ppermute(here, "exp", [(i, i ^ 1) for i in range(n_exp)])
    up_total, down_total = totals
    qkv_total, out_total, router_total, dgain1, dgain2, stats = layout(
        heads, info, here, there, gain1
    )
    stat_roots = stats[0, EXPERTS + 1 : EXPERTS + 4]
    return (
        output[None],
        input_grad[None],
        dgain1,
        qkv_total,
        out_total,
        dgain2,
        router_total.T,
        up_total,
        down_total,
        stat_roots,
    )


def solution(mesh):
    return jax.shard_map(
        body,
        mesh=mesh,
        in_specs=(
            P("exp", "seq", None),
            P("exp", None),
            P("exp", "seq", None),
            P(),
            P(),
            P(),
            P(),
            P(),
            P("exp", None, None),
            P("exp", None, None),
            P("exp", None, None),
            P("exp", None, None),
            P("exp", "seq", None),
        ),
        out_specs=(
            P("exp", "seq", None),
            P("exp", "seq", None),
            P(),
            P(),
            P(),
            P(),
            P(),
            P("exp", None, None),
            P("exp", None, None),
            P(),
        ),
        check_vma=False,
    )
```

```python
import jax
import jax.numpy as jnp
from jax import lax
from jax.experimental import pallas as pl
from jax.experimental.pallas import tpu as pltpu
from jax.sharding import PartitionSpec as P

D = 768
HEADS = 12
HEAD = 64
EXPERTS = 32
FROZEN = 16
CAP = 48

EPS = 1e-06
MASKED = -1e30
BF = jnp.bfloat16
F32 = jnp.float32
TANH_A = 0.7978845608028654
TANH_B = 0.044715
GRAD_ROWS = 1536
GRAD_TILE = 768
MISC = 896
GAIN1_AT = 64
VMEM_BYTES = 56 * 1024 * 1024


def mm(a, b):
    return jnp.dot(a, b, preferred_element_type=F32)


def mm_nt(a, b):
    return lax.dot_general(a, b, (((1,), (1,)), ((), ())), preferred_element_type=F32)


def ein(form, a, b):
    return jnp.einsum(form, a, b, preferred_element_type=F32)


def mm_tn(a, b):
    return lax.dot_general(a, b, (((0,), (0,)), ((), ())), preferred_element_type=F32)


def params():
    return pltpu.CompilerParams(vmem_limit_bytes=VMEM_BYTES)


def cost(micros):
    return pl.CostEstimate(flops=int(micros * 1.1e9), bytes_accessed=0, transcendentals=0)


def whole(shape):
    return pl.BlockSpec(shape, lambda *unused: (0,) * len(shape))


def called(
    kernel,
    name,
    outs,
    info,
    operands,
    in_specs=None,
    scratch=(),
    micros=5,
    grid=(1,),
    out_specs=None,
    aliases=None,
    deps=(),
    through=(),
):
    specs = [None] * len(operands) if in_specs is None else in_specs
    specs = [whole(a.shape) if b is None else b for a, b in zip(operands, specs)]
    results = [whole(shape) for shape, unused in outs] if out_specs is None else list(out_specs)
    shapes = [jax.ShapeDtypeStruct(shape, kind) for shape, kind in outs]
    shapes += [jax.ShapeDtypeStruct(a.shape, a.dtype) for a in through]
    held = pl.BlockSpec(memory_space=pl.ANY)
    aliases = dict(aliases or {})
    for i in range(len(through)):
        aliases[1 + len(operands) + i] = len(outs) + i
    extra = len(through) + len(deps)

    def inner(info_ref, *refs):
        ins, rest = refs[: len(operands)], refs[len(operands) + extra :]
        kernel(info_ref, *ins, *rest[: len(outs)], *rest[len(outs) + len(through) :])

    call = pl.pallas_call(
        inner,
        out_shape=shapes,
        grid_spec=pltpu.PrefetchScalarGridSpec(
            num_scalar_prefetch=1,
            grid=grid,
            in_specs=specs + [held] * extra,
            out_specs=results + [held] * len(through),
            scratch_shapes=list(scratch),
        ),
        input_output_aliases=aliases,
        compiler_params=params(),
        cost_estimate=cost(micros),
        name=name,
    )
    return list(call(info, *operands, *through, *deps))


def released(info, arrays, deps):
    def kernel(info_ref, out_ref):
        out_ref[...] = jnp.zeros_like(out_ref)

    return called(kernel, "released", [((8, 128), F32)], info, [], micros=1, deps=deps, through=arrays)[1:]


INFO = 2


def doc_start(info_ref, position):
    bound = 0
    start = jnp.zeros_like(position)
    for i in range(INFO, info_ref.shape[0]):
        bound = bound + info_ref[i]
        start = jnp.where(position >= bound, bound, start)
    return start


def doc_end(info_ref):
    bound = 0
    for i in range(INFO, info_ref.shape[0]):
        bound = bound + info_ref[i]
    return bound


def need_mask(info_ref, key_start, last_query):
    return doc_start(info_ref, jnp.full((1, 128), last_query, jnp.int32))[0, 0] > key_start


def route_kernel(local, info_ref, routes_ref, g_ref, pick_ref, train_ref, frozen_ref):
    tok = g_ref.shape[0]
    half = pick_ref.shape[0] // 2
    first, second = routes_ref[0:1, :], routes_ref[1:2, :]
    row = lax.broadcasted_iota(jnp.int32, (EXPERTS, tok), 0)
    expert = jnp.where(row < FROZEN, row + FROZEN, row - FROZEN)
    position = info_ref[0] * tok + lax.broadcasted_iota(jnp.int32, (EXPERTS, tok), 1)
    live = ((expert == first) | (expert == second)) & (position < doc_end(info_ref))
    earlier = lax.broadcasted_iota(jnp.int32, (tok, tok), 0) < lax.broadcasted_iota(
        jnp.int32, (tok, tok), 1
    )
    place = mm(jnp.where(live, 1.0, 0.0).astype(BF), jnp.where(earlier, 1.0, 0.0).astype(BF))
    place = jnp.where(live, place, -1.0)
    slot = lax.broadcasted_iota(jnp.int32, (CAP, tok), 0).astype(F32)
    sums = jnp.broadcast_to((first + second).astype(F32), (16, tok)).astype(BF)
    sum_row = lax.broadcasted_iota(jnp.int32, (16, CAP), 0)
    for part, out_ref in ((0, train_ref), (1, frozen_ref)):
        for d in range(FROZEN // local):
            found = jnp.zeros((16, CAP), F32)
            for i in range(local):
                e = part * FROZEN + d * local + i
                taken = jnp.where(place[e : e + 1, :] == slot, 1.0, 0.0).astype(BF)
                pick_ref[e * CAP : (e + 1) * CAP, :] = taken
                found = jnp.where(sum_row == i, mm_nt(sums, taken), found)
            out_ref[d, local * CAP :, :] = jnp.zeros((16, D), BF)
            out_ref[d, local * CAP :, 0:CAP] = found.astype(BF)
        rows = mm(pick_ref[part * half : (part + 1) * half, :], g_ref[...]).astype(BF)
        for d in range(FROZEN // local):
            out_ref[d, : local * CAP, :] = rows[d * local * CAP : (d + 1) * local * CAP, :]


def route(info, local, routes, g):
    tok = g.shape[0]
    sent = (FROZEN // local, local * CAP + 16, D)

    def kernel(*refs):
        route_kernel(local, *refs)

    return called(
        kernel,
        "route",
        [((EXPERTS * CAP, tok), BF), (sent, BF), (sent, BF)],
        info,
        [routes, g],
        micros=6,
    )


def slot_sums(tile, local_id):
    parts = []
    for i in range(tile.shape[0]):
        turned = tile[i].astype(F32).T
        lane = lax.broadcasted_iota(jnp.int32, turned.shape, 1)
        column = jnp.sum(jnp.where(lane == local_id, turned, 0.0), axis=1, keepdims=True)
        parts.append(column[:CAP, :])
    return jnp.concatenate(parts, axis=0)


def gelu_parts(h):
    h2 = h * h
    t = jnp.tanh(h * (TANH_A + (TANH_A * TANH_B) * h2))
    half = 0.5 * t + 0.5
    act = h * half
    slope = half + act * (1.0 - half) * (2.0 * TANH_A + (6.0 * TANH_A * TANH_B) * h2)
    return act, slope


def attend_kernel(step, last, info_ref, x_ref, gain_ref, w_q_ref, w_k_ref, w_v_ref, *refs):
    first = step == 0
    refs = list(refs)
    if first:
        n1_ref, q_ref = refs[:2]
        refs = refs[2:]
    else:
        q_ref, m_in, l_in, acc_in, n1_ref = refs[:5]
        refs = refs[5:]
    if last:
        attn_ref = refs.pop(0)
        l_ref = refs.pop(0)
        m_ref, acc_ref, k_all, v_all = refs
    else:
        m_ref, l_ref, acc_ref, k_all, v_all = refs
    block = info_ref[0] - step
    rows = x_ref.shape[0]
    pairs = k_all.shape[0]

    x = x_ref[...].astype(F32)
    n1 = x * lax.rsqrt(jnp.mean(x * x, axis=1, keepdims=True) + EPS) * gain_ref[...]
    n1_ref[...] = n1.astype(BF)

    def project():
        n1 = n1_ref[...]
        for i in range(pairs // 2):
            cols = slice(i * 4 * HEAD, (i + 1) * 4 * HEAD)
            k = mm(n1, w_k_ref[:, cols]).astype(BF)
            v = mm(n1, w_v_ref[:, cols]).T.astype(BF)
            for j in range(2):
                k_all[2 * i + j] = k[:, j * 2 * HEAD : (j + 1) * 2 * HEAD]
                v_all[2 * i + j] = v[j * 2 * HEAD : (j + 1) * 2 * HEAD, :]
            if first:
                q = mm(n1, w_q_ref[:, cols]).astype(BF) * jnp.asarray(HEAD**-0.5, BF)
                for j in range(2):
                    q_ref[2 * i + j] = q[:, j * 2 * HEAD : (j + 1) * 2 * HEAD]

    def attend(masked):
        key_pos = block * rows + lax.broadcasted_iota(jnp.int32, (rows, rows), 0)
        query_pos = info_ref[0] * rows + lax.broadcasted_iota(jnp.int32, (1, rows), 1)
        start = doc_start(info_ref, query_pos)

        def pair(p, carry):
            q = q_ref[p]
            k = k_all[p]
            lane = lax.broadcasted_iota(jnp.int32, q.shape, 1)
            zero = jnp.zeros_like(q)
            found = [
                mm_nt(k, jnp.where(lane < HEAD, q, zero)),
                mm_nt(k, jnp.where(lane < HEAD, zero, q)),
            ]
            for half in range(2):
                scores = found[half]
                if masked:
                    allowed = key_pos >= start
                    if first:
                        allowed = allowed & (key_pos <= query_pos)
                    scores = jnp.where(allowed, scores, MASKED)
                top = jnp.max(scores, axis=0, keepdims=True)
                if not first:
                    old = m_in[p, half : half + 1, :]
                    top = jnp.maximum(top, old)
                probs = jnp.exp(scores - top)
                total = jnp.sum(probs, axis=0, keepdims=True)
                value = mm(v_all[p, half * HEAD : (half + 1) * HEAD, :], probs.astype(BF))
                part = pl.ds(pl.multiple_of(p * 2 * HEAD + half * HEAD, HEAD), HEAD)
                if not first:
                    decay = jnp.exp(old - top)
                    total = total + l_in[p, half : half + 1, :] * decay
                    value = value + acc_in[part, :] * decay
                m_ref[p, half : half + 1, :] = top
                l_ref[p, half : half + 1, :] = total
                acc_ref[part, :] = value
            return carry

        lax.fori_loop(0, pairs, pair, 0)

    if first:
        project()
        attend(True)
    else:
        masked = need_mask(info_ref, block * rows, info_ref[0] * rows + rows - 1)

        @pl.when(block >= 0)
        def _():
            project()

        @pl.when((block >= 0) & masked)
        def _():
            attend(True)

        @pl.when((block >= 0) & jnp.logical_not(masked))
        def _():
            attend(False)

        @pl.when(block < 0)
        def _():
            m_ref[...] = m_in[...]
            l_ref[...] = l_in[...]
            acc_ref[...] = acc_in[...]

    if last:
        for p in range(pairs):
            for half in range(2):
                part = slice((2 * p + half) * HEAD, (2 * p + half + 1) * HEAD)
                total = l_ref[p, half : half + 1, :]
                acc_ref[part, :] = acc_ref[part, :] / total
                l_ref[p, half : half + 1, :] = m_ref[p, half : half + 1, :] + jnp.log(total)
            part = slice(p * 2 * HEAD, (p + 1) * 2 * HEAD)
            attn_ref[:, part] = acc_ref[part, :].T.astype(BF)


def attend_step(step, last, info, x, gain, w, state, deps=(), through=()):
    tok = x.shape[0]
    pairs = HEADS // 2
    stat, acc = ((pairs, 2, tok), F32), ((D, tok), F32)
    row, by_pair = ((tok, D), BF), ((pairs, tok, 2 * HEAD), BF)
    outs = [row] + ([by_pair] if step == 0 else []) + ([row, stat] if last else [stat, stat, acc])
    scratch = [pltpu.VMEM(*by_pair), pltpu.VMEM((pairs, 2 * HEAD, tok), BF)]
    if last:
        scratch = [pltpu.VMEM(*stat), pltpu.VMEM(*acc)] + scratch

    def kernel(*refs):
        attend_kernel(step, last, *refs)

    square = (D, D)
    return called(
        kernel,
        "attend_step",
        outs,
        info,
        [x, gain, w, w, w, *state],
        [
            None,
            None,
            pl.BlockSpec(square, lambda i, r: (0, 0)),
            pl.BlockSpec(square, lambda i, r: (0, 1)),
            pl.BlockSpec(square, lambda i, r: (0, 2)),
        ]
        + [None] * len(state),
        scratch,
        micros=13,
        deps=deps,
        through=through,
    )


def attend_back_kernel(blocks, heads, info_ref, qkv_ref, misc_ref, *refs):
    n1_refs, do_refs, out_refs = [refs[i * blocks : (i + 1) * blocks] for i in range(3)]
    part_ref, dq_ref, dk_ref, dv_ref, k_mine, v_mine, k_t, do_all, lse_all, delta_all, out_all = refs[
        3 * blocks :
    ]
    rows = qkv_ref.shape[0] // blocks
    tiles, deep, width = do_refs[0].shape
    lane = lax.broadcasted_iota(jnp.int32, (rows, 2 * HEAD), 1)
    dq_ref[...] = jnp.zeros_like(dq_ref)

    def turn(b):
        return lax.rem(info_ref[0] - b + blocks, blocks)

    for b in range(blocks):
        do_all[b] = do_refs[b][:, :width, :].reshape(rows, width)
        stats = [do_refs[b][t, width:, :].astype(F32) for t in range(tiles)]
        stats = jnp.concatenate(stats, axis=1)
        delta_all[b] = stats[:heads] + stats[heads : 2 * heads]
        lse_all[b] = stats[2 * heads : 3 * heads] + stats[3 * heads : 4 * heads]

    def key_step(kb, carry):
        kt = turn(kb)
        key_rows = pl.ds(pl.multiple_of(kt * rows, rows), rows)
        for h in range(heads):
            first = (h // 2) * 2 * HEAD
            k = qkv_ref[key_rows, width + first : width + first + 2 * HEAD]
            v = qkv_ref[key_rows, 2 * width + first : 2 * width + first + 2 * HEAD]
            mine = (lane < HEAD) if h % 2 == 0 else (lane >= HEAD)
            zero = jnp.zeros_like(k)
            k_mine[h] = jnp.where(mine, k, zero)
            v_mine[h] = jnp.where(mine, v, zero)
            k_t[h] = k.T[(h % 2) * HEAD : (h % 2 + 1) * HEAD, :]
        dk_ref[...] = jnp.zeros_like(dk_ref)
        dv_ref[...] = jnp.zeros_like(dv_ref)

        def pair(qb, diagonal, masked):
            qt = turn(qb)
            query_rows = pl.ds(pl.multiple_of(qt * rows, rows), rows)
            if masked:
                key_pos = kb * rows + lax.broadcasted_iota(jnp.int32, (rows, rows), 0)
                query_pos = qb * rows + lax.broadcasted_iota(jnp.int32, (1, rows), 1)
                allowed = key_pos >= doc_start(info_ref, query_pos)
                if diagonal:
                    allowed = allowed & (key_pos <= query_pos)

            def of_head(h):
                cols = slice((h // 2) * 2 * HEAD, (h // 2 + 1) * 2 * HEAD)
                return qkv_ref[query_rows, cols], do_all[qt, :, cols]

            def products(h):
                q, do = of_head(h)
                return mm_nt(k_mine[h], q), mm_nt(v_mine[h], do)

            later = products(0)
            for h in range(heads):
                scores, dprobs = later
                if h + 1 < heads:
                    later = products(h + 1)
                q, do = of_head(h)
                probs = jnp.exp(scores - lse_all[qt, h : h + 1, :])
                if masked:
                    probs = jnp.where(allowed, probs, 0.0)
                dscores = (probs * (dprobs - delta_all[qt, h : h + 1, :])).astype(BF)
                dv_ref[h] += mm(probs.astype(BF), do)
                dk_ref[h] += mm(dscores, q)
                dq_ref[qt, h] += mm(k_t[h], dscores)

        pair(kb, True, True)

        def query_step(qb, carry):
            masked = need_mask(info_ref, kb * rows, qb * rows + rows - 1)

            @pl.when(masked)
            def _():
                pair(qb, False, True)

            @pl.when(jnp.logical_not(masked))
            def _():
                pair(qb, False, False)

            return carry

        lax.fori_loop(kb + 1, blocks, query_step, 0)
        for h in range(heads):
            part = slice((h % 2) * HEAD, (h % 2 + 1) * HEAD)
            for i, grad_ref in ((1, dk_ref), (2, dv_ref)):
                at = (i * heads + h) * HEAD
                out_all[kt, at : at + HEAD, :] = grad_ref[h].T[part, :].astype(BF)
        return carry

    lax.fori_loop(0, blocks, key_step, 0)
    total = 0.0
    for b in range(blocks):
        for h in range(heads):
            out_all[b, h * HEAD : (h + 1) * HEAD, :] = (dq_ref[b, h] * HEAD**-0.5).astype(BF)
        grads = out_all[b]
        out_refs[b][...] = grads
        total = total + mm(grads, n1_refs[b][...])
    part_ref[:, :MISC] = misc_ref[...]
    part_ref[:, MISC:] = total.T.astype(BF)


def attend_back(heads, info, qkv, misc, n1, dos, deps):
    rows = qkv.shape[0]
    blocks = len(dos)
    tiles, deep, width = dos[0].shape
    tok = rows // blocks
    cols = 3 * heads * HEAD

    def kernel(*refs):
        attend_back_kernel(blocks, heads, *refs)

    *grads, part = called(
        kernel,
        "attend_back",
        [((cols, tok), BF)] * blocks + [((D, MISC + cols), BF)],
        info,
        [qkv, misc, *n1, *dos],
        scratch=[
            pltpu.VMEM((blocks, heads, HEAD, tok), F32),
            pltpu.VMEM((heads, tok, 2 * HEAD), F32),
            pltpu.VMEM((heads, tok, 2 * HEAD), F32),
            pltpu.VMEM((heads, tok, 2 * HEAD), BF),
            pltpu.VMEM((heads, tok, 2 * HEAD), BF),
            pltpu.VMEM((heads, HEAD, tok), BF),
            pltpu.VMEM((blocks, tok, width), BF),
            pltpu.VMEM((blocks, heads, tok), F32),
            pltpu.VMEM((blocks, heads, tok), F32),
            pltpu.VMEM((blocks, cols, tok), BF),
        ],
        micros=32,
        deps=deps,
    )
    return grads, part


def project_back_kernel(blocks, info_ref, w_ref, *refs):
    out_ref = refs[blocks]
    rows = refs[0].shape[0]
    for b in range(blocks):
        out_ref[b * rows : (b + 1) * rows, :] = mm_nt(refs[b][...], w_ref[...]).astype(BF)


def project_back(info, w, n1, deps):
    blocks = len(n1)

    def kernel(*refs):
        project_back_kernel(blocks, *refs)

    shape = (blocks * n1[0].shape[0], w.shape[0])
    return called(kernel, "project_back", [(shape, BF)], info, [w, *n1], micros=7, deps=deps)[0]


def slot_gate(own, sums, x, router):
    lane = lax.broadcasted_iota(jnp.int32, (x.shape[0], router.shape[1]), 1)
    other = sums.astype(jnp.int32) - own
    signs = jnp.where(lane == own, 1.0, 0.0) - jnp.where(lane == other, 1.0, 0.0)
    margin = jnp.sum(mm(x, router) * signs, axis=1, keepdims=True)
    return 1.0 / (1.0 + jnp.exp(-margin)), signs


def expert_kernel(
    first_id, info_ref, x_ref, g_ref, sums_ref, router_ref, up_ref, down_ref, drouter_ref, *refs
):
    backs, handed = (refs[:1], refs[1:-6]) if len(refs) == 10 else (refs[:2], ())
    xs, dos, gate_ref, signs_ref, eacc, dacc = refs[-6:]
    expert = pl.program_id(0)
    step = pl.program_id(1)
    rows = xs.shape[0]
    block = x_ref.shape

    @pl.when(step == 0)
    def _():
        x = x_ref[...].reshape(rows, D)
        xs[...] = x
        own = first_id + info_ref[1] * pl.num_programs(0) + expert
        gate, signs = slot_gate(own, slot_sums(sums_ref, expert), x, router_ref[...])
        gate_ref[...] = gate
        signs_ref[...] = signs
        do = (gate * g_ref[...].reshape(rows, D).astype(F32)).astype(BF)
        dos[...] = do
        if handed:
            handed[0][...] = do.reshape(block)
            for x_out in handed[1:]:
                x_out[...] = x.reshape(block)

    act, slope = gelu_parts(mm(xs[...], up_ref[0]))
    dhid = (mm_nt(dos[...], down_ref[0]) * slope).astype(BF)
    out = mm(act.astype(BF), down_ref[0])
    dx = mm_nt(dhid, up_ref[0])

    @pl.when(step == 0)
    def _():
        eacc[...] = out
        dacc[...] = dx

    @pl.when(step > 0)
    def _():
        eacc[...] += out
        dacc[...] += dx

    @pl.when(step == pl.num_programs(1) - 1)
    def _():
        out = eacc[...]
        gate = gate_ref[...]
        g = g_ref[...].reshape(rows, D).astype(F32)
        mix = (gate * out).astype(BF).reshape(block)
        dgate = jnp.sum(g * out, axis=1, keepdims=True)
        dlogits = (gate * (1.0 - gate) * dgate * signs_ref[...]).astype(BF)
        dx = dacc[...] + mm_nt(dlogits, router_ref[...])
        dx = dx.astype(BF).reshape(block)
        if handed:
            backs[0][:, 0] = dx
            backs[0][:, 1] = mix
        else:
            backs[0][...] = dx
            backs[1][...] = mix
        drouter = mm_tn(dlogits, xs[...])

        @pl.when(expert == 0)
        def _():
            drouter_ref[...] = drouter

        @pl.when(expert > 0)
        def _():
            drouter_ref[...] += drouter


def expert_rows(first_id, info, x, g, router, up, down, handing, deps, through=()):
    sources, experts = x.shape[:2]
    rows = sources * CAP
    hidden = up.shape[2]
    tile = 1536
    row_spec = pl.BlockSpec((sources, 1, CAP, D), lambda e, f, r: (0, e, 0, 0))


    def kernel(*refs):
        expert_kernel(first_id, *refs)

    outs, out_specs = [((router.shape[1], D), F32)], [whole((router.shape[1], D))]
    if handing:
        outs += [((sources, 2) + x.shape[1:], BF)]
        out_specs += [pl.BlockSpec((sources, 2, 1, CAP, D), lambda e, f, r: (0, 0, e, 0, 0))]
    else:
        outs += [(x.shape, BF), (x.shape, BF)]
        out_specs += [row_spec, row_spec]
    if handing:
        outs += [(x.shape, BF)] * 3
        out_specs += [row_spec] * 3

    return called(
        kernel,
        "expert_rows",
        outs,
        info,
        [x, g, g, router, up, down],
        [
            row_spec,
            pl.BlockSpec((sources, CAP, D), lambda e, f, r: (0, e, 0)),
            pl.BlockSpec((sources, 16, 128), lambda e, f, r: (0, experts * CAP // 16, 0)),
            None,
            pl.BlockSpec((1, D, tile), lambda e, f, r: (e, 0, f)),
            pl.BlockSpec((1, tile, D), lambda e, f, r: (e, f, 0)),
        ],
        [
            pltpu.VMEM((rows, D), BF),
            pltpu.VMEM((rows, D), BF),
            pltpu.VMEM((rows, 1), F32),
            pltpu.VMEM((rows, 128), F32),
            pltpu.VMEM((rows, D), F32),
            pltpu.VMEM((rows, D), F32),
        ],
        micros=23,
        grid=(experts, hidden // tile),
        out_specs=out_specs,
        deps=deps,
        through=through,
    )


def gated_kernel(count, info_ref, router_ref, *refs):
    x_refs, g_refs, sum_refs, out_refs = [refs[i * count : (i + 1) * count] for i in range(4)]
    for i, again_ref in enumerate(refs[4 * count :]):
        again_ref[...] = x_refs[i][...]
    sources, experts = x_refs[0].shape[:2]
    for b in range(count):
        for e in range(experts):
            own = FROZEN + info_ref[1] * experts + e
            x = x_refs[b][:, e].reshape(sources * CAP, D)
            gate, unused = slot_gate(own, slot_sums(sum_refs[b], e), x, router_ref[...])
            g = g_refs[b][:, e * CAP : (e + 1) * CAP, :].reshape(sources * CAP, D).astype(F32)
            out_refs[b][:, e] = (gate * g).astype(BF).reshape(sources, CAP, D)


def gated(info, router, xs, gs, sums, deps=(), again=0):
    count = len(xs)

    def kernel(*refs):
        gated_kernel(count, *refs)

    return called(
        kernel,
        "gated",
        [(x.shape, BF) for x in [*xs, *xs[:again]]],
        info,
        [router, *xs, *gs, *sums],
        micros=1,
        deps=deps,
    )


def expert_grad_kernel(group, add, info_ref, ins, dup_ref, ddown_ref, done_ref, xs, dos):
    up_ref, down_ref = ins[:2]
    x_refs, do_refs = ins[2 : 2 + group], ins[2 + group : 2 + 2 * group]
    rows = xs.shape[0] // group

    @pl.when(pl.program_id(0) == 0)
    def _():
        done_ref[...] = jnp.zeros_like(done_ref)
        for b in range(group):
            part = slice(b * rows, (b + 1) * rows)
            xs[part, :] = x_refs[b][...].reshape(rows, D)
            dos[part, :] = do_refs[b][...].reshape(rows, D)

    act, slope = gelu_parts(mm(xs[...], up_ref[0]))
    dhid = (mm_nt(dos[...], down_ref[0]) * slope).astype(BF)
    ddown = mm_tn(act.astype(BF), dos[...])
    dup = mm_tn(xs[...], dhid)
    if add:
        ddown = ddown + ins[-1][0]
        dup = dup + ins[-2][0]
    ddown_ref[0] = ddown
    dup_ref[0] = dup


def expert_grads(expert, span, first, group, info, xs, dos, up, down, totals, deps, through):
    sources, experts = dos[0].shape[:2]
    rows = group * sources * CAP
    tile = GRAD_TILE
    start, count = span
    add = first > 0
    up_spec = pl.BlockSpec((1, D, tile), lambda f, r: (expert, 0, start + f))
    down_spec = pl.BlockSpec((1, tile, D), lambda f, r: (expert, start + f, 0))
    in_specs = [up_spec, down_spec]
    in_specs += [pl.BlockSpec((sources, 1, CAP, D), lambda f, r: (0, expert, 0, 0))] * (2 * group)
    part = slice(first, first + group)
    operands = [up, down, *xs[part], *dos[part]]
    aliases = {}
    if totals is not None:
        aliases = {1 + len(operands): 0, 2 + len(operands): 1}
        in_specs += [up_spec, down_spec] if add else [pl.BlockSpec(memory_space=pl.ANY)] * 2
        operands += list(totals)

    def kernel(info_ref, *refs):
        ins, rest = refs[: len(operands)], refs[len(operands) :]
        expert_grad_kernel(group, add, info_ref, ins, *rest)

    return called(
        kernel,
        "expert_grads",
        [(up.shape, F32), (down.shape, F32), ((8, 128), F32)],
        info,
        operands,
        in_specs,
        [pltpu.VMEM((rows, D), BF), pltpu.VMEM((rows, D), BF)],
        micros=9 * count,
        grid=(count,),
        out_specs=[up_spec, down_spec, whole((8, 128))],
        aliases=aliases,
        deps=deps,
        through=through,
    )


def expert_grads_part(expert, span, info, xs, dos, up, down, totals, deps, through):
    blocks = len(xs)
    group = max(1, min(blocks, GRAD_ROWS // (dos[0].shape[0] * CAP)))
    for first in range(0, blocks, group):
        dup, ddown, done, *through = expert_grads(
            expert, span, first, group, info, xs, dos, up, down, totals, deps, through
        )
        totals = [dup, ddown]
    return totals, [done, *through]


def token_forward_kernel(
    info_ref, attn_ref, x_ref, gain_ref, w_ref, pick_ref, mid_ref, square_ref, train_ref, frozen_ref
):
    tok = x_ref.shape[0]
    half = pick_ref.shape[0] // 2
    branch = mm(attn_ref[...], w_ref[...])
    mid = x_ref[...].astype(F32) + branch
    mid_ref[...] = mid
    r = lax.rsqrt(jnp.mean(mid * mid, axis=1, keepdims=True) + EPS)
    n2 = (mid * r * gain_ref[...]).astype(BF)
    train_ref[...] = mm(pick_ref[:half, :], n2).astype(BF)
    frozen_ref[...] = mm(pick_ref[half:, :], n2).astype(BF)
    position = info_ref[0] * tok + lax.broadcasted_iota(jnp.int32, (tok, D), 0)
    square = jnp.where(position < doc_end(info_ref), branch * branch, 0.0)
    square_ref[...] = jnp.sum(square, axis=0, keepdims=True)


def token_forward(info, attn, x, gain, w, pick):
    tok = x.shape[0]
    half = ((pick.shape[0] // 2, D), BF)
    return called(
        token_forward_kernel,
        "token_forward",
        [((tok, D), F32), ((1, D), F32), half, half],
        info,
        [attn, x, gain, w, pick],
        [None] * 5,
        micros=6,
    )


def token_back_kernel(
    heads,
    groups,
    info_ref,
    pick_ref,
    dx_t_ref,
    dx_f_ref,
    mid_ref,
    g_ref,
    gain_ref,
    w_ref,
    wg_ref,
    attn_ref,
    lse_ref,
    head_ref,
    *refs,
):
    send_refs = refs[:groups]
    dmid_ref, dbranch_ref, dgain_ref = refs[groups:]
    tiles, deep, width = send_refs[0].shape
    tok = mid_ref.shape[0]
    half = pick_ref.shape[0] // 2

    dn2 = mm_tn(pick_ref[:half, :], dx_t_ref[...].reshape(half, D))
    dn2 = dn2 + mm_tn(pick_ref[half:, :], dx_f_ref[...].reshape(half, D))
    mid = mid_ref[...]
    r = lax.rsqrt(jnp.mean(mid * mid, axis=1, keepdims=True) + EPS)
    u = mid * r
    dgain_ref[...] = jnp.sum(dn2 * u, axis=0, keepdims=True)
    scaled = dn2 * gain_ref[...]
    dmid = g_ref[...].astype(F32) + r * (scaled - u * jnp.mean(scaled * u, axis=1, keepdims=True))
    dmid_ref[...] = dmid
    dbranch = dmid.astype(BF)
    dbranch_ref[...] = dbranch

    dattn = mm_nt(dbranch, w_ref[...]).astype(BF).astype(F32)
    prod = dattn * attn_ref[...].astype(F32)
    high = prod.astype(BF)
    low = (prod - high.astype(F32)).astype(BF)
    for turn in range(groups):
        g = lax.rem(info_ref[0] + turn, groups)
        sent = mm_nt(dbranch, wg_ref[g]).astype(BF)
        delta = mm_nt(head_ref[g], high) + mm_nt(head_ref[g], low)
        parts = []
        for stat in (delta[:heads], lse_ref[g][:heads]):
            high_part = stat.astype(BF).astype(F32)
            parts += [high_part, stat - high_part]
        blank = jnp.zeros((16 - 4 * heads, tok), F32)
        stats = jnp.concatenate(parts + [blank], axis=0).astype(BF)
        for t in range(tiles):
            part = slice(t * width, (t + 1) * width)
            send_refs[turn][t, :width, :] = sent[part, :]
            send_refs[turn][t, width:, :] = stats[:, part]


def token_back(
    heads, groups, width, info, pick, dx_t, dx_f, mid, g, gain, w, w_groups, attn, lse, head_rows, deps, through
):
    tok = mid.shape[0]
    tiles = tok // width

    def kernel(*refs):
        token_back_kernel(heads, groups, *refs)

    outs = [((tiles, width + 16, width), BF)] * groups
    operands = [pick, dx_t, dx_f, mid, g, gain, w, w_groups, attn, lse, head_rows]
    half = (dx_f.shape[0], 1) + dx_f.shape[1:]
    found = called(
        kernel,
        "token_back",
        outs + [((tok, D), F32), ((tok, D), BF), ((1, D), F32)],
        info,
        operands,
        [None, pl.BlockSpec(half, lambda i, r: (0, 0, 0, 0, 0))] + [None] * (len(operands) - 2),
        micros=10,
        deps=deps,
        through=through,
    )
    return [found[:groups]] + found[groups:]


def token_mix_kernel(
    info_ref, pick_ref, mix_t_ref, mix_f_ref, mid_ref, x_ref, attn_ref, dbranch_ref, rt_ref, rf_ref, dgain_ref, square_ref, out_ref, misc_ref
):
    tok = mid_ref.shape[0]
    half = pick_ref.shape[0] // 2
    mix = mm_tn(pick_ref[:half, :], mix_t_ref[...].reshape(half, D))
    mix = mix + mm_tn(pick_ref[half:, :], mix_f_ref[...].reshape(half, D))
    out_ref[...] = (mid_ref[...] + mix).astype(BF)
    valid = info_ref[0] * tok + lax.broadcasted_iota(jnp.int32, (tok, D), 0) < doc_end(info_ref)
    x = x_ref[...].astype(F32)
    stats = [
        jnp.sum(jnp.where(valid, x * x, 0.0)),
        jnp.sum(square_ref[...]),
        jnp.sum(jnp.where(valid, mix * mix, 0.0)),
        jnp.clip(doc_end(info_ref) - info_ref[0] * tok, 0, tok).astype(F32),
    ]
    misc_ref[:, :D] = mm_tn(attn_ref[...], dbranch_ref[...]).astype(BF)
    tail = (rt_ref[...] + rf_ref[...]).T
    gains = jnp.broadcast_to(dgain_ref[...], (8, D)).T[:, 0:1]
    row = lax.broadcasted_iota(jnp.int32, tail.shape, 0)
    lane = lax.broadcasted_iota(jnp.int32, tail.shape, 1)
    tail = jnp.where(lane < EXPERTS, tail, 0.0) + jnp.where(lane == EXPERTS, gains, 0.0)
    for i, stat in enumerate(stats):
        tail = tail + jnp.where((lane == EXPERTS + 1 + i) & (row == 0), stat, 0.0)
    misc_ref[:, D : D + 128] = tail.astype(BF)


def token_mix(info, pick, back_t, mix_f, mid, x, attn, dbranch, router_t, router_f, dgain, square):
    tok = mid.shape[0]
    operands = [pick, back_t, mix_f, mid, x, attn, dbranch, router_t, router_f, dgain, square]
    half = (mix_f.shape[0], 1) + mix_f.shape[1:]
    return called(
        token_mix_kernel,
        "token_mix",
        [((tok, D), BF), ((D, MISC), BF)],
        info,
        operands,
        [None, pl.BlockSpec(half, lambda i, r: (0, 1, 0, 0, 0))] + [None] * (len(operands) - 2),
        micros=1,
    )


def input_grad_kernel(heads, blocks, info_ref, x_ref, gain_ref, dmid_ref, w_ref, *refs):
    grad_refs, out_ref = refs[:blocks], refs[blocks]
    wide = heads * HEAD
    dn1 = 0.0
    for turn in range(blocks):
        g = lax.rem(info_ref[0] + turn, blocks)
        for c in range(3):
            rows = pl.ds(pl.multiple_of(c * blocks * wide + g * wide, HEAD), wide)
            part = grad_refs[turn][c * wide : (c + 1) * wide, :]
            dn1 = dn1 + mm_tn(part, w_ref[rows, :])
    x = x_ref[...].astype(F32)
    r = lax.rsqrt(jnp.mean(x * x, axis=1, keepdims=True) + EPS)
    u = x * r
    scaled = dn1 * gain_ref[...]
    dx = r * (scaled - u * jnp.mean(scaled * u, axis=1, keepdims=True))
    out_ref[...] = (dmid_ref[...] + dx).astype(BF)


def input_grad_rows(heads, info, x, gain, dmid, w_t, grads, deps):
    blocks = len(grads)

    def kernel(*refs):
        input_grad_kernel(heads, blocks, *refs)

    operands = [x, gain, dmid, w_t, *grads]
    return called(
        kernel, "input_grad", [(x.shape, BF)], info, operands, micros=8, deps=deps
    )[0]


def sum_kernel(info_ref, a_ref, w_ref, out_ref):
    total = a_ref[0].astype(F32)
    for i in range(1, a_ref.shape[0]):
        total = total + a_ref[i].astype(F32)
    out_ref[...] = total.astype(BF)
    gain = jnp.sum(total[:, MISC:] * w_ref[...].astype(F32), axis=1, keepdims=True)
    lane = lax.broadcasted_iota(jnp.int32, (total.shape[0], 128), 1)
    out_ref[:, D:MISC] = jnp.where(lane == GAIN1_AT, gain, total[:, D:MISC]).astype(BF)


def sum_parts(info, a, w, deps):
    return called(sum_kernel, "sum_parts", [(a.shape[1:], BF)], info, [a, w], micros=3, deps=deps)[0]


def join_kernel(info_ref, *refs):
    found, out_ref, again_ref = refs[:-2], refs[-2], refs[-1]
    total = found[0][:, :MISC].astype(F32)
    for ref in found[1:]:
        total = total + ref[:, :MISC].astype(F32)
    out_ref[:, :MISC] = total.astype(BF)
    cols = found[0].shape[1] - MISC
    for i, ref in enumerate(found):
        out_ref[:, MISC + i * cols : MISC + (i + 1) * cols] = ref[:, MISC:]
    again_ref[...] = out_ref[...]


def join_blocks(info, found, deps):
    rows, cols = found[0].shape
    shape = (rows, MISC + len(found) * (cols - MISC))
    return called(
        join_kernel, "join_blocks", [(shape, BF)] * 2, info, list(found), micros=3, deps=deps
    )


def layout_kernel(heads, info_ref, here_ref, there_ref, gain_ref, qkv_ref, out_ref, router_ref, gain1_ref, gain2_ref, stat_ref, tails):
    step = pl.program_id(0)
    rows = here_ref.shape[1]
    wide = heads * HEAD
    groups = (here_ref.shape[2] - MISC) // (3 * wide)

    def lay(part, piece):
        out_ref[part, :] = piece[:, :D].astype(F32)
        tail = piece[:, D:MISC].astype(F32)
        for turn in range(groups):
            g = lax.rem(info_ref[0] - turn + groups, groups)
            for c in range(3):
                at = MISC + (3 * turn + c) * wide
                grad = piece[:, at : at + wide].astype(F32)
                for g_now in range(groups):
                    cols = min(wide, D - g_now * wide)
                    to = c * D + g_now * wide
                    if cols > 0:

                        @pl.when(g == g_now)
                        def _():
                            qkv_ref[part, to : to + cols] = grad[:, :cols]

        return tail

    mine = lax.rem(info_ref[1], 2)
    for core in range(2):
        part = slice(core * rows, (core + 1) * rows)
        at = pl.ds(pl.multiple_of((2 * step + core) * rows, rows), rows)

        @pl.when(mine == core)
        def _():
            tails[at, :] = lay(part, here_ref[0])

        @pl.when(mine != core)
        def _():
            tails[at, :] = lay(part, there_ref[0])

    @pl.when(step == pl.num_programs(0) - 1)
    def _():
        turned = tails[...].T
        gain1_ref[...] = turned[GAIN1_AT] / gain_ref[0]
        gain2_ref[...] = turned[EXPERTS]
        router_ref[...] = turned[:EXPERTS]
        stats = tails[0:8, :]
        lane = lax.broadcasted_iota(jnp.int32, stats.shape, 1)
        count = jnp.sum(jnp.where(lane == EXPERTS + 4, stats, 0.0), axis=1, keepdims=True)
        used = (lane > EXPERTS) & (lane < EXPERTS + 4)
        stat_ref[...] = jnp.sqrt(jnp.where(used, stats, 0.0) / (jnp.maximum(count, 1.0) * D))


def layout(heads, info, here, there, gain):
    chips, rows, width = here.shape

    def kernel(*refs):
        layout_kernel(heads, *refs)

    piece_spec = pl.BlockSpec((1, rows, width), lambda e, r: (e ^ (r[1] // 2), 0, 0))

    def row_spec(cols):
        return pl.BlockSpec((2 * rows, cols), lambda e, r: (e, 0))

    return called(
        kernel,
        "layout",
        [((D, 3 * D), F32), ((D, D), F32), ((EXPERTS, D), F32), ((D,), F32), ((D,), F32), ((8, 128), F32)],
        info,
        [here, there, gain],
        [piece_spec, piece_spec, None],
        [pltpu.VMEM((D, 128), F32)],
        micros=12,
        grid=(chips,),
        out_specs=[row_spec(3 * D), row_spec(D), whole((EXPERTS, D)), whole((D,)), whole((D,)), whole((8, 128))],
    )


def shifted(x, by, count):
    return lax.ppermute(x, "seq", [(i, (i + by) % count) for i in range(count)])


def swap(x, axis):
    return lax.all_to_all(x, axis, split_axis=0, concat_axis=0, tiled=True)


def both_ways(found, step, count):
    found = [shifted(found[0], 1, count), shifted(found[1], -1, count)] if 2 * step < count else [
        shifted(found[0], 1, count)
    ]
    return found


def body(
    layer_input,
    lengths,
    routes,
    norm1_gain,
    qkv_weight,
    out_weight,
    norm2_gain,
    router_weight,
    frozen_up,
    frozen_down,
    train_up,
    train_down,
    cotangent,
):
    tok = layer_input.shape[1]
    n_seq = lax.axis_size("seq")
    n_exp = lax.axis_size("exp")
    rank = lax.axis_index("seq")
    column = lax.axis_index("exp")
    heads = -(-HEADS // n_seq)
    wide = heads * HEAD
    width = (heads + heads % 2) * HEAD
    local = FROZEN // n_exp
    x_own = layer_input[0]
    g_own = cotangent[0]
    gain1 = norm1_gain[None, :]
    gain2 = norm2_gain[None, :]
    info = jnp.concatenate([jnp.stack([rank, column]).astype(jnp.int32), lengths[0]])

    w_t = qkv_weight.T
    w_parts = jnp.pad(w_t.reshape(3, D, D), ((0, 0), (0, n_seq * wide - D), (0, 0)))
    w_mine = lax.dynamic_slice_in_dim(w_parts, rank * wide, wide, axis=1)
    w_chunk = lax.dynamic_slice_in_dim(w_mine, column * (D // n_exp), D // n_exp, axis=2)
    w_chunk = w_chunk.reshape(3 * wide, D // n_exp).T
    w_mine = w_mine * jnp.asarray([HEAD**-0.5, 1.0, 1.0], BF)[:, None, None]
    w_mine = jnp.pad(w_mine, ((0, 0), (0, width - wide), (0, 0))).reshape(3 * width, D)
    w_parts = w_parts.reshape(3 * n_seq * wide, D)
    out_groups = jnp.pad(out_weight, ((0, n_seq * wide - D), (0, 0)))
    out_groups = jnp.pad(out_groups.reshape(n_seq, wide, D), ((0, 0), (0, width - wide), (0, 0)))
    feature_head = jnp.arange(D, dtype=jnp.int32) // HEAD
    row_id = jnp.arange(8, dtype=jnp.int32)[None, :] + heads * jnp.arange(n_seq, dtype=jnp.int32)[:, None]
    row_id = jnp.where(jnp.arange(8)[None, :] < heads, row_id, -1)
    head_rows = (row_id[:, :, None] == feature_head[None, None, :]).astype(BF)
    router = jnp.pad(router_weight, ((0, 0), (0, 128 - EXPERTS)))

    pick, g_train, g_frozen = route(info, local, routes[0].T, g_own)
    early = max(n_seq - 3, 0)
    x_now = x_own
    n1_list = []
    state = ()
    for step in range(n_seq):
        last = step == n_seq - 1
        if last:
            [g_rows] = released(info, [g_train[:, : local * CAP]], [x_now])
        x_next = None if last else shifted(x_now, 1, n_seq)
        found = attend_step(
            step,
            last,
            info,
            x_now,
            gain1,
            qkv_weight,
            state,
            through=[g_train] if step == early else [g_frozen] if step == early + 1 else [],
        )
        if step == early:
            g_train = swap(found.pop(), "exp")
        elif step == early + 1:
            g_frozen = swap(found.pop(), "exp")
        n1_list.append(found[0])
        state = tuple(found[1:]) if step == 0 else (state[0],) + tuple(found[1:])
        x_now = x_next
    unused_q, attn, lse = state

    mid, branch_squares, rows_train, rows_frozen = token_forward(
        info, attn, x_own, gain2, out_weight, pick
    )
    x_train = swap(rows_train.reshape(n_exp, local, CAP, D), "exp")
    x_frozen = swap(rows_frozen.reshape(n_exp, local, CAP, D), "exp")

    steps = range(1, n_seq // 2 + 1)
    g_steps = [both_ways([g_rows, g_rows], 1, n_seq)]
    for step in steps[1:]:
        g_steps.append(both_ways(g_steps[-1], step, n_seq))
    router_t, back_t, do_own, x_up, x_down, sums_own = expert_rows(
        FROZEN,
        info,
        x_train,
        g_train,
        router,
        train_up,
        train_down,
        True,
        g_steps[0],
        [g_train[:, local * CAP :, :128]],
    )
    sums = {by: shifted(sums_own, by, n_seq) for by in range(1, n_seq)}
    sum_steps = [
        [sums[step]] + ([sums[n_seq - step]] if 2 * step < n_seq else []) for step in steps
    ]
    back_t = swap(back_t, "exp")
    x_own_rows = x_up
    router_f, dx_f_out, mix_f = expert_rows(
        0,
        info,
        x_frozen,
        g_frozen,
        router,
        frozen_up,
        frozen_down,
        False,
        [w_mine, w_chunk] + [g for step in g_steps for g in step],
    )
    dx_f = swap(dx_f_out, "exp")
    x_steps = [both_ways([x_up, x_down], 1, n_seq)]
    qkv_mine = project_back(info, w_mine, n1_list, [dx_f_out])

    lse_rows = jnp.pad(lse.reshape(HEADS, tok), ((0, heads * n_seq - HEADS), (0, 0)))
    lse_rows = jnp.pad(lse_rows.reshape(n_seq, heads, tok), ((0, 0), (0, 8 - heads), (0, 0)))
    send, dmid, dbranch, dgain2, mix_f = token_back(
        heads,
        n_seq,
        width,
        info,
        pick,
        back_t,
        dx_f,
        mid,
        g_own,
        gain2,
        out_weight,
        out_groups,
        attn,
        lse_rows,
        head_rows,
        [qkv_mine, *x_steps[0], *sums.values()],
        [mix_f],
    )
    dos = [send[0]] + [shifted(send[step], step, n_seq) for step in range(1, n_seq)]
    mix_f = swap(mix_f, "exp")
    sends = 0 if n_seq < 4 else 1 if n_seq == 4 else 2
    found = gated(info, router, x_steps[0], g_steps[0], sum_steps[0], [send[0]], sends)
    gated_steps, x_go = [found[: len(x_steps[0])]], found[len(x_steps[0]) :]
    output, misc = token_mix(
        info, pick, back_t, mix_f, mid, x_own, attn, dbranch, router_t, router_f, dgain2, branch_squares
    )

    if len(steps) > 1:
        x_go = released(info, x_go, [misc, *dos])
    for step in steps[1:]:
        x_steps.append(both_ways(x_go if step == 2 else x_steps[-1], step, n_seq))
    dqkv, part = attend_back(heads, info, qkv_mine, misc, n1_list, dos, gated_steps[0])

    parts = swap(part.reshape(n_exp, D // n_exp, part.shape[1]), "exp")
    dqkv_own = [dqkv[0]] + [shifted(dqkv[step], -step, n_seq) for step in range(1, n_seq)]

    for i in range(1, len(x_steps)):
        gated_steps.append(gated(info, router, x_steps[i], g_steps[i], sum_steps[i], [dqkv[0]]))
    xs = [x_own_rows] + [x for step in x_steps for x in step]
    gs = [do_own] + [g for step in gated_steps for g in step]
    tiles = train_up.shape[2] // GRAD_TILE
    grad_parts = [(expert, (0, tiles)) for expert in range(local - 1)]
    grad_parts += [(local - 1, (first, tiles // 2)) for first in (0, tiles // 2)]
    totals = None

    def more_grads(wait, totals, through=()):
        expert, span = grad_parts.pop(0)
        return expert_grads_part(
            expert, span, info, xs, gs, train_up, train_down, totals, wait, through
        )

    totals, done = more_grads([dqkv[0]], totals)
    piece = sum_parts(info, parts, w_chunk, done)

    found = [shifted(piece, step, n_seq) for step in range(1, n_seq)]
    if len(grad_parts) > 1:
        totals, done = more_grads([piece], totals)
    found, again = join_blocks(info, [piece] + found, done)
    here = [lax.ppermute(found, "exp", [(i, i ^ m) for i in range(n_exp)]) for m in range(2, n_exp, 2)]
    input_grad = input_grad_rows(heads, info, x_own, gain1, dmid, w_parts, dqkv_own, done)
    while grad_parts:
        totals, (done, again) = more_grads([input_grad], totals, [again])
    here = jnp.stack([again] + here)
    there = lax.ppermute(here, "exp", [(i, i ^ 1) for i in range(n_exp)])
    up_total, down_total = totals
    qkv_total, out_total, router_total, dgain1, dgain2, stats = layout(
        heads, info, here, there, gain1
    )
    stat_roots = stats[0, EXPERTS + 1 : EXPERTS + 4]
    return (
        output[None],
        input_grad[None],
        dgain1,
        qkv_total,
        out_total,
        dgain2,
        router_total.T,
        up_total,
        down_total,
        stat_roots,
    )


def solution(mesh):
    return jax.shard_map(
        body,
        mesh=mesh,
        in_specs=(
            P("exp", "seq", None),
            P("exp", None),
            P("exp", "seq", None),
            P(),
            P(),
            P(),
            P(),
            P(),
            P("exp", None, None),
            P("exp", None, None),
            P("exp", None, None),
            P("exp", None, None),
            P("exp", "seq", None),
        ),
        out_specs=(
            P("exp", "seq", None),
            P("exp", "seq", None),
            P(),
            P(),
            P(),
            P(),
            P(),
            P("exp", None, None),
            P("exp", None, None),
            P(),
        ),
        check_vma=False,
    )
```

```python
import jax
import jax.numpy as jnp
from jax import lax
from jax.experimental import pallas as pl
from jax.experimental.pallas import tpu as pltpu
from jax.sharding import PartitionSpec as P

D = 768
HEADS = 12
HEAD = 64
EXPERTS = 32
FROZEN = 16
CAP = 48

EPS = 1e-06
MASKED = -1e30
BF = jnp.bfloat16
F32 = jnp.float32
TANH_A = 0.7978845608028654
TANH_B = 0.044715
GRAD_ROWS = 1536
GRAD_TILE = 512
MISC = 896
GAIN1_AT = 64
VMEM_BYTES = 56 * 1024 * 1024


def mm(a, b):
    return jnp.dot(a, b, preferred_element_type=F32)


def mm_nt(a, b):
    return lax.dot_general(a, b, (((1,), (1,)), ((), ())), preferred_element_type=F32)


def ein(form, a, b):
    return jnp.einsum(form, a, b, preferred_element_type=F32)


def mm_tn(a, b):
    return lax.dot_general(a, b, (((0,), (0,)), ((), ())), preferred_element_type=F32)


def params():
    return pltpu.CompilerParams(vmem_limit_bytes=VMEM_BYTES)


def cost(micros):
    return pl.CostEstimate(flops=int(micros * 1.1e9), bytes_accessed=0, transcendentals=0)


def whole(shape):
    return pl.BlockSpec(shape, lambda *unused: (0,) * len(shape))


def called(
    kernel,
    name,
    outs,
    info,
    operands,
    in_specs=None,
    scratch=(),
    micros=5,
    grid=(1,),
    out_specs=None,
    aliases=None,
    deps=(),
    through=(),
):
    specs = [None] * len(operands) if in_specs is None else in_specs
    specs = [whole(a.shape) if b is None else b for a, b in zip(operands, specs)]
    results = [whole(shape) for shape, unused in outs] if out_specs is None else list(out_specs)
    shapes = [jax.ShapeDtypeStruct(shape, kind) for shape, kind in outs]
    shapes += [jax.ShapeDtypeStruct(a.shape, a.dtype) for a in through]
    held = pl.BlockSpec(memory_space=pl.ANY)
    aliases = dict(aliases or {})
    for i in range(len(through)):
        aliases[1 + len(operands) + i] = len(outs) + i
    extra = len(through) + len(deps)

    def inner(info_ref, *refs):
        ins, rest = refs[: len(operands)], refs[len(operands) + extra :]
        kernel(info_ref, *ins, *rest[: len(outs)], *rest[len(outs) + len(through) :])

    call = pl.pallas_call(
        inner,
        out_shape=shapes,
        grid_spec=pltpu.PrefetchScalarGridSpec(
            num_scalar_prefetch=1,
            grid=grid,
            in_specs=specs + [held] * extra,
            out_specs=results + [held] * len(through),
            scratch_shapes=list(scratch),
        ),
        input_output_aliases=aliases,
        compiler_params=params(),
        cost_estimate=cost(micros),
        name=name,
    )
    return list(call(info, *operands, *through, *deps))


def released(info, arrays, deps):
    def kernel(info_ref, out_ref):
        out_ref[...] = jnp.zeros_like(out_ref)

    return called(kernel, "released", [((8, 128), F32)], info, [], micros=1, deps=deps, through=arrays)[1:]


INFO = 2


def doc_start(info_ref, position):
    bound = 0
    start = jnp.zeros_like(position)
    for i in range(INFO, info_ref.shape[0]):
        bound = bound + info_ref[i]
        start = jnp.where(position >= bound, bound, start)
    return start


def doc_end(info_ref):
    bound = 0
    for i in range(INFO, info_ref.shape[0]):
        bound = bound + info_ref[i]
    return bound


def need_mask(info_ref, key_start, last_query):
    return doc_start(info_ref, jnp.full((1, 128), last_query, jnp.int32))[0, 0] > key_start


def route_kernel(local, info_ref, routes_ref, g_ref, pick_ref, train_ref, frozen_ref):
    tok = g_ref.shape[0]
    half = pick_ref.shape[0] // 2
    first, second = routes_ref[0:1, :], routes_ref[1:2, :]
    row = lax.broadcasted_iota(jnp.int32, (EXPERTS, tok), 0)
    expert = jnp.where(row < FROZEN, row + FROZEN, row - FROZEN)
    position = info_ref[0] * tok + lax.broadcasted_iota(jnp.int32, (EXPERTS, tok), 1)
    live = ((expert == first) | (expert == second)) & (position < doc_end(info_ref))
    earlier = lax.broadcasted_iota(jnp.int32, (tok, tok), 0) < lax.broadcasted_iota(
        jnp.int32, (tok, tok), 1
    )
    place = mm(jnp.where(live, 1.0, 0.0).astype(BF), jnp.where(earlier, 1.0, 0.0).astype(BF))
    place = jnp.where(live, place, -1.0)
    slot = lax.broadcasted_iota(jnp.int32, (CAP, tok), 0).astype(F32)
    sums = jnp.broadcast_to((first + second).astype(F32), (16, tok)).astype(BF)
    sum_row = lax.broadcasted_iota(jnp.int32, (16, CAP), 0)
    for part, out_ref in ((0, train_ref), (1, frozen_ref)):
        for d in range(FROZEN // local):
            found = jnp.zeros((16, CAP), F32)
            for i in range(local):
                e = part * FROZEN + d * local + i
                taken = jnp.where(place[e : e + 1, :] == slot, 1.0, 0.0).astype(BF)
                pick_ref[e * CAP : (e + 1) * CAP, :] = taken
                found = jnp.where(sum_row == i, mm_nt(sums, taken), found)
            out_ref[d, local * CAP :, :] = jnp.zeros((16, D), BF)
            out_ref[d, local * CAP :, 0:CAP] = found.astype(BF)
        rows = mm(pick_ref[part * half : (part + 1) * half, :], g_ref[...]).astype(BF)
        for d in range(FROZEN // local):
            out_ref[d, : local * CAP, :] = rows[d * local * CAP : (d + 1) * local * CAP, :]


def route(info, local, routes, g):
    tok = g.shape[0]
    sent = (FROZEN // local, local * CAP + 16, D)

    def kernel(*refs):
        route_kernel(local, *refs)

    return called(
        kernel,
        "route",
        [((EXPERTS * CAP, tok), BF), (sent, BF), (sent, BF)],
        info,
        [routes, g],
        micros=6,
    )


def slot_sums(tile, local_id):
    parts = []
    for i in range(tile.shape[0]):
        turned = tile[i].astype(F32).T
        lane = lax.broadcasted_iota(jnp.int32, turned.shape, 1)
        column = jnp.sum(jnp.where(lane == local_id, turned, 0.0), axis=1, keepdims=True)
        parts.append(column[:CAP, :])
    return jnp.concatenate(parts, axis=0)


def gelu_parts(h):
    h2 = h * h
    t = jnp.tanh(h * (TANH_A + (TANH_A * TANH_B) * h2))
    half = 0.5 * t + 0.5
    act = h * half
    slope = half + act * (1.0 - half) * (2.0 * TANH_A + (6.0 * TANH_A * TANH_B) * h2)
    return act, slope


def attend_kernel(step, last, info_ref, x_ref, gain_ref, w_q_ref, w_k_ref, w_v_ref, *refs):
    first = step == 0
    refs = list(refs)
    if first:
        n1_ref, q_ref = refs[:2]
        refs = refs[2:]
    else:
        q_ref, m_in, l_in, acc_in, n1_ref = refs[:5]
        refs = refs[5:]
    if last:
        attn_ref = refs.pop(0)
        l_ref = refs.pop(0)
        m_ref, acc_ref, k_all, v_all = refs
    else:
        m_ref, l_ref, acc_ref, k_all, v_all = refs
    block = info_ref[0] - step
    rows = x_ref.shape[0]
    pairs = k_all.shape[0]

    x = x_ref[...].astype(F32)
    n1 = x * lax.rsqrt(jnp.mean(x * x, axis=1, keepdims=True) + EPS) * gain_ref[...]
    n1_ref[...] = n1.astype(BF)

    def project():
        n1 = n1_ref[...]
        for i in range(pairs // 2):
            cols = slice(i * 4 * HEAD, (i + 1) * 4 * HEAD)
            k = mm(n1, w_k_ref[:, cols]).astype(BF)
            v = mm(n1, w_v_ref[:, cols]).T.astype(BF)
            for j in range(2):
                k_all[2 * i + j] = k[:, j * 2 * HEAD : (j + 1) * 2 * HEAD]
                v_all[2 * i + j] = v[j * 2 * HEAD : (j + 1) * 2 * HEAD, :]
            if first:
                q = mm(n1, w_q_ref[:, cols]).astype(BF) * jnp.asarray(HEAD**-0.5, BF)
                for j in range(2):
                    q_ref[2 * i + j] = q[:, j * 2 * HEAD : (j + 1) * 2 * HEAD]

    def attend(masked):
        key_pos = block * rows + lax.broadcasted_iota(jnp.int32, (rows, rows), 0)
        query_pos = info_ref[0] * rows + lax.broadcasted_iota(jnp.int32, (1, rows), 1)
        start = doc_start(info_ref, query_pos)

        def pair(p, carry):
            q = q_ref[p]
            k = k_all[p]
            lane = lax.broadcasted_iota(jnp.int32, q.shape, 1)
            zero = jnp.zeros_like(q)
            found = [
                mm_nt(k, jnp.where(lane < HEAD, q, zero)),
                mm_nt(k, jnp.where(lane < HEAD, zero, q)),
            ]
            for half in range(2):
                scores = found[half]
                if masked:
                    allowed = key_pos >= start
                    if first:
                        allowed = allowed & (key_pos <= query_pos)
                    scores = jnp.where(allowed, scores, MASKED)
                top = jnp.max(scores, axis=0, keepdims=True)
                if not first:
                    old = m_in[p, half : half + 1, :]
                    top = jnp.maximum(top, old)
                probs = jnp.exp(scores - top)
                total = jnp.sum(probs, axis=0, keepdims=True)
                value = mm(v_all[p, half * HEAD : (half + 1) * HEAD, :], probs.astype(BF))
                part = pl.ds(pl.multiple_of(p * 2 * HEAD + half * HEAD, HEAD), HEAD)
                if not first:
                    decay = jnp.exp(old - top)
                    total = total + l_in[p, half : half + 1, :] * decay
                    value = value + acc_in[part, :] * decay
                m_ref[p, half : half + 1, :] = top
                l_ref[p, half : half + 1, :] = total
                acc_ref[part, :] = value
            return carry

        lax.fori_loop(0, pairs, pair, 0)

    if first:
        project()
        attend(True)
    else:
        masked = need_mask(info_ref, block * rows, info_ref[0] * rows + rows - 1)

        @pl.when(block >= 0)
        def _():
            project()

        @pl.when((block >= 0) & masked)
        def _():
            attend(True)

        @pl.when((block >= 0) & jnp.logical_not(masked))
        def _():
            attend(False)

        @pl.when(block < 0)
        def _():
            m_ref[...] = m_in[...]
            l_ref[...] = l_in[...]
            acc_ref[...] = acc_in[...]

    if last:
        for p in range(pairs):
            for half in range(2):
                part = slice((2 * p + half) * HEAD, (2 * p + half + 1) * HEAD)
                total = l_ref[p, half : half + 1, :]
                acc_ref[part, :] = acc_ref[part, :] / total
                l_ref[p, half : half + 1, :] = m_ref[p, half : half + 1, :] + jnp.log(total)
            part = slice(p * 2 * HEAD, (p + 1) * 2 * HEAD)
            attn_ref[:, part] = acc_ref[part, :].T.astype(BF)


def attend_step(step, last, info, x, gain, w, state, deps=(), through=()):
    tok = x.shape[0]
    pairs = HEADS // 2
    stat, acc = ((pairs, 2, tok), F32), ((D, tok), F32)
    row, by_pair = ((tok, D), BF), ((pairs, tok, 2 * HEAD), BF)
    outs = [row] + ([by_pair] if step == 0 else []) + ([row, stat] if last else [stat, stat, acc])
    scratch = [pltpu.VMEM(*by_pair), pltpu.VMEM((pairs, 2 * HEAD, tok), BF)]
    if last:
        scratch = [pltpu.VMEM(*stat), pltpu.VMEM(*acc)] + scratch

    def kernel(*refs):
        attend_kernel(step, last, *refs)

    square = (D, D)
    return called(
        kernel,
        "attend_step",
        outs,
        info,
        [x, gain, w, w, w, *state],
        [
            None,
            None,
            pl.BlockSpec(square, lambda i, r: (0, 0)),
            pl.BlockSpec(square, lambda i, r: (0, 1)),
            pl.BlockSpec(square, lambda i, r: (0, 2)),
        ]
        + [None] * len(state),
        scratch,
        micros=13,
        deps=deps,
        through=through,
    )


def attend_back_kernel(blocks, heads, info_ref, qkv_ref, misc_ref, *refs):
    n1_refs, do_refs, out_refs = [refs[i * blocks : (i + 1) * blocks] for i in range(3)]
    part_ref, dq_ref, dk_ref, dv_ref, k_mine, v_mine, k_t, do_all, lse_all, delta_all, out_all = refs[
        3 * blocks :
    ]
    rows = qkv_ref.shape[0] // blocks
    tiles, deep, width = do_refs[0].shape
    lane = lax.broadcasted_iota(jnp.int32, (rows, 2 * HEAD), 1)
    dq_ref[...] = jnp.zeros_like(dq_ref)

    def turn(b):
        return lax.rem(info_ref[0] - b + blocks, blocks)

    for b in range(blocks):
        do_all[b] = do_refs[b][:, :width, :].reshape(rows, width)
        stats = [do_refs[b][t, width:, :].astype(F32) for t in range(tiles)]
        stats = jnp.concatenate(stats, axis=1)
        delta_all[b] = stats[:heads] + stats[heads : 2 * heads]
        lse_all[b] = stats[2 * heads : 3 * heads] + stats[3 * heads : 4 * heads]

    def key_step(kb, carry):
        kt = turn(kb)
        key_rows = pl.ds(pl.multiple_of(kt * rows, rows), rows)
        for h in range(heads):
            first = (h // 2) * 2 * HEAD
            k = qkv_ref[key_rows, width + first : width + first + 2 * HEAD]
            v = qkv_ref[key_rows, 2 * width + first : 2 * width + first + 2 * HEAD]
            mine = (lane < HEAD) if h % 2 == 0 else (lane >= HEAD)
            zero = jnp.zeros_like(k)
            k_mine[h] = jnp.where(mine, k, zero)
            v_mine[h] = jnp.where(mine, v, zero)
            k_t[h] = k.T[(h % 2) * HEAD : (h % 2 + 1) * HEAD, :]
        dk_ref[...] = jnp.zeros_like(dk_ref)
        dv_ref[...] = jnp.zeros_like(dv_ref)

        def pair(qb, diagonal, masked):
            qt = turn(qb)
            query_rows = pl.ds(pl.multiple_of(qt * rows, rows), rows)
            if masked:
                key_pos = kb * rows + lax.broadcasted_iota(jnp.int32, (rows, rows), 0)
                query_pos = qb * rows + lax.broadcasted_iota(jnp.int32, (1, rows), 1)
                allowed = key_pos >= doc_start(info_ref, query_pos)
                if diagonal:
                    allowed = allowed & (key_pos <= query_pos)

            def of_head(h):
                cols = slice((h // 2) * 2 * HEAD, (h // 2 + 1) * 2 * HEAD)
                return qkv_ref[query_rows, cols], do_all[qt, :, cols]

            def products(h):
                q, do = of_head(h)
                return mm_nt(k_mine[h], q), mm_nt(v_mine[h], do)

            later = products(0)
            for h in range(heads):
                scores, dprobs = later
                if h + 1 < heads:
                    later = products(h + 1)
                q, do = of_head(h)
                probs = jnp.exp(scores - lse_all[qt, h : h + 1, :])
                if masked:
                    probs = jnp.where(allowed, probs, 0.0)
                dscores = (probs * (dprobs - delta_all[qt, h : h + 1, :])).astype(BF)
                dv_ref[h] += mm(probs.astype(BF), do)
                dk_ref[h] += mm(dscores, q)
                dq_ref[qt, h] += mm(k_t[h], dscores)

        pair(kb, True, True)

        def query_step(qb, carry):
            masked = need_mask(info_ref, kb * rows, qb * rows + rows - 1)

            @pl.when(masked)
            def _():
                pair(qb, False, True)

            @pl.when(jnp.logical_not(masked))
            def _():
                pair(qb, False, False)

            return carry

        lax.fori_loop(kb + 1, blocks, query_step, 0)
        for h in range(heads):
            part = slice((h % 2) * HEAD, (h % 2 + 1) * HEAD)
            for i, grad_ref in ((1, dk_ref), (2, dv_ref)):
                at = (i * heads + h) * HEAD
                out_all[kt, at : at + HEAD, :] = grad_ref[h].T[part, :].astype(BF)
        return carry

    lax.fori_loop(0, blocks, key_step, 0)
    total = 0.0
    for b in range(blocks):
        for h in range(heads):
            out_all[b, h * HEAD : (h + 1) * HEAD, :] = (dq_ref[b, h] * HEAD**-0.5).astype(BF)
        grads = out_all[b]
        out_refs[b][...] = grads
        total = total + mm(grads, n1_refs[b][...])
    part_ref[:, :MISC] = misc_ref[...]
    part_ref[:, MISC:] = total.T.astype(BF)


def attend_back(heads, info, qkv, misc, n1, dos, deps):
    rows = qkv.shape[0]
    blocks = len(dos)
    tiles, deep, width = dos[0].shape
    tok = rows // blocks
    cols = 3 * heads * HEAD

    def kernel(*refs):
        attend_back_kernel(blocks, heads, *refs)

    *grads, part = called(
        kernel,
        "attend_back",
        [((cols, tok), BF)] * blocks + [((D, MISC + cols), BF)],
        info,
        [qkv, misc, *n1, *dos],
        scratch=[
            pltpu.VMEM((blocks, heads, HEAD, tok), F32),
            pltpu.VMEM((heads, tok, 2 * HEAD), F32),
            pltpu.VMEM((heads, tok, 2 * HEAD), F32),
            pltpu.VMEM((heads, tok, 2 * HEAD), BF),
            pltpu.VMEM((heads, tok, 2 * HEAD), BF),
            pltpu.VMEM((heads, HEAD, tok), BF),
            pltpu.VMEM((blocks, tok, width), BF),
            pltpu.VMEM((blocks, heads, tok), F32),
            pltpu.VMEM((blocks, heads, tok), F32),
            pltpu.VMEM((blocks, cols, tok), BF),
        ],
        micros=32,
        deps=deps,
    )
    return grads, part


def project_back_kernel(blocks, info_ref, w_ref, *refs):
    out_ref = refs[blocks]
    rows = refs[0].shape[0]
    for b in range(blocks):
        out_ref[b * rows : (b + 1) * rows, :] = mm_nt(refs[b][...], w_ref[...]).astype(BF)


def project_back(info, w, n1, deps):
    blocks = len(n1)

    def kernel(*refs):
        project_back_kernel(blocks, *refs)

    shape = (blocks * n1[0].shape[0], w.shape[0])
    return called(kernel, "project_back", [(shape, BF)], info, [w, *n1], micros=7, deps=deps)[0]


def slot_gate(own, sums, x, router):
    lane = lax.broadcasted_iota(jnp.int32, (x.shape[0], router.shape[1]), 1)
    other = sums.astype(jnp.int32) - own
    signs = jnp.where(lane == own, 1.0, 0.0) - jnp.where(lane == other, 1.0, 0.0)
    margin = jnp.sum(mm(x, router) * signs, axis=1, keepdims=True)
    return 1.0 / (1.0 + jnp.exp(-margin)), signs


def expert_kernel(
    first_id, info_ref, x_ref, g_ref, sums_ref, router_ref, up_ref, down_ref, drouter_ref, *refs
):
    backs, handed = (refs[:1], refs[1:-6]) if len(refs) == 10 else (refs[:2], ())
    xs, dos, gate_ref, signs_ref, eacc, dacc = refs[-6:]
    expert = pl.program_id(0)
    step = pl.program_id(1)
    rows = xs.shape[0]
    block = x_ref.shape

    @pl.when(step == 0)
    def _():
        x = x_ref[...].reshape(rows, D)
        xs[...] = x
        own = first_id + info_ref[1] * pl.num_programs(0) + expert
        gate, signs = slot_gate(own, slot_sums(sums_ref, expert), x, router_ref[...])
        gate_ref[...] = gate
        signs_ref[...] = signs
        do = (gate * g_ref[...].reshape(rows, D).astype(F32)).astype(BF)
        dos[...] = do
        if handed:
            handed[0][...] = do.reshape(block)
            for x_out in handed[1:]:
                x_out[...] = x.reshape(block)

    act, slope = gelu_parts(mm(xs[...], up_ref[0]))
    dhid = (mm_nt(dos[...], down_ref[0]) * slope).astype(BF)
    out = mm(act.astype(BF), down_ref[0])
    dx = mm_nt(dhid, up_ref[0])

    @pl.when(step == 0)
    def _():
        eacc[...] = out
        dacc[...] = dx

    @pl.when(step > 0)
    def _():
        eacc[...] += out
        dacc[...] += dx

    @pl.when(step == pl.num_programs(1) - 1)
    def _():
        out = eacc[...]
        gate = gate_ref[...]
        g = g_ref[...].reshape(rows, D).astype(F32)
        mix = (gate * out).astype(BF).reshape(block)
        dgate = jnp.sum(g * out, axis=1, keepdims=True)
        dlogits = (gate * (1.0 - gate) * dgate * signs_ref[...]).astype(BF)
        dx = dacc[...] + mm_nt(dlogits, router_ref[...])
        dx = dx.astype(BF).reshape(block)
        if handed:
            backs[0][:, 0] = dx
            backs[0][:, 1] = mix
        else:
            backs[0][...] = dx
            backs[1][...] = mix
        drouter = mm_tn(dlogits, xs[...])

        @pl.when(expert == 0)
        def _():
            drouter_ref[...] = drouter

        @pl.when(expert > 0)
        def _():
            drouter_ref[...] += drouter


def expert_rows(first_id, info, x, g, router, up, down, handing, deps, through=()):
    sources, experts = x.shape[:2]
    rows = sources * CAP
    hidden = up.shape[2]
    tile = 1536
    row_spec = pl.BlockSpec((sources, 1, CAP, D), lambda e, f, r: (0, e, 0, 0))


    def kernel(*refs):
        expert_kernel(first_id, *refs)

    outs, out_specs = [((router.shape[1], D), F32)], [whole((router.shape[1], D))]
    if handing:
        outs += [((sources, 2) + x.shape[1:], BF)]
        out_specs += [pl.BlockSpec((sources, 2, 1, CAP, D), lambda e, f, r: (0, 0, e, 0, 0))]
    else:
        outs += [(x.shape, BF), (x.shape, BF)]
        out_specs += [row_spec, row_spec]
    if handing:
        outs += [(x.shape, BF)] * 3
        out_specs += [row_spec] * 3

    return called(
        kernel,
        "expert_rows",
        outs,
        info,
        [x, g, g, router, up, down],
        [
            row_spec,
            pl.BlockSpec((sources, CAP, D), lambda e, f, r: (0, e, 0)),
            pl.BlockSpec((sources, 16, 128), lambda e, f, r: (0, experts * CAP // 16, 0)),
            None,
            pl.BlockSpec((1, D, tile), lambda e, f, r: (e, 0, f)),
            pl.BlockSpec((1, tile, D), lambda e, f, r: (e, f, 0)),
        ],
        [
            pltpu.VMEM((rows, D), BF),
            pltpu.VMEM((rows, D), BF),
            pltpu.VMEM((rows, 1), F32),
            pltpu.VMEM((rows, 128), F32),
            pltpu.VMEM((rows, D), F32),
            pltpu.VMEM((rows, D), F32),
        ],
        micros=23,
        grid=(experts, hidden // tile),
        out_specs=out_specs,
        deps=deps,
        through=through,
    )


def gated_kernel(count, info_ref, router_ref, *refs):
    x_refs, g_refs, sum_refs, out_refs = [refs[i * count : (i + 1) * count] for i in range(4)]
    for i, again_ref in enumerate(refs[4 * count :]):
        again_ref[...] = x_refs[i][...]
    sources, experts = x_refs[0].shape[:2]
    for b in range(count):
        for e in range(experts):
            own = FROZEN + info_ref[1] * experts + e
            x = x_refs[b][:, e].reshape(sources * CAP, D)
            gate, unused = slot_gate(own, slot_sums(sum_refs[b], e), x, router_ref[...])
            g = g_refs[b][:, e * CAP : (e + 1) * CAP, :].reshape(sources * CAP, D).astype(F32)
            out_refs[b][:, e] = (gate * g).astype(BF).reshape(sources, CAP, D)


def gated(info, router, xs, gs, sums, deps=(), again=0):
    count = len(xs)

    def kernel(*refs):
        gated_kernel(count, *refs)

    return called(
        kernel,
        "gated",
        [(x.shape, BF) for x in [*xs, *xs[:again]]],
        info,
        [router, *xs, *gs, *sums],
        micros=1,
        deps=deps,
    )


def expert_grad_kernel(group, add, info_ref, ins, dup_ref, ddown_ref, done_ref, xs, dos):
    up_ref, down_ref = ins[:2]
    x_refs, do_refs = ins[2 : 2 + group], ins[2 + group : 2 + 2 * group]
    rows = xs.shape[0] // group

    @pl.when(pl.program_id(0) == 0)
    def _():
        done_ref[...] = jnp.zeros_like(done_ref)
        for b in range(group):
            part = slice(b * rows, (b + 1) * rows)
            xs[part, :] = x_refs[b][...].reshape(rows, D)
            dos[part, :] = do_refs[b][...].reshape(rows, D)

    act, slope = gelu_parts(mm(xs[...], up_ref[0]))
    dhid = (mm_nt(dos[...], down_ref[0]) * slope).astype(BF)
    ddown = mm_tn(act.astype(BF), dos[...])
    dup = mm_tn(xs[...], dhid)
    if add:
        ddown = ddown + ins[-1][0]
        dup = dup + ins[-2][0]
    ddown_ref[0] = ddown
    dup_ref[0] = dup


def expert_grads(expert, span, first, group, info, xs, dos, up, down, totals, deps, through):
    sources, experts = dos[0].shape[:2]
    rows = group * sources * CAP
    tile = GRAD_TILE
    start, count = span
    add = first > 0
    up_spec = pl.BlockSpec((1, D, tile), lambda f, r: (expert, 0, start + f))
    down_spec = pl.BlockSpec((1, tile, D), lambda f, r: (expert, start + f, 0))
    in_specs = [up_spec, down_spec]
    in_specs += [pl.BlockSpec((sources, 1, CAP, D), lambda f, r: (0, expert, 0, 0))] * (2 * group)
    part = slice(first, first + group)
    operands = [up, down, *xs[part], *dos[part]]
    aliases = {}
    if totals is not None:
        aliases = {1 + len(operands): 0, 2 + len(operands): 1}
        in_specs += [up_spec, down_spec] if add else [pl.BlockSpec(memory_space=pl.ANY)] * 2
        operands += list(totals)

    def kernel(info_ref, *refs):
        ins, rest = refs[: len(operands)], refs[len(operands) :]
        expert_grad_kernel(group, add, info_ref, ins, *rest)

    return called(
        kernel,
        "expert_grads",
        [(up.shape, F32), (down.shape, F32), ((8, 128), F32)],
        info,
        operands,
        in_specs,
        [pltpu.VMEM((rows, D), BF), pltpu.VMEM((rows, D), BF)],
        micros=9 * count,
        grid=(count,),
        out_specs=[up_spec, down_spec, whole((8, 128))],
        aliases=aliases,
        deps=deps,
        through=through,
    )


def expert_grads_part(expert, span, info, xs, dos, up, down, totals, deps, through):
    blocks = len(xs)
    group = max(1, min(blocks, GRAD_ROWS // (dos[0].shape[0] * CAP)))
    for first in range(0, blocks, group):
        dup, ddown, done, *through = expert_grads(
            expert, span, first, group, info, xs, dos, up, down, totals, deps, through
        )
        totals = [dup, ddown]
    return totals, [done, *through]


def token_forward_kernel(
    info_ref, attn_ref, x_ref, gain_ref, w_ref, pick_ref, mid_ref, square_ref, train_ref, frozen_ref
):
    tok = x_ref.shape[0]
    half = pick_ref.shape[0] // 2
    branch = mm(attn_ref[...], w_ref[...])
    mid = x_ref[...].astype(F32) + branch
    mid_ref[...] = mid
    r = lax.rsqrt(jnp.mean(mid * mid, axis=1, keepdims=True) + EPS)
    n2 = (mid * r * gain_ref[...]).astype(BF)
    train_ref[...] = mm(pick_ref[:half, :], n2).astype(BF)
    frozen_ref[...] = mm(pick_ref[half:, :], n2).astype(BF)
    position = info_ref[0] * tok + lax.broadcasted_iota(jnp.int32, (tok, D), 0)
    square = jnp.where(position < doc_end(info_ref), branch * branch, 0.0)
    square_ref[...] = jnp.sum(square, axis=0, keepdims=True)


def token_forward(info, attn, x, gain, w, pick):
    tok = x.shape[0]
    half = ((pick.shape[0] // 2, D), BF)
    return called(
        token_forward_kernel,
        "token_forward",
        [((tok, D), F32), ((1, D), F32), half, half],
        info,
        [attn, x, gain, w, pick],
        [None] * 5,
        micros=6,
    )


def token_back_kernel(
    heads,
    groups,
    info_ref,
    pick_ref,
    dx_t_ref,
    dx_f_ref,
    mid_ref,
    g_ref,
    gain_ref,
    w_ref,
    wg_ref,
    attn_ref,
    lse_ref,
    head_ref,
    *refs,
):
    send_refs = refs[:groups]
    dmid_ref, dbranch_ref, dgain_ref = refs[groups:]
    tiles, deep, width = send_refs[0].shape
    tok = mid_ref.shape[0]
    half = pick_ref.shape[0] // 2

    dn2 = mm_tn(pick_ref[:half, :], dx_t_ref[...].reshape(half, D))
    dn2 = dn2 + mm_tn(pick_ref[half:, :], dx_f_ref[...].reshape(half, D))
    mid = mid_ref[...]
    r = lax.rsqrt(jnp.mean(mid * mid, axis=1, keepdims=True) + EPS)
    u = mid * r
    dgain_ref[...] = jnp.sum(dn2 * u, axis=0, keepdims=True)
    scaled = dn2 * gain_ref[...]
    dmid = g_ref[...].astype(F32) + r * (scaled - u * jnp.mean(scaled * u, axis=1, keepdims=True))
    dmid_ref[...] = dmid
    dbranch = dmid.astype(BF)
    dbranch_ref[...] = dbranch

    dattn = mm_nt(dbranch, w_ref[...]).astype(BF).astype(F32)
    prod = dattn * attn_ref[...].astype(F32)
    high = prod.astype(BF)
    low = (prod - high.astype(F32)).astype(BF)
    for turn in range(groups):
        g = lax.rem(info_ref[0] + turn, groups)
        sent = mm_nt(dbranch, wg_ref[g]).astype(BF)
        delta = mm_nt(head_ref[g], high) + mm_nt(head_ref[g], low)
        parts = []
        for stat in (delta[:heads], lse_ref[g][:heads]):
            high_part = stat.astype(BF).astype(F32)
            parts += [high_part, stat - high_part]
        blank = jnp.zeros((16 - 4 * heads, tok), F32)
        stats = jnp.concatenate(parts + [blank], axis=0).astype(BF)
        for t in range(tiles):
            part = slice(t * width, (t + 1) * width)
            send_refs[turn][t, :width, :] = sent[part, :]
            send_refs[turn][t, width:, :] = stats[:, part]


def token_back(
    heads, groups, width, info, pick, dx_t, dx_f, mid, g, gain, w, w_groups, attn, lse, head_rows, deps, through
):
    tok = mid.shape[0]
    tiles = tok // width

    def kernel(*refs):
        token_back_kernel(heads, groups, *refs)

    outs = [((tiles, width + 16, width), BF)] * groups
    operands = [pick, dx_t, dx_f, mid, g, gain, w, w_groups, attn, lse, head_rows]
    half = (dx_f.shape[0], 1) + dx_f.shape[1:]
    found = called(
        kernel,
        "token_back",
        outs + [((tok, D), F32), ((tok, D), BF), ((1, D), F32)],
        info,
        operands,
        [None, pl.BlockSpec(half, lambda i, r: (0, 0, 0, 0, 0))] + [None] * (len(operands) - 2),
        micros=10,
        deps=deps,
        through=through,
    )
    return [found[:groups]] + found[groups:]


def token_mix_kernel(
    info_ref, pick_ref, mix_t_ref, mix_f_ref, mid_ref, x_ref, attn_ref, dbranch_ref, rt_ref, rf_ref, dgain_ref, square_ref, out_ref, misc_ref
):
    tok = mid_ref.shape[0]
    half = pick_ref.shape[0] // 2
    mix = mm_tn(pick_ref[:half, :], mix_t_ref[...].reshape(half, D))
    mix = mix + mm_tn(pick_ref[half:, :], mix_f_ref[...].reshape(half, D))
    out_ref[...] = (mid_ref[...] + mix).astype(BF)
    valid = info_ref[0] * tok + lax.broadcasted_iota(jnp.int32, (tok, D), 0) < doc_end(info_ref)
    x = x_ref[...].astype(F32)
    stats = [
        jnp.sum(jnp.where(valid, x * x, 0.0)),
        jnp.sum(square_ref[...]),
        jnp.sum(jnp.where(valid, mix * mix, 0.0)),
        jnp.clip(doc_end(info_ref) - info_ref[0] * tok, 0, tok).astype(F32),
    ]
    misc_ref[:, :D] = mm_tn(attn_ref[...], dbranch_ref[...]).astype(BF)
    tail = (rt_ref[...] + rf_ref[...]).T
    gains = jnp.broadcast_to(dgain_ref[...], (8, D)).T[:, 0:1]
    row = lax.broadcasted_iota(jnp.int32, tail.shape, 0)
    lane = lax.broadcasted_iota(jnp.int32, tail.shape, 1)
    tail = jnp.where(lane < EXPERTS, tail, 0.0) + jnp.where(lane == EXPERTS, gains, 0.0)
    for i, stat in enumerate(stats):
        tail = tail + jnp.where((lane == EXPERTS + 1 + i) & (row == 0), stat, 0.0)
    misc_ref[:, D : D + 128] = tail.astype(BF)


def token_mix(info, pick, back_t, mix_f, mid, x, attn, dbranch, router_t, router_f, dgain, square):
    tok = mid.shape[0]
    operands = [pick, back_t, mix_f, mid, x, attn, dbranch, router_t, router_f, dgain, square]
    half = (mix_f.shape[0], 1) + mix_f.shape[1:]
    return called(
        token_mix_kernel,
        "token_mix",
        [((tok, D), BF), ((D, MISC), BF)],
        info,
        operands,
        [None, pl.BlockSpec(half, lambda i, r: (0, 1, 0, 0, 0))] + [None] * (len(operands) - 2),
        micros=1,
    )


def input_grad_kernel(heads, blocks, info_ref, x_ref, gain_ref, dmid_ref, w_ref, *refs):
    grad_refs, out_ref = refs[:blocks], refs[blocks]
    wide = heads * HEAD
    dn1 = 0.0
    for turn in range(blocks):
        g = lax.rem(info_ref[0] + turn, blocks)
        for c in range(3):
            rows = pl.ds(pl.multiple_of(c * blocks * wide + g * wide, HEAD), wide)
            part = grad_refs[turn][c * wide : (c + 1) * wide, :]
            dn1 = dn1 + mm_tn(part, w_ref[rows, :])
    x = x_ref[...].astype(F32)
    r = lax.rsqrt(jnp.mean(x * x, axis=1, keepdims=True) + EPS)
    u = x * r
    scaled = dn1 * gain_ref[...]
    dx = r * (scaled - u * jnp.mean(scaled * u, axis=1, keepdims=True))
    out_ref[...] = (dmid_ref[...] + dx).astype(BF)


def input_grad_rows(heads, info, x, gain, dmid, w_t, grads, deps):
    blocks = len(grads)

    def kernel(*refs):
        input_grad_kernel(heads, blocks, *refs)

    operands = [x, gain, dmid, w_t, *grads]
    return called(
        kernel, "input_grad", [(x.shape, BF)], info, operands, micros=8, deps=deps
    )[0]


def sum_kernel(info_ref, a_ref, w_ref, out_ref):
    total = a_ref[0].astype(F32)
    for i in range(1, a_ref.shape[0]):
        total = total + a_ref[i].astype(F32)
    out_ref[...] = total.astype(BF)
    gain = jnp.sum(total[:, MISC:] * w_ref[...].astype(F32), axis=1, keepdims=True)
    lane = lax.broadcasted_iota(jnp.int32, (total.shape[0], 128), 1)
    out_ref[:, D:MISC] = jnp.where(lane == GAIN1_AT, gain, total[:, D:MISC]).astype(BF)


def sum_parts(info, a, w, deps):
    return called(sum_kernel, "sum_parts", [(a.shape[1:], BF)], info, [a, w], micros=3, deps=deps)[0]


def join_kernel(info_ref, *refs):
    found, out_ref, again_ref = refs[:-2], refs[-2], refs[-1]
    total = found[0][:, :MISC].astype(F32)
    for ref in found[1:]:
        total = total + ref[:, :MISC].astype(F32)
    out_ref[:, :MISC] = total.astype(BF)
    cols = found[0].shape[1] - MISC
    for i, ref in enumerate(found):
        out_ref[:, MISC + i * cols : MISC + (i + 1) * cols] = ref[:, MISC:]
    again_ref[...] = out_ref[...]


def join_blocks(info, found, deps):
    rows, cols = found[0].shape
    shape = (rows, MISC + len(found) * (cols - MISC))
    return called(
        join_kernel, "join_blocks", [(shape, BF)] * 2, info, list(found), micros=3, deps=deps
    )


def layout_kernel(heads, info_ref, here_ref, there_ref, gain_ref, qkv_ref, out_ref, router_ref, gain1_ref, gain2_ref, stat_ref, tails):
    step = pl.program_id(0)
    rows = here_ref.shape[1]
    wide = heads * HEAD
    groups = (here_ref.shape[2] - MISC) // (3 * wide)

    def lay(part, piece):
        out_ref[part, :] = piece[:, :D].astype(F32)
        tail = piece[:, D:MISC].astype(F32)
        for turn in range(groups):
            g = lax.rem(info_ref[0] - turn + groups, groups)
            for c in range(3):
                at = MISC + (3 * turn + c) * wide
                grad = piece[:, at : at + wide].astype(F32)
                for g_now in range(groups):
                    cols = min(wide, D - g_now * wide)
                    to = c * D + g_now * wide
                    if cols > 0:

                        @pl.when(g == g_now)
                        def _():
                            qkv_ref[part, to : to + cols] = grad[:, :cols]

        return tail

    mine = lax.rem(info_ref[1], 2)
    for core in range(2):
        part = slice(core * rows, (core + 1) * rows)
        at = pl.ds(pl.multiple_of((2 * step + core) * rows, rows), rows)

        @pl.when(mine == core)
        def _():
            tails[at, :] = lay(part, here_ref[0])

        @pl.when(mine != core)
        def _():
            tails[at, :] = lay(part, there_ref[0])

    @pl.when(step == pl.num_programs(0) - 1)
    def _():
        turned = tails[...].T
        gain1_ref[...] = turned[GAIN1_AT] / gain_ref[0]
        gain2_ref[...] = turned[EXPERTS]
        router_ref[...] = turned[:EXPERTS]
        stats = tails[0:8, :]
        lane = lax.broadcasted_iota(jnp.int32, stats.shape, 1)
        count = jnp.sum(jnp.where(lane == EXPERTS + 4, stats, 0.0), axis=1, keepdims=True)
        used = (lane > EXPERTS) & (lane < EXPERTS + 4)
        stat_ref[...] = jnp.sqrt(jnp.where(used, stats, 0.0) / (jnp.maximum(count, 1.0) * D))


def layout(heads, info, here, there, gain):
    chips, rows, width = here.shape

    def kernel(*refs):
        layout_kernel(heads, *refs)

    piece_spec = pl.BlockSpec((1, rows, width), lambda e, r: (e ^ (r[1] // 2), 0, 0))

    def row_spec(cols):
        return pl.BlockSpec((2 * rows, cols), lambda e, r: (e, 0))

    return called(
        kernel,
        "layout",
        [((D, 3 * D), F32), ((D, D), F32), ((EXPERTS, D), F32), ((D,), F32), ((D,), F32), ((8, 128), F32)],
        info,
        [here, there, gain],
        [piece_spec, piece_spec, None],
        [pltpu.VMEM((D, 128), F32)],
        micros=12,
        grid=(chips,),
        out_specs=[row_spec(3 * D), row_spec(D), whole((EXPERTS, D)), whole((D,)), whole((D,)), whole((8, 128))],
    )


def shifted(x, by, count):
    return lax.ppermute(x, "seq", [(i, (i + by) % count) for i in range(count)])


def swap(x, axis):
    return lax.all_to_all(x, axis, split_axis=0, concat_axis=0, tiled=True)


def both_ways(found, step, count):
    found = [shifted(found[0], 1, count), shifted(found[1], -1, count)] if 2 * step < count else [
        shifted(found[0], 1, count)
    ]
    return found


def body(
    layer_input,
    lengths,
    routes,
    norm1_gain,
    qkv_weight,
    out_weight,
    norm2_gain,
    router_weight,
    frozen_up,
    frozen_down,
    train_up,
    train_down,
    cotangent,
):
    tok = layer_input.shape[1]
    n_seq = lax.axis_size("seq")
    n_exp = lax.axis_size("exp")
    rank = lax.axis_index("seq")
    column = lax.axis_index("exp")
    heads = -(-HEADS // n_seq)
    wide = heads * HEAD
    width = (heads + heads % 2) * HEAD
    local = FROZEN // n_exp
    x_own = layer_input[0]
    g_own = cotangent[0]
    gain1 = norm1_gain[None, :]
    gain2 = norm2_gain[None, :]
    info = jnp.concatenate([jnp.stack([rank, column]).astype(jnp.int32), lengths[0]])

    w_t = qkv_weight.T
    w_parts = jnp.pad(w_t.reshape(3, D, D), ((0, 0), (0, n_seq * wide - D), (0, 0)))
    w_mine = lax.dynamic_slice_in_dim(w_parts, rank * wide, wide, axis=1)
    w_chunk = lax.dynamic_slice_in_dim(w_mine, column * (D // n_exp), D // n_exp, axis=2)
    w_chunk = w_chunk.reshape(3 * wide, D // n_exp).T
    w_mine = w_mine * jnp.asarray([HEAD**-0.5, 1.0, 1.0], BF)[:, None, None]
    w_mine = jnp.pad(w_mine, ((0, 0), (0, width - wide), (0, 0))).reshape(3 * width, D)
    w_parts = w_parts.reshape(3 * n_seq * wide, D)
    out_groups = jnp.pad(out_weight, ((0, n_seq * wide - D), (0, 0)))
    out_groups = jnp.pad(out_groups.reshape(n_seq, wide, D), ((0, 0), (0, width - wide), (0, 0)))
    feature_head = jnp.arange(D, dtype=jnp.int32) // HEAD
    row_id = jnp.arange(8, dtype=jnp.int32)[None, :] + heads * jnp.arange(n_seq, dtype=jnp.int32)[:, None]
    row_id = jnp.where(jnp.arange(8)[None, :] < heads, row_id, -1)
    head_rows = (row_id[:, :, None] == feature_head[None, None, :]).astype(BF)
    router = jnp.pad(router_weight, ((0, 0), (0, 128 - EXPERTS)))

    pick, g_train, g_frozen = route(info, local, routes[0].T, g_own)
    early = max(n_seq - 3, 0)
    x_now = x_own
    n1_list = []
    state = ()
    for step in range(n_seq):
        last = step == n_seq - 1
        if last:
            [g_rows] = released(info, [g_train[:, : local * CAP]], [x_now])
        x_next = None if last else shifted(x_now, 1, n_seq)
        found = attend_step(
            step,
            last,
            info,
            x_now,
            gain1,
            qkv_weight,
            state,
            through=[g_train] if step == early else [g_frozen] if step == early + 1 else [],
        )
        if step == early:
            g_train = swap(found.pop(), "exp")
        elif step == early + 1:
            g_frozen = swap(found.pop(), "exp")
        n1_list.append(found[0])
        state = tuple(found[1:]) if step == 0 else (state[0],) + tuple(found[1:])
        x_now = x_next
    unused_q, attn, lse = state

    mid, branch_squares, rows_train, rows_frozen = token_forward(
        info, attn, x_own, gain2, out_weight, pick
    )
    x_train = swap(rows_train.reshape(n_exp, local, CAP, D), "exp")
    x_frozen = swap(rows_frozen.reshape(n_exp, local, CAP, D), "exp")

    steps = range(1, n_seq // 2 + 1)
    g_steps = [both_ways([g_rows, g_rows], 1, n_seq)]
    for step in steps[1:]:
        g_steps.append(both_ways(g_steps[-1], step, n_seq))
    router_t, back_t, do_own, x_up, x_down, sums_own = expert_rows(
        FROZEN,
        info,
        x_train,
        g_train,
        router,
        train_up,
        train_down,
        True,
        g_steps[0],
        [g_train[:, local * CAP :, :128]],
    )
    sums = {by: shifted(sums_own, by, n_seq) for by in range(1, n_seq)}
    sum_steps = [
        [sums[step]] + ([sums[n_seq - step]] if 2 * step < n_seq else []) for step in steps
    ]
    back_t = swap(back_t, "exp")
    x_own_rows = x_up
    router_f, dx_f_out, mix_f = expert_rows(
        0,
        info,
        x_frozen,
        g_frozen,
        router,
        frozen_up,
        frozen_down,
        False,
        [w_mine, w_chunk] + [g for step in g_steps for g in step],
    )
    dx_f = swap(dx_f_out, "exp")
    x_steps = [both_ways([x_up, x_down], 1, n_seq)]
    qkv_mine = project_back(info, w_mine, n1_list, [dx_f_out])

    lse_rows = jnp.pad(lse.reshape(HEADS, tok), ((0, heads * n_seq - HEADS), (0, 0)))
    lse_rows = jnp.pad(lse_rows.reshape(n_seq, heads, tok), ((0, 0), (0, 8 - heads), (0, 0)))
    send, dmid, dbranch, dgain2, mix_f = token_back(
        heads,
        n_seq,
        width,
        info,
        pick,
        back_t,
        dx_f,
        mid,
        g_own,
        gain2,
        out_weight,
        out_groups,
        attn,
        lse_rows,
        head_rows,
        [qkv_mine, *x_steps[0], *sums.values()],
        [mix_f],
    )
    dos = [send[0]] + [shifted(send[step], step, n_seq) for step in range(1, n_seq)]
    mix_f = swap(mix_f, "exp")
    sends = 0 if n_seq < 4 else 1 if n_seq == 4 else 2
    found = gated(info, router, x_steps[0], g_steps[0], sum_steps[0], [send[0]], sends)
    gated_steps, x_go = [found[: len(x_steps[0])]], found[len(x_steps[0]) :]
    output, misc = token_mix(
        info, pick, back_t, mix_f, mid, x_own, attn, dbranch, router_t, router_f, dgain2, branch_squares
    )

    if len(steps) > 1:
        x_go = released(info, x_go, [misc, *dos])
    for step in steps[1:]:
        x_steps.append(both_ways(x_go if step == 2 else x_steps[-1], step, n_seq))
    dqkv, part = attend_back(heads, info, qkv_mine, misc, n1_list, dos, gated_steps[0])

    parts = swap(part.reshape(n_exp, D // n_exp, part.shape[1]), "exp")
    dqkv_own = [dqkv[0]] + [shifted(dqkv[step], -step, n_seq) for step in range(1, n_seq)]

    for i in range(1, len(x_steps)):
        gated_steps.append(gated(info, router, x_steps[i], g_steps[i], sum_steps[i], [dqkv[0]]))
    xs = [x_own_rows] + [x for step in x_steps for x in step]
    gs = [do_own] + [g for step in gated_steps for g in step]
    tiles = train_up.shape[2] // GRAD_TILE
    grad_parts = [(expert, (0, tiles)) for expert in range(local - 1)]
    grad_parts += [(local - 1, (first, tiles // 2)) for first in (0, tiles // 2)]
    totals = None

    def more_grads(wait, totals, through=()):
        expert, span = grad_parts.pop(0)
        return expert_grads_part(
            expert, span, info, xs, gs, train_up, train_down, totals, wait, through
        )

    totals, done = more_grads([dqkv[0]], totals)
    piece = sum_parts(info, parts, w_chunk, done)

    found = [shifted(piece, step, n_seq) for step in range(1, n_seq)]
    if len(grad_parts) > 1:
        totals, done = more_grads([piece], totals)
    found, again = join_blocks(info, [piece] + found, done)
    here = [lax.ppermute(found, "exp", [(i, i ^ m) for i in range(n_exp)]) for m in range(2, n_exp, 2)]
    input_grad = input_grad_rows(heads, info, x_own, gain1, dmid, w_parts, dqkv_own, done)
    while grad_parts:
        totals, (done, again) = more_grads([input_grad], totals, [again])
    here = jnp.stack([again] + here)
    there = lax.ppermute(here, "exp", [(i, i ^ 1) for i in range(n_exp)])
    up_total, down_total = totals
    qkv_total, out_total, router_total, dgain1, dgain2, stats = layout(
        heads, info, here, there, gain1
    )
    stat_roots = stats[0, EXPERTS + 1 : EXPERTS + 4]
    return (
        output[None],
        input_grad[None],
        dgain1,
        qkv_total,
        out_total,
        dgain2,
        router_total.T,
        up_total,
        down_total,
        stat_roots,
    )


def solution(mesh):
    return jax.shard_map(
        body,
        mesh=mesh,
        in_specs=(
            P("exp", "seq", None),
            P("exp", None),
            P("exp", "seq", None),
            P(),
            P(),
            P(),
            P(),
            P(),
            P("exp", None, None),
            P("exp", None, None),
            P("exp", None, None),
            P("exp", None, None),
            P("exp", "seq", None),
        ),
        out_specs=(
            P("exp", "seq", None),
            P("exp", "seq", None),
            P(),
            P(),
            P(),
            P(),
            P(),
            P("exp", None, None),
            P("exp", None, None),
            P(),
        ),
        check_vma=False,
    )
```

```python
import jax
import jax.numpy as jnp
from jax import lax
from jax.experimental import pallas as pl
from jax.experimental.pallas import tpu as pltpu
from jax.sharding import PartitionSpec as P

D = 768
HEADS = 12
HEAD = 64
EXPERTS = 32
FROZEN = 16
CAP = 48

EPS = 1e-06
MASKED = -1e30
BF = jnp.bfloat16
F32 = jnp.float32
TANH_A = 0.7978845608028654
TANH_B = 0.044715
GRAD_ROWS = 1536
GRAD_TILE = 512
MISC = 896
GAIN1_AT = 64
VMEM_BYTES = 56 * 1024 * 1024


def mm(a, b):
    return jnp.dot(a, b, preferred_element_type=F32)


def mm_nt(a, b):
    return lax.dot_general(a, b, (((1,), (1,)), ((), ())), preferred_element_type=F32)


def ein(form, a, b):
    return jnp.einsum(form, a, b, preferred_element_type=F32)


def mm_tn(a, b):
    return lax.dot_general(a, b, (((0,), (0,)), ((), ())), preferred_element_type=F32)


def params():
    return pltpu.CompilerParams(vmem_limit_bytes=VMEM_BYTES)


def cost(micros):
    return pl.CostEstimate(flops=int(micros * 1.1e9), bytes_accessed=0, transcendentals=0)


def whole(shape):
    return pl.BlockSpec(shape, lambda *unused: (0,) * len(shape))


def called(
    kernel,
    name,
    outs,
    info,
    operands,
    in_specs=None,
    scratch=(),
    micros=5,
    grid=(1,),
    out_specs=None,
    aliases=None,
    deps=(),
    through=(),
):
    specs = [None] * len(operands) if in_specs is None else in_specs
    specs = [whole(a.shape) if b is None else b for a, b in zip(operands, specs)]
    results = [whole(shape) for shape, unused in outs] if out_specs is None else list(out_specs)
    shapes = [jax.ShapeDtypeStruct(shape, kind) for shape, kind in outs]
    shapes += [jax.ShapeDtypeStruct(a.shape, a.dtype) for a in through]
    held = pl.BlockSpec(memory_space=pl.ANY)
    aliases = dict(aliases or {})
    for i in range(len(through)):
        aliases[1 + len(operands) + i] = len(outs) + i
    extra = len(through) + len(deps)

    def inner(info_ref, *refs):
        ins, rest = refs[: len(operands)], refs[len(operands) + extra :]
        kernel(info_ref, *ins, *rest[: len(outs)], *rest[len(outs) + len(through) :])

    call = pl.pallas_call(
        inner,
        out_shape=shapes,
        grid_spec=pltpu.PrefetchScalarGridSpec(
            num_scalar_prefetch=1,
            grid=grid,
            in_specs=specs + [held] * extra,
            out_specs=results + [held] * len(through),
            scratch_shapes=list(scratch),
        ),
        input_output_aliases=aliases,
        compiler_params=params(),
        cost_estimate=cost(micros),
        name=name,
    )
    return list(call(info, *operands, *through, *deps))


def released(info, arrays, deps):
    def kernel(info_ref, out_ref):
        out_ref[...] = jnp.zeros_like(out_ref)

    return called(kernel, "released", [((8, 128), F32)], info, [], micros=1, deps=deps, through=arrays)[1:]


INFO = 2


def doc_start(info_ref, position):
    bound = 0
    start = jnp.zeros_like(position)
    for i in range(INFO, info_ref.shape[0]):
        bound = bound + info_ref[i]
        start = jnp.where(position >= bound, bound, start)
    return start


def doc_end(info_ref):
    bound = 0
    for i in range(INFO, info_ref.shape[0]):
        bound = bound + info_ref[i]
    return bound


def need_mask(info_ref, key_start, last_query):
    return doc_start(info_ref, jnp.full((1, 128), last_query, jnp.int32))[0, 0] > key_start


def route_kernel(local, info_ref, routes_ref, g_ref, pick_ref, train_ref, frozen_ref):
    tok = g_ref.shape[0]
    half = pick_ref.shape[0] // 2
    first, second = routes_ref[0:1, :], routes_ref[1:2, :]
    row = lax.broadcasted_iota(jnp.int32, (EXPERTS, tok), 0)
    expert = jnp.where(row < FROZEN, row + FROZEN, row - FROZEN)
    position = info_ref[0] * tok + lax.broadcasted_iota(jnp.int32, (EXPERTS, tok), 1)
    live = ((expert == first) | (expert == second)) & (position < doc_end(info_ref))
    earlier = lax.broadcasted_iota(jnp.int32, (tok, tok), 0) < lax.broadcasted_iota(
        jnp.int32, (tok, tok), 1
    )
    place = mm(jnp.where(live, 1.0, 0.0).astype(BF), jnp.where(earlier, 1.0, 0.0).astype(BF))
    place = jnp.where(live, place, -1.0)
    slot = lax.broadcasted_iota(jnp.int32, (CAP, tok), 0).astype(F32)
    sums = jnp.broadcast_to((first + second).astype(F32), (16, tok)).astype(BF)
    sum_row = lax.broadcasted_iota(jnp.int32, (16, CAP), 0)
    for part, out_ref in ((0, train_ref), (1, frozen_ref)):
        for d in range(FROZEN // local):
            found = jnp.zeros((16, CAP), F32)
            for i in range(local):
                e = part * FROZEN + d * local + i
                taken = jnp.where(place[e : e + 1, :] == slot, 1.0, 0.0).astype(BF)
                pick_ref[e * CAP : (e + 1) * CAP, :] = taken
                found = jnp.where(sum_row == i, mm_nt(sums, taken), found)
            out_ref[d, local * CAP :, :] = jnp.zeros((16, D), BF)
            out_ref[d, local * CAP :, 0:CAP] = found.astype(BF)
        rows = mm(pick_ref[part * half : (part + 1) * half, :], g_ref[...]).astype(BF)
        for d in range(FROZEN // local):
            out_ref[d, : local * CAP, :] = rows[d * local * CAP : (d + 1) * local * CAP, :]


def route(info, local, routes, g):
    tok = g.shape[0]
    sent = (FROZEN // local, local * CAP + 16, D)

    def kernel(*refs):
        route_kernel(local, *refs)

    return called(
        kernel,
        "route",
        [((EXPERTS * CAP, tok), BF), (sent, BF), (sent, BF)],
        info,
        [routes, g],
        micros=6,
    )


def slot_sums(tile, local_id):
    parts = []
    for i in range(tile.shape[0]):
        turned = tile[i].astype(F32).T
        lane = lax.broadcasted_iota(jnp.int32, turned.shape, 1)
        column = jnp.sum(jnp.where(lane == local_id, turned, 0.0), axis=1, keepdims=True)
        parts.append(column[:CAP, :])
    return jnp.concatenate(parts, axis=0)


def gelu_parts(h):
    h2 = h * h
    t = jnp.tanh(h * (TANH_A + (TANH_A * TANH_B) * h2))
    half = 0.5 * t + 0.5
    act = h * half
    slope = half + act * (1.0 - half) * (2.0 * TANH_A + (6.0 * TANH_A * TANH_B) * h2)
    return act, slope


def attend_kernel(step, last, info_ref, x_ref, gain_ref, w_q_ref, w_k_ref, w_v_ref, *refs):
    first = step == 0
    refs = list(refs)
    if first:
        n1_ref, q_ref = refs[:2]
        refs = refs[2:]
    else:
        q_ref, m_in, l_in, acc_in, n1_ref = refs[:5]
        refs = refs[5:]
    if last:
        attn_ref = refs.pop(0)
        l_ref = refs.pop(0)
        m_ref, acc_ref, k_all, v_all = refs
    else:
        m_ref, l_ref, acc_ref, k_all, v_all = refs
    block = info_ref[0] - step
    rows = x_ref.shape[0]
    pairs = k_all.shape[0]

    x = x_ref[...].astype(F32)
    n1 = x * lax.rsqrt(jnp.mean(x * x, axis=1, keepdims=True) + EPS) * gain_ref[...]
    n1_ref[...] = n1.astype(BF)

    def project():
        n1 = n1_ref[...]
        for i in range(pairs // 2):
            cols = slice(i * 4 * HEAD, (i + 1) * 4 * HEAD)
            k = mm(n1, w_k_ref[:, cols]).astype(BF)
            v = mm(n1, w_v_ref[:, cols]).T.astype(BF)
            for j in range(2):
                k_all[2 * i + j] = k[:, j * 2 * HEAD : (j + 1) * 2 * HEAD]
                v_all[2 * i + j] = v[j * 2 * HEAD : (j + 1) * 2 * HEAD, :]
            if first:
                q = mm(n1, w_q_ref[:, cols]).astype(BF) * jnp.asarray(HEAD**-0.5, BF)
                for j in range(2):
                    q_ref[2 * i + j] = q[:, j * 2 * HEAD : (j + 1) * 2 * HEAD]

    def attend(masked):
        key_pos = block * rows + lax.broadcasted_iota(jnp.int32, (rows, rows), 0)
        query_pos = info_ref[0] * rows + lax.broadcasted_iota(jnp.int32, (1, rows), 1)
        start = doc_start(info_ref, query_pos)

        def pair(p, carry):
            q = q_ref[p]
            k = k_all[p]
            lane = lax.broadcasted_iota(jnp.int32, q.shape, 1)
            zero = jnp.zeros_like(q)
            found = [
                mm_nt(k, jnp.where(lane < HEAD, q, zero)),
                mm_nt(k, jnp.where(lane < HEAD, zero, q)),
            ]
            for half in range(2):
                scores = found[half]
                if masked:
                    allowed = key_pos >= start
                    if first:
                        allowed = allowed & (key_pos <= query_pos)
                    scores = jnp.where(allowed, scores, MASKED)
                top = jnp.max(scores, axis=0, keepdims=True)
                if not first:
                    old = m_in[p, half : half + 1, :]
                    top = jnp.maximum(top, old)
                probs = jnp.exp(scores - top)
                total = jnp.sum(probs, axis=0, keepdims=True)
                value = mm(v_all[p, half * HEAD : (half + 1) * HEAD, :], probs.astype(BF))
                part = pl.ds(pl.multiple_of(p * 2 * HEAD + half * HEAD, HEAD), HEAD)
                if not first:
                    decay = jnp.exp(old - top)
                    total = total + l_in[p, half : half + 1, :] * decay
                    value = value + acc_in[part, :] * decay
                m_ref[p, half : half + 1, :] = top
                l_ref[p, half : half + 1, :] = total
                acc_ref[part, :] = value
            return carry

        lax.fori_loop(0, pairs, pair, 0)

    if first:
        project()
        attend(True)
    else:
        masked = need_mask(info_ref, block * rows, info_ref[0] * rows + rows - 1)

        @pl.when(block >= 0)
        def _():
            project()

        @pl.when((block >= 0) & masked)
        def _():
            attend(True)

        @pl.when((block >= 0) & jnp.logical_not(masked))
        def _():
            attend(False)

        @pl.when(block < 0)
        def _():
            m_ref[...] = m_in[...]
            l_ref[...] = l_in[...]
            acc_ref[...] = acc_in[...]

    if last:
        for p in range(pairs):
            for half in range(2):
                part = slice((2 * p + half) * HEAD, (2 * p + half + 1) * HEAD)
                total = l_ref[p, half : half + 1, :]
                acc_ref[part, :] = acc_ref[part, :] / total
                l_ref[p, half : half + 1, :] = m_ref[p, half : half + 1, :] + jnp.log(total)
            part = slice(p * 2 * HEAD, (p + 1) * 2 * HEAD)
            attn_ref[:, part] = acc_ref[part, :].T.astype(BF)


def attend_step(step, last, info, x, gain, w, state, deps=(), through=()):
    tok = x.shape[0]
    pairs = HEADS // 2
    stat, acc = ((pairs, 2, tok), F32), ((D, tok), F32)
    row, by_pair = ((tok, D), BF), ((pairs, tok, 2 * HEAD), BF)
    outs = [row] + ([by_pair] if step == 0 else []) + ([row, stat] if last else [stat, stat, acc])
    scratch = [pltpu.VMEM(*by_pair), pltpu.VMEM((pairs, 2 * HEAD, tok), BF)]
    if last:
        scratch = [pltpu.VMEM(*stat), pltpu.VMEM(*acc)] + scratch

    def kernel(*refs):
        attend_kernel(step, last, *refs)

    square = (D, D)
    return called(
        kernel,
        "attend_step",
        outs,
        info,
        [x, gain, w, w, w, *state],
        [
            None,
            None,
            pl.BlockSpec(square, lambda i, r: (0, 0)),
            pl.BlockSpec(square, lambda i, r: (0, 1)),
            pl.BlockSpec(square, lambda i, r: (0, 2)),
        ]
        + [None] * len(state),
        scratch,
        micros=13,
        deps=deps,
        through=through,
    )


def attend_back_kernel(blocks, heads, info_ref, qkv_ref, misc_ref, *refs):
    n1_refs, do_refs, out_refs = [refs[i * blocks : (i + 1) * blocks] for i in range(3)]
    part_ref, dq_ref, dk_ref, dv_ref, k_mine, v_mine, k_t, do_all, lse_all, delta_all, out_all = refs[
        3 * blocks :
    ]
    rows = qkv_ref.shape[0] // blocks
    tiles, deep, width = do_refs[0].shape
    lane = lax.broadcasted_iota(jnp.int32, (rows, 2 * HEAD), 1)
    dq_ref[...] = jnp.zeros_like(dq_ref)

    def turn(b):
        return lax.rem(info_ref[0] - b + blocks, blocks)

    for b in range(blocks):
        do_all[b] = do_refs[b][:, :width, :].reshape(rows, width)
        stats = [do_refs[b][t, width:, :].astype(F32) for t in range(tiles)]
        stats = jnp.concatenate(stats, axis=1)
        delta_all[b] = stats[:heads] + stats[heads : 2 * heads]
        lse_all[b] = stats[2 * heads : 3 * heads] + stats[3 * heads : 4 * heads]

    def key_step(kb, carry):
        kt = turn(kb)
        key_rows = pl.ds(pl.multiple_of(kt * rows, rows), rows)
        for h in range(heads):
            first = (h // 2) * 2 * HEAD
            k = qkv_ref[key_rows, width + first : width + first + 2 * HEAD]
            v = qkv_ref[key_rows, 2 * width + first : 2 * width + first + 2 * HEAD]
            mine = (lane < HEAD) if h % 2 == 0 else (lane >= HEAD)
            zero = jnp.zeros_like(k)
            k_mine[h] = jnp.where(mine, k, zero)
            v_mine[h] = jnp.where(mine, v, zero)
            k_t[h] = k.T[(h % 2) * HEAD : (h % 2 + 1) * HEAD, :]
        dk_ref[...] = jnp.zeros_like(dk_ref)
        dv_ref[...] = jnp.zeros_like(dv_ref)

        def pair(qb, diagonal, masked):
            qt = turn(qb)
            query_rows = pl.ds(pl.multiple_of(qt * rows, rows), rows)
            if masked:
                key_pos = kb * rows + lax.broadcasted_iota(jnp.int32, (rows, rows), 0)
                query_pos = qb * rows + lax.broadcasted_iota(jnp.int32, (1, rows), 1)
                allowed = key_pos >= doc_start(info_ref, query_pos)
                if diagonal:
                    allowed = allowed & (key_pos <= query_pos)

            def of_head(h):
                cols = slice((h // 2) * 2 * HEAD, (h // 2 + 1) * 2 * HEAD)
                return qkv_ref[query_rows, cols], do_all[qt, :, cols]

            def products(h):
                q, do = of_head(h)
                return mm_nt(k_mine[h], q), mm_nt(v_mine[h], do)

            later = products(0)
            for h in range(heads):
                scores, dprobs = later
                if h + 1 < heads:
                    later = products(h + 1)
                q, do = of_head(h)
                probs = jnp.exp(scores - lse_all[qt, h : h + 1, :])
                if masked:
                    probs = jnp.where(allowed, probs, 0.0)
                dscores = (probs * (dprobs - delta_all[qt, h : h + 1, :])).astype(BF)
                dv_ref[h] += mm(probs.astype(BF), do)
                dk_ref[h] += mm(dscores, q)
                dq_ref[qt, h] += mm(k_t[h], dscores)

        pair(kb, True, True)

        def query_step(qb, carry):
            masked = need_mask(info_ref, kb * rows, qb * rows + rows - 1)

            @pl.when(masked)
            def _():
                pair(qb, False, True)

            @pl.when(jnp.logical_not(masked))
            def _():
                pair(qb, False, False)

            return carry

        lax.fori_loop(kb + 1, blocks, query_step, 0)
        for h in range(heads):
            part = slice((h % 2) * HEAD, (h % 2 + 1) * HEAD)
            for i, grad_ref in ((1, dk_ref), (2, dv_ref)):
                at = (i * heads + h) * HEAD
                out_all[kt, at : at + HEAD, :] = grad_ref[h].T[part, :].astype(BF)
        return carry

    lax.fori_loop(0, blocks, key_step, 0)
    total = 0.0
    for b in range(blocks):
        for h in range(heads):
            out_all[b, h * HEAD : (h + 1) * HEAD, :] = (dq_ref[b, h] * HEAD**-0.5).astype(BF)
        grads = out_all[b]
        out_refs[b][...] = grads
        total = total + mm(grads, n1_refs[b][...])
    part_ref[:, :MISC] = misc_ref[...]
    part_ref[:, MISC:] = total.T.astype(BF)


def attend_back(heads, info, qkv, misc, n1, dos, deps):
    rows = qkv.shape[0]
    blocks = len(dos)
    tiles, deep, width = dos[0].shape
    tok = rows // blocks
    cols = 3 * heads * HEAD

    def kernel(*refs):
        attend_back_kernel(blocks, heads, *refs)

    *grads, part = called(
        kernel,
        "attend_back",
        [((cols, tok), BF)] * blocks + [((D, MISC + cols), BF)],
        info,
        [qkv, misc, *n1, *dos],
        scratch=[
            pltpu.VMEM((blocks, heads, HEAD, tok), F32),
            pltpu.VMEM((heads, tok, 2 * HEAD), F32),
            pltpu.VMEM((heads, tok, 2 * HEAD), F32),
            pltpu.VMEM((heads, tok, 2 * HEAD), BF),
            pltpu.VMEM((heads, tok, 2 * HEAD), BF),
            pltpu.VMEM((heads, HEAD, tok), BF),
            pltpu.VMEM((blocks, tok, width), BF),
            pltpu.VMEM((blocks, heads, tok), F32),
            pltpu.VMEM((blocks, heads, tok), F32),
            pltpu.VMEM((blocks, cols, tok), BF),
        ],
        micros=32,
        deps=deps,
    )
    return grads, part


def project_back_kernel(blocks, info_ref, w_ref, *refs):
    out_ref = refs[blocks]
    rows = refs[0].shape[0]
    for b in range(blocks):
        out_ref[b * rows : (b + 1) * rows, :] = mm_nt(refs[b][...], w_ref[...]).astype(BF)


def project_back(info, w, n1, deps):
    blocks = len(n1)

    def kernel(*refs):
        project_back_kernel(blocks, *refs)

    shape = (blocks * n1[0].shape[0], w.shape[0])
    return called(kernel, "project_back", [(shape, BF)], info, [w, *n1], micros=7, deps=deps)[0]


def slot_gate(own, sums, x, router):
    lane = lax.broadcasted_iota(jnp.int32, (x.shape[0], router.shape[1]), 1)
    other = sums.astype(jnp.int32) - own
    signs = jnp.where(lane == own, 1.0, 0.0) - jnp.where(lane == other, 1.0, 0.0)
    margin = jnp.sum(mm(x, router) * signs, axis=1, keepdims=True)
    return 1.0 / (1.0 + jnp.exp(-margin)), signs


def expert_kernel(
    first_id, info_ref, x_ref, g_ref, sums_ref, router_ref, up_ref, down_ref, drouter_ref, *refs
):
    backs, handed = (refs[:1], refs[1:-6]) if len(refs) == 10 else (refs[:2], ())
    xs, dos, gate_ref, signs_ref, eacc, dacc = refs[-6:]
    expert = pl.program_id(0)
    step = pl.program_id(1)
    rows = xs.shape[0]
    block = x_ref.shape

    @pl.when(step == 0)
    def _():
        x = x_ref[...].reshape(rows, D)
        xs[...] = x
        own = first_id + info_ref[1] * pl.num_programs(0) + expert
        gate, signs = slot_gate(own, slot_sums(sums_ref, expert), x, router_ref[...])
        gate_ref[...] = gate
        signs_ref[...] = signs
        do = (gate * g_ref[...].reshape(rows, D).astype(F32)).astype(BF)
        dos[...] = do
        if handed:
            handed[0][...] = do.reshape(block)
            for x_out in handed[1:]:
                x_out[...] = x.reshape(block)

    act, slope = gelu_parts(mm(xs[...], up_ref[0]))
    dhid = (mm_nt(dos[...], down_ref[0]) * slope).astype(BF)
    out = mm(act.astype(BF), down_ref[0])
    dx = mm_nt(dhid, up_ref[0])

    @pl.when(step == 0)
    def _():
        eacc[...] = out
        dacc[...] = dx

    @pl.when(step > 0)
    def _():
        eacc[...] += out
        dacc[...] += dx

    @pl.when(step == pl.num_programs(1) - 1)
    def _():
        out = eacc[...]
        gate = gate_ref[...]
        g = g_ref[...].reshape(rows, D).astype(F32)
        mix = (gate * out).astype(BF).reshape(block)
        dgate = jnp.sum(g * out, axis=1, keepdims=True)
        dlogits = (gate * (1.0 - gate) * dgate * signs_ref[...]).astype(BF)
        dx = dacc[...] + mm_nt(dlogits, router_ref[...])
        dx = dx.astype(BF).reshape(block)
        if handed:
            backs[0][:, 0] = dx
            backs[0][:, 1] = mix
        else:
            backs[0][...] = dx
            backs[1][...] = mix
        drouter = mm_tn(dlogits, xs[...])

        @pl.when(expert == 0)
        def _():
            drouter_ref[...] = drouter

        @pl.when(expert > 0)
        def _():
            drouter_ref[...] += drouter


def expert_rows(first_id, info, x, g, router, up, down, handing, deps, through=()):
    sources, experts = x.shape[:2]
    rows = sources * CAP
    hidden = up.shape[2]
    tile = 1536
    row_spec = pl.BlockSpec((sources, 1, CAP, D), lambda e, f, r: (0, e, 0, 0))


    def kernel(*refs):
        expert_kernel(first_id, *refs)

    outs, out_specs = [((router.shape[1], D), F32)], [whole((router.shape[1], D))]
    if handing:
        outs += [((sources, 2) + x.shape[1:], BF)]
        out_specs += [pl.BlockSpec((sources, 2, 1, CAP, D), lambda e, f, r: (0, 0, e, 0, 0))]
    else:
        outs += [(x.shape, BF), (x.shape, BF)]
        out_specs += [row_spec, row_spec]
    if handing:
        outs += [(x.shape, BF)] * 3
        out_specs += [row_spec] * 3

    return called(
        kernel,
        "expert_rows",
        outs,
        info,
        [x, g, g, router, up, down],
        [
            row_spec,
            pl.BlockSpec((sources, CAP, D), lambda e, f, r: (0, e, 0)),
            pl.BlockSpec((sources, 16, 128), lambda e, f, r: (0, experts * CAP // 16, 0)),
            None,
            pl.BlockSpec((1, D, tile), lambda e, f, r: (e, 0, f)),
            pl.BlockSpec((1, tile, D), lambda e, f, r: (e, f, 0)),
        ],
        [
            pltpu.VMEM((rows, D), BF),
            pltpu.VMEM((rows, D), BF),
            pltpu.VMEM((rows, 1), F32),
            pltpu.VMEM((rows, 128), F32),
            pltpu.VMEM((rows, D), F32),
            pltpu.VMEM((rows, D), F32),
        ],
        micros=23,
        grid=(experts, hidden // tile),
        out_specs=out_specs,
        deps=deps,
        through=through,
    )


def gated_kernel(count, info_ref, router_ref, *refs):
    x_refs, g_refs, sum_refs, out_refs = [refs[i * count : (i + 1) * count] for i in range(4)]
    for i, again_ref in enumerate(refs[4 * count :]):
        again_ref[...] = x_refs[i][...]
    sources, experts = x_refs[0].shape[:2]
    for b in range(count):
        for e in range(experts):
            own = FROZEN + info_ref[1] * experts + e
            x = x_refs[b][:, e].reshape(sources * CAP, D)
            gate, unused = slot_gate(own, slot_sums(sum_refs[b], e), x, router_ref[...])
            g = g_refs[b][:, e * CAP : (e + 1) * CAP, :].reshape(sources * CAP, D).astype(F32)
            out_refs[b][:, e] = (gate * g).astype(BF).reshape(sources, CAP, D)


def gated(info, router, xs, gs, sums, deps=(), again=0):
    count = len(xs)

    def kernel(*refs):
        gated_kernel(count, *refs)

    return called(
        kernel,
        "gated",
        [(x.shape, BF) for x in [*xs, *xs[:again]]],
        info,
        [router, *xs, *gs, *sums],
        micros=1,
        deps=deps,
    )


def expert_grad_kernel(group, add, info_ref, ins, dup_ref, ddown_ref, done_ref, xs, dos):
    up_ref, down_ref = ins[:2]
    x_refs, do_refs = ins[2 : 2 + group], ins[2 + group : 2 + 2 * group]
    rows = xs.shape[0] // group

    @pl.when(pl.program_id(0) == 0)
    def _():
        done_ref[...] = jnp.zeros_like(done_ref)
        for b in range(group):
            part = slice(b * rows, (b + 1) * rows)
            xs[part, :] = x_refs[b][...].reshape(rows, D)
            dos[part, :] = do_refs[b][...].reshape(rows, D)

    act, slope = gelu_parts(mm(xs[...], up_ref[0]))
    dhid = (mm_nt(dos[...], down_ref[0]) * slope).astype(BF)
    ddown = mm_tn(act.astype(BF), dos[...])
    dup = mm_tn(xs[...], dhid)
    if add:
        ddown = ddown + ins[-1][0]
        dup = dup + ins[-2][0]
    ddown_ref[0] = ddown
    dup_ref[0] = dup


def expert_grads(expert, span, first, group, info, xs, dos, up, down, totals, deps, through):
    sources, experts = dos[0].shape[:2]
    rows = group * sources * CAP
    tile = GRAD_TILE
    start, count = span
    add = first > 0
    up_spec = pl.BlockSpec((1, D, tile), lambda f, r: (expert, 0, start + f))
    down_spec = pl.BlockSpec((1, tile, D), lambda f, r: (expert, start + f, 0))
    in_specs = [up_spec, down_spec]
    in_specs += [pl.BlockSpec((sources, 1, CAP, D), lambda f, r: (0, expert, 0, 0))] * (2 * group)
    part = slice(first, first + group)
    operands = [up, down, *xs[part], *dos[part]]
    aliases = {}
    if totals is not None:
        aliases = {1 + len(operands): 0, 2 + len(operands): 1}
        in_specs += [up_spec, down_spec] if add else [pl.BlockSpec(memory_space=pl.ANY)] * 2
        operands += list(totals)

    def kernel(info_ref, *refs):
        ins, rest = refs[: len(operands)], refs[len(operands) :]
        expert_grad_kernel(group, add, info_ref, ins, *rest)

    return called(
        kernel,
        "expert_grads",
        [(up.shape, F32), (down.shape, F32), ((8, 128), F32)],
        info,
        operands,
        in_specs,
        [pltpu.VMEM((rows, D), BF), pltpu.VMEM((rows, D), BF)],
        micros=9 * count,
        grid=(count,),
        out_specs=[up_spec, down_spec, whole((8, 128))],
        aliases=aliases,
        deps=deps,
        through=through,
    )


def expert_grads_part(expert, span, info, xs, dos, up, down, totals, deps, through):
    blocks = len(xs)
    group = max(1, min(blocks, GRAD_ROWS // (dos[0].shape[0] * CAP)))
    for first in range(0, blocks, group):
        dup, ddown, done, *through = expert_grads(
            expert, span, first, group, info, xs, dos, up, down, totals, deps, through
        )
        totals = [dup, ddown]
    return totals, [done, *through]


def token_forward_kernel(
    info_ref, attn_ref, x_ref, gain_ref, w_ref, pick_ref, mid_ref, square_ref, train_ref, frozen_ref
):
    tok = x_ref.shape[0]
    half = pick_ref.shape[0] // 2
    branch = mm(attn_ref[...], w_ref[...])
    mid = x_ref[...].astype(F32) + branch
    mid_ref[...] = mid
    r = lax.rsqrt(jnp.mean(mid * mid, axis=1, keepdims=True) + EPS)
    n2 = (mid * r * gain_ref[...]).astype(BF)
    train_ref[...] = mm(pick_ref[:half, :], n2).astype(BF)
    frozen_ref[...] = mm(pick_ref[half:, :], n2).astype(BF)
    position = info_ref[0] * tok + lax.broadcasted_iota(jnp.int32, (tok, D), 0)
    square = jnp.where(position < doc_end(info_ref), branch * branch, 0.0)
    square_ref[...] = jnp.sum(square, axis=0, keepdims=True)


def token_forward(info, attn, x, gain, w, pick):
    tok = x.shape[0]
    half = ((pick.shape[0] // 2, D), BF)
    return called(
        token_forward_kernel,
        "token_forward",
        [((tok, D), F32), ((1, D), F32), half, half],
        info,
        [attn, x, gain, w, pick],
        [None] * 5,
        micros=6,
    )


def token_back_kernel(
    heads,
    groups,
    info_ref,
    pick_ref,
    dx_t_ref,
    dx_f_ref,
    mid_ref,
    g_ref,
    gain_ref,
    w_ref,
    wg_ref,
    attn_ref,
    lse_ref,
    head_ref,
    *refs,
):
    send_refs = refs[:groups]
    dmid_ref, dbranch_ref, dgain_ref = refs[groups:]
    tiles, deep, width = send_refs[0].shape
    tok = mid_ref.shape[0]
    half = pick_ref.shape[0] // 2

    dn2 = mm_tn(pick_ref[:half, :], dx_t_ref[...].reshape(half, D))
    dn2 = dn2 + mm_tn(pick_ref[half:, :], dx_f_ref[...].reshape(half, D))
    mid = mid_ref[...]
    r = lax.rsqrt(jnp.mean(mid * mid, axis=1, keepdims=True) + EPS)
    u = mid * r
    dgain_ref[...] = jnp.sum(dn2 * u, axis=0, keepdims=True)
    scaled = dn2 * gain_ref[...]
    dmid = g_ref[...].astype(F32) + r * (scaled - u * jnp.mean(scaled * u, axis=1, keepdims=True))
    dmid_ref[...] = dmid
    dbranch = dmid.astype(BF)
    dbranch_ref[...] = dbranch

    dattn = mm_nt(dbranch, w_ref[...]).astype(BF).astype(F32)
    prod = dattn * attn_ref[...].astype(F32)
    high = prod.astype(BF)
    low = (prod - high.astype(F32)).astype(BF)
    for turn in range(groups):
        g = lax.rem(info_ref[0] + turn, groups)
        sent = mm_nt(dbranch, wg_ref[g]).astype(BF)
        delta = mm_nt(head_ref[g], high) + mm_nt(head_ref[g], low)
        parts = []
        for stat in (delta[:heads], lse_ref[g][:heads]):
            high_part = stat.astype(BF).astype(F32)
            parts += [high_part, stat - high_part]
        blank = jnp.zeros((16 - 4 * heads, tok), F32)
        stats = jnp.concatenate(parts + [blank], axis=0).astype(BF)
        for t in range(tiles):
            part = slice(t * width, (t + 1) * width)
            send_refs[turn][t, :width, :] = sent[part, :]
            send_refs[turn][t, width:, :] = stats[:, part]


def token_back(
    heads, groups, width, info, pick, dx_t, dx_f, mid, g, gain, w, w_groups, attn, lse, head_rows, deps, through
):
    tok = mid.shape[0]
    tiles = tok // width

    def kernel(*refs):
        token_back_kernel(heads, groups, *refs)

    outs = [((tiles, width + 16, width), BF)] * groups
    operands = [pick, dx_t, dx_f, mid, g, gain, w, w_groups, attn, lse, head_rows]
    half = (dx_f.shape[0], 1) + dx_f.shape[1:]
    found = called(
        kernel,
        "token_back",
        outs + [((tok, D), F32), ((tok, D), BF), ((1, D), F32)],
        info,
        operands,
        [None, pl.BlockSpec(half, lambda i, r: (0, 0, 0, 0, 0))] + [None] * (len(operands) - 2),
        micros=10,
        deps=deps,
        through=through,
    )
    return [found[:groups]] + found[groups:]


def token_mix_kernel(
    info_ref, pick_ref, mix_t_ref, mix_f_ref, mid_ref, x_ref, attn_ref, dbranch_ref, rt_ref, rf_ref, dgain_ref, square_ref, out_ref, misc_ref
):
    tok = mid_ref.shape[0]
    half = pick_ref.shape[0] // 2
    mix = mm_tn(pick_ref[:half, :], mix_t_ref[...].reshape(half, D))
    mix = mix + mm_tn(pick_ref[half:, :], mix_f_ref[...].reshape(half, D))
    out_ref[...] = (mid_ref[...] + mix).astype(BF)
    valid = info_ref[0] * tok + lax.broadcasted_iota(jnp.int32, (tok, D), 0) < doc_end(info_ref)
    x = x_ref[...].astype(F32)
    stats = [
        jnp.sum(jnp.where(valid, x * x, 0.0)),
        jnp.sum(square_ref[...]),
        jnp.sum(jnp.where(valid, mix * mix, 0.0)),
        jnp.clip(doc_end(info_ref) - info_ref[0] * tok, 0, tok).astype(F32),
    ]
    misc_ref[:, :D] = mm_tn(attn_ref[...], dbranch_ref[...]).astype(BF)
    tail = (rt_ref[...] + rf_ref[...]).T
    gains = jnp.broadcast_to(dgain_ref[...], (8, D)).T[:, 0:1]
    row = lax.broadcasted_iota(jnp.int32, tail.shape, 0)
    lane = lax.broadcasted_iota(jnp.int32, tail.shape, 1)
    tail = jnp.where(lane < EXPERTS, tail, 0.0) + jnp.where(lane == EXPERTS, gains, 0.0)
    for i, stat in enumerate(stats):
        tail = tail + jnp.where((lane == EXPERTS + 1 + i) & (row == 0), stat, 0.0)
    misc_ref[:, D : D + 128] = tail.astype(BF)


def token_mix(info, pick, back_t, mix_f, mid, x, attn, dbranch, router_t, router_f, dgain, square):
    tok = mid.shape[0]
    operands = [pick, back_t, mix_f, mid, x, attn, dbranch, router_t, router_f, dgain, square]
    half = (mix_f.shape[0], 1) + mix_f.shape[1:]
    return called(
        token_mix_kernel,
        "token_mix",
        [((tok, D), BF), ((D, MISC), BF)],
        info,
        operands,
        [None, pl.BlockSpec(half, lambda i, r: (0, 1, 0, 0, 0))] + [None] * (len(operands) - 2),
        micros=1,
    )


def input_grad_kernel(heads, blocks, info_ref, x_ref, gain_ref, dmid_ref, w_ref, *refs):
    grad_refs, out_ref = refs[:blocks], refs[blocks]
    wide = heads * HEAD
    dn1 = 0.0
    for turn in range(blocks):
        g = lax.rem(info_ref[0] + turn, blocks)
        for c in range(3):
            rows = pl.ds(pl.multiple_of(c * blocks * wide + g * wide, HEAD), wide)
            part = grad_refs[turn][c * wide : (c + 1) * wide, :]
            dn1 = dn1 + mm_tn(part, w_ref[rows, :])
    x = x_ref[...].astype(F32)
    r = lax.rsqrt(jnp.mean(x * x, axis=1, keepdims=True) + EPS)
    u = x * r
    scaled = dn1 * gain_ref[...]
    dx = r * (scaled - u * jnp.mean(scaled * u, axis=1, keepdims=True))
    out_ref[...] = (dmid_ref[...] + dx).astype(BF)


def input_grad_rows(heads, info, x, gain, dmid, w_t, grads, deps):
    blocks = len(grads)

    def kernel(*refs):
        input_grad_kernel(heads, blocks, *refs)

    operands = [x, gain, dmid, w_t, *grads]
    return called(
        kernel, "input_grad", [(x.shape, BF)], info, operands, micros=8, deps=deps
    )[0]


def sum_kernel(info_ref, a_ref, w_ref, out_ref):
    total = a_ref[0].astype(F32)
    for i in range(1, a_ref.shape[0]):
        total = total + a_ref[i].astype(F32)
    out_ref[...] = total.astype(BF)
    gain = jnp.sum(total[:, MISC:] * w_ref[...].astype(F32), axis=1, keepdims=True)
    lane = lax.broadcasted_iota(jnp.int32, (total.shape[0], 128), 1)
    out_ref[:, D:MISC] = jnp.where(lane == GAIN1_AT, gain, total[:, D:MISC]).astype(BF)


def sum_parts(info, a, w, deps):
    return called(sum_kernel, "sum_parts", [(a.shape[1:], BF)], info, [a, w], micros=3, deps=deps)[0]


def join_kernel(info_ref, *refs):
    found, out_ref, again_ref = refs[:-2], refs[-2], refs[-1]
    total = found[0][:, :MISC].astype(F32)
    for ref in found[1:]:
        total = total + ref[:, :MISC].astype(F32)
    out_ref[:, :MISC] = total.astype(BF)
    cols = found[0].shape[1] - MISC
    for i, ref in enumerate(found):
        out_ref[:, MISC + i * cols : MISC + (i + 1) * cols] = ref[:, MISC:]
    again_ref[...] = out_ref[...]


def join_blocks(info, found, deps):
    rows, cols = found[0].shape
    shape = (rows, MISC + len(found) * (cols - MISC))
    return called(
        join_kernel, "join_blocks", [(shape, BF)] * 2, info, list(found), micros=3, deps=deps
    )


def lay_piece(heads, info_ref, piece, qkv_ref, out_ref):
    wide = heads * HEAD
    groups = (piece.shape[1] - MISC) // (3 * wide)
    out_ref[...] = piece[:, :D].astype(F32)
    for turn in range(groups):
        g = lax.rem(info_ref[0] - turn + groups, groups)
        for c in range(3):
            at = MISC + (3 * turn + c) * wide
            grad = piece[:, at : at + wide].astype(F32)
            for g_now in range(groups):
                cols = min(wide, D - g_now * wide)
                to = c * D + g_now * wide
                if cols > 0:

                    @pl.when(g == g_now)
                    def _():
                        qkv_ref[:, to : to + cols] = grad[:, :cols]


def layout_first_kernel(heads, info_ref, here_ref, qkv_ref, out_ref):
    lay_piece(heads, info_ref, here_ref[0], qkv_ref, out_ref)


def layout_last_kernel(
    heads,
    info_ref,
    there_ref,
    here_ref,
    gain_ref,
    held_qkv,
    held_out,
    qkv_ref,
    out_ref,
    router_ref,
    gain1_ref,
    gain2_ref,
    stat_ref,
    tails,
):
    step = pl.program_id(0)
    rows = here_ref.shape[1]
    core = lax.rem(info_ref[1], 2)
    lay_piece(heads, info_ref, there_ref[0], qkv_ref, out_ref)
    mine = pl.ds(pl.multiple_of((2 * step + core) * rows, rows), rows)
    others = pl.ds(pl.multiple_of((2 * step + 1 - core) * rows, rows), rows)
    tails[mine, :] = here_ref[0].astype(F32)
    tails[others, :] = there_ref[0][:, D:MISC].astype(F32)

    @pl.when(step == pl.num_programs(0) - 1)
    def _():
        turned = tails[...].T
        gain1_ref[...] = turned[GAIN1_AT] / gain_ref[0]
        gain2_ref[...] = turned[EXPERTS]
        router_ref[...] = turned[:EXPERTS]
        stats = tails[0:8, :]
        lane = lax.broadcasted_iota(jnp.int32, stats.shape, 1)
        count = jnp.sum(jnp.where(lane == EXPERTS + 4, stats, 0.0), axis=1, keepdims=True)
        used = (lane > EXPERTS) & (lane < EXPERTS + 4)
        stat_ref[...] = jnp.sqrt(jnp.where(used, stats, 0.0) / (jnp.maximum(count, 1.0) * D))


def layout(heads, info, here, there, gain):
    chips, rows, width = here.shape

    def first_kernel(*refs):
        layout_first_kernel(heads, *refs)

    def last_kernel(*refs):
        layout_last_kernel(heads, *refs)

    piece_spec = pl.BlockSpec((1, rows, width), lambda e, r: (e ^ (r[1] // 2), 0, 0))
    tail_spec = pl.BlockSpec((1, rows, MISC - D), lambda e, r: (e ^ (r[1] // 2), 0, D // (MISC - D)))
    held = pl.BlockSpec(memory_space=pl.ANY)

    def mine(cols):
        return pl.BlockSpec((rows, cols), lambda e, r: (2 * e + lax.rem(r[1], 2), 0))

    def others(cols):
        return pl.BlockSpec((rows, cols), lambda e, r: (2 * e + 1 - lax.rem(r[1], 2), 0))

    outs = [((D, 3 * D), F32), ((D, D), F32)]
    totals = called(
        first_kernel,
        "layout_first",
        outs,
        info,
        [here],
        [piece_spec],
        micros=6,
        grid=(chips,),
        out_specs=[mine(3 * D), mine(D)],
    )
    return called(
        last_kernel,
        "layout_last",
        outs + [((EXPERTS, D), F32), ((D,), F32), ((D,), F32), ((8, 128), F32)],
        info,
        [there, here, gain, *totals],
        [piece_spec, tail_spec, None, held, held],
        [pltpu.VMEM((D, 128), F32)],
        micros=7,
        grid=(chips,),
        out_specs=[others(3 * D), others(D), whole((EXPERTS, D)), whole((D,)), whole((D,)), whole((8, 128))],
        aliases={4: 0, 5: 1},
    )


def shifted(x, by, count):
    return lax.ppermute(x, "seq", [(i, (i + by) % count) for i in range(count)])


def swap(x, axis):
    return lax.all_to_all(x, axis, split_axis=0, concat_axis=0, tiled=True)


def both_ways(found, step, count):
    found = [shifted(found[0], 1, count), shifted(found[1], -1, count)] if 2 * step < count else [
        shifted(found[0], 1, count)
    ]
    return found


def body(
    layer_input,
    lengths,
    routes,
    norm1_gain,
    qkv_weight,
    out_weight,
    norm2_gain,
    router_weight,
    frozen_up,
    frozen_down,
    train_up,
    train_down,
    cotangent,
):
    tok = layer_input.shape[1]
    n_seq = lax.axis_size("seq")
    n_exp = lax.axis_size("exp")
    rank = lax.axis_index("seq")
    column = lax.axis_index("exp")
    heads = -(-HEADS // n_seq)
    wide = heads * HEAD
    width = (heads + heads % 2) * HEAD
    local = FROZEN // n_exp
    x_own = layer_input[0]
    g_own = cotangent[0]
    gain1 = norm1_gain[None, :]
    gain2 = norm2_gain[None, :]
    info = jnp.concatenate([jnp.stack([rank, column]).astype(jnp.int32), lengths[0]])

    w_t = qkv_weight.T
    w_parts = jnp.pad(w_t.reshape(3, D, D), ((0, 0), (0, n_seq * wide - D), (0, 0)))
    w_mine = lax.dynamic_slice_in_dim(w_parts, rank * wide, wide, axis=1)
    w_chunk = lax.dynamic_slice_in_dim(w_mine, column * (D // n_exp), D // n_exp, axis=2)
    w_chunk = w_chunk.reshape(3 * wide, D // n_exp).T
    w_mine = w_mine * jnp.asarray([HEAD**-0.5, 1.0, 1.0], BF)[:, None, None]
    w_mine = jnp.pad(w_mine, ((0, 0), (0, width - wide), (0, 0))).reshape(3 * width, D)
    w_parts = w_parts.reshape(3 * n_seq * wide, D)
    out_groups = jnp.pad(out_weight, ((0, n_seq * wide - D), (0, 0)))
    out_groups = jnp.pad(out_groups.reshape(n_seq, wide, D), ((0, 0), (0, width - wide), (0, 0)))
    feature_head = jnp.arange(D, dtype=jnp.int32) // HEAD
    row_id = jnp.arange(8, dtype=jnp.int32)[None, :] + heads * jnp.arange(n_seq, dtype=jnp.int32)[:, None]
    row_id = jnp.where(jnp.arange(8)[None, :] < heads, row_id, -1)
    head_rows = (row_id[:, :, None] == feature_head[None, None, :]).astype(BF)
    router = jnp.pad(router_weight, ((0, 0), (0, 128 - EXPERTS)))

    pick, g_train, g_frozen = route(info, local, routes[0].T, g_own)
    early = max(n_seq - 3, 0)
    x_now = x_own
    n1_list = []
    state = ()
    for step in range(n_seq):
        last = step == n_seq - 1
        if last:
            [g_rows] = released(info, [g_train[:, : local * CAP]], [x_now])
        x_next = None if last else shifted(x_now, 1, n_seq)
        found = attend_step(
            step,
            last,
            info,
            x_now,
            gain1,
            qkv_weight,
            state,
            through=[g_train] if step == early else [g_frozen] if step == early + 1 else [],
        )
        if step == early:
            g_train = swap(found.pop(), "exp")
        elif step == early + 1:
            g_frozen = swap(found.pop(), "exp")
        n1_list.append(found[0])
        state = tuple(found[1:]) if step == 0 else (state[0],) + tuple(found[1:])
        x_now = x_next
    unused_q, attn, lse = state

    mid, branch_squares, rows_train, rows_frozen = token_forward(
        info, attn, x_own, gain2, out_weight, pick
    )
    x_train = swap(rows_train.reshape(n_exp, local, CAP, D), "exp")
    x_frozen = swap(rows_frozen.reshape(n_exp, local, CAP, D), "exp")

    steps = range(1, n_seq // 2 + 1)
    g_steps = [both_ways([g_rows, g_rows], 1, n_seq)]
    for step in steps[1:]:
        g_steps.append(both_ways(g_steps[-1], step, n_seq))
    router_t, back_t, do_own, x_up, x_down, sums_own = expert_rows(
        FROZEN,
        info,
        x_train,
        g_train,
        router,
        train_up,
        train_down,
        True,
        g_steps[0],
        [g_train[:, local * CAP :, :128]],
    )
    sums = {by: shifted(sums_own, by, n_seq) for by in range(1, n_seq)}
    sum_steps = [
        [sums[step]] + ([sums[n_seq - step]] if 2 * step < n_seq else []) for step in steps
    ]
    back_t = swap(back_t, "exp")
    x_own_rows = x_up
    router_f, dx_f_out, mix_f = expert_rows(
        0,
        info,
        x_frozen,
        g_frozen,
        router,
        frozen_up,
        frozen_down,
        False,
        [w_mine, w_chunk] + [g for step in g_steps for g in step],
    )
    dx_f = swap(dx_f_out, "exp")
    x_steps = [both_ways([x_up, x_down], 1, n_seq)]
    qkv_mine = project_back(info, w_mine, n1_list, [dx_f_out])

    lse_rows = jnp.pad(lse.reshape(HEADS, tok), ((0, heads * n_seq - HEADS), (0, 0)))
    lse_rows = jnp.pad(lse_rows.reshape(n_seq, heads, tok), ((0, 0), (0, 8 - heads), (0, 0)))
    send, dmid, dbranch, dgain2, mix_f = token_back(
        heads,
        n_seq,
        width,
        info,
        pick,
        back_t,
        dx_f,
        mid,
        g_own,
        gain2,
        out_weight,
        out_groups,
        attn,
        lse_rows,
        head_rows,
        [qkv_mine, *x_steps[0], *sums.values()],
        [mix_f],
    )
    dos = [send[0]] + [shifted(send[step], step, n_seq) for step in range(1, n_seq)]
    mix_f = swap(mix_f, "exp")
    sends = 0 if n_seq < 4 else 1 if n_seq == 4 else 2
    found = gated(info, router, x_steps[0], g_steps[0], sum_steps[0], [send[0]], sends)
    gated_steps, x_go = [found[: len(x_steps[0])]], found[len(x_steps[0]) :]
    output, misc = token_mix(
        info, pick, back_t, mix_f, mid, x_own, attn, dbranch, router_t, router_f, dgain2, branch_squares
    )

    if len(steps) > 1:
        x_go = released(info, x_go, [misc, *dos])
    for step in steps[1:]:
        x_steps.append(both_ways(x_go if step == 2 else x_steps[-1], step, n_seq))
    dqkv, part = attend_back(heads, info, qkv_mine, misc, n1_list, dos, gated_steps[0])

    parts = swap(part.reshape(n_exp, D // n_exp, part.shape[1]), "exp")
    dqkv_own = [dqkv[0]] + [shifted(dqkv[step], -step, n_seq) for step in range(1, n_seq)]

    for i in range(1, len(x_steps)):
        gated_steps.append(gated(info, router, x_steps[i], g_steps[i], sum_steps[i], [dqkv[0]]))
    xs = [x_own_rows] + [x for step in x_steps for x in step]
    gs = [do_own] + [g for step in gated_steps for g in step]
    tiles = train_up.shape[2] // GRAD_TILE
    grad_parts = [(expert, (0, tiles)) for expert in range(local - 1)]
    grad_parts += [(local - 1, (first, tiles // 2)) for first in (0, tiles // 2)]
    totals = None

    def more_grads(wait, totals, through=()):
        expert, span = grad_parts.pop(0)
        return expert_grads_part(
            expert, span, info, xs, gs, train_up, train_down, totals, wait, through
        )

    totals, done = more_grads([dqkv[0]], totals)
    piece = sum_parts(info, parts, w_chunk, done)

    found = [shifted(piece, step, n_seq) for step in range(1, n_seq)]
    if len(grad_parts) > 1:
        totals, done = more_grads([piece], totals)
    found, again = join_blocks(info, [piece] + found, done)
    here = [lax.ppermute(found, "exp", [(i, i ^ m) for i in range(n_exp)]) for m in range(2, n_exp, 2)]
    input_grad = input_grad_rows(heads, info, x_own, gain1, dmid, w_parts, dqkv_own, done)
    while grad_parts:
        totals, (done, again) = more_grads([input_grad], totals, [again])
    here = jnp.stack([again] + here)
    there = lax.ppermute(here, "exp", [(i, i ^ 1) for i in range(n_exp)])
    up_total, down_total = totals
    qkv_total, out_total, router_total, dgain1, dgain2, stats = layout(
        heads, info, here, there, gain1
    )
    stat_roots = stats[0, EXPERTS + 1 : EXPERTS + 4]
    return (
        output[None],
        input_grad[None],
        dgain1,
        qkv_total,
        out_total,
        dgain2,
        router_total.T,
        up_total,
        down_total,
        stat_roots,
    )


def solution(mesh):
    return jax.shard_map(
        body,
        mesh=mesh,
        in_specs=(
            P("exp", "seq", None),
            P("exp", None),
            P("exp", "seq", None),
            P(),
            P(),
            P(),
            P(),
            P(),
            P("exp", None, None),
            P("exp", None, None),
            P("exp", None, None),
            P("exp", None, None),
            P("exp", "seq", None),
        ),
        out_specs=(
            P("exp", "seq", None),
            P("exp", "seq", None),
            P(),
            P(),
            P(),
            P(),
            P(),
            P("exp", None, None),
            P("exp", None, None),
            P(),
        ),
        check_vma=False,
    )
```
